32 devices in a mesh: grp: 4 (over y, x), tm: 8 (over z, core).
Axes of the slice: x: 2, y: 2, z: 4, core: 2. Of those that a mesh axis runs over, the one named last changes fastest.
Arguments:
- frames: float32 [32768, 768], P(('grp', 'tm')), may hold values from -6 to 6
- targets: float32 [32768, 256], P(('grp', 'tm')), may hold values from -6 to 6
- lengths: int32 [32, 3], P(('grp', 'tm')), may hold values from 1 to 512, 1024 in all within a row
- span_starts: int32 [32768], P(('grp', 'tm')), may hold values from 0 to 1, as said below
- distractors: int32 [32768, 100], P(('grp', 'tm')), may hold values from 0 to 1023
- w_query: float32 [768, 768], replicated, may hold values from -0.21875 to 0.21875
- b_query: float32 [768], replicated, may hold values from -2 to 2
- w_key: float32 [768, 768], replicated, may hold values from -0.21875 to 0.21875
- w_value: float32 [768, 768], replicated, may hold values from -0.21875 to 0.21875
- b_value: float32 [768], replicated, may hold values from -2 to 2
- w_out: float32 [768, 768], replicated, may hold values from -1.75 to 1.75
- b_out: float32 [768], replicated, may hold values from -2 to 2
- norm_gain: float32 [768], replicated, may hold values from 0.5 to 1.5
- norm_bias: float32 [768], replicated, may hold values from -2 to 2
- w_up: float32 [768, 3072], replicated, may hold values from -0.21875 to 0.21875
- b_up: float32 [3072], replicated, may hold values from -2 to 2
- w_down: float32 [3072, 768], replicated, may hold values from -0.109375 to 0.109375
- b_down: float32 [768], replicated, may hold values from -2 to 2
- final_gain: float32 [768], replicated, may hold values from 0.5 to 1.5
- final_bias: float32 [768], replicated, may hold values from -2 to 2
- w_final: float32 [768, 256], replicated, may hold values from -0.21875 to 0.21875
- b_final: float32 [256], replicated, may hold values from -2 to 2
- w_target: float32 [256, 256], replicated, may hold values from -0.375 to 0.375
- b_target: float32 [256], replicated, may hold values from -2 to 2
Outputs:
- frame_loss: float32 [32768], P(('grp', 'tm'))
- input_grad: float32 [32768, 768], P(('grp', 'tm'))
- target_grad: float32 [32768, 256], P(('grp', 'tm'))
- grad_w_query: float32 [768, 768], P('tm')
- grad_b_query: float32 [768], P('tm')
- grad_w_key: float32 [768, 768], P('tm')
- grad_w_value: float32 [768, 768], P('tm')
- grad_b_value: float32 [768], P('tm')
- grad_w_out: float32 [768, 768], P('tm')
- grad_b_out: float32 [768], P('tm')
- grad_norm_gain: float32 [768], P('tm')
- grad_norm_bias: float32 [768], P('tm')
- grad_w_up: float32 [768, 3072], P('tm')
- grad_b_up: float32 [3072], P('tm')
- grad_w_down: float32 [3072, 768], P('tm')
- grad_b_down: float32 [768], P('tm')
- grad_final_gain: float32 [768], P('tm')
- grad_final_bias: float32 [768], P('tm')
- grad_w_final: float32 [768, 256], P('tm')
- grad_b_final: float32 [256], P('tm')
- grad_w_target: float32 [256, 256], P('tm')
- grad_b_target: float32 [256], P('tm')
The draws below stay inside these ranges and needn't reach their ends.
Inputs may be any that keep to these rules, and one draw needn't show every extreme that they name: Row i holds the lengths of the 3 utterances of device i, in order, summing to 1024. `span_starts`: 1 marks a frame where a masked span of 10 frames begins.
All inputs are finite; a program needn't handle non-finite values.
Results may differ from the reference program's by a relative error of at most 0.018.
The reference program's roundings to bfloat16 on the way count: a program that leaves them out, or rounds other values in their place, can miss the bound.
Values may be sent and summed in bfloat16 or wider, within the bound.
No kernel may reach another device: no remote copies, remote signals or barrier semaphores. Data moves between devices by JAX's collectives and lax.ppermute only.
A program may use at most 448 MiB of HBM per device.

```python
import math
import jax
import jax.numpy as jnp
import numpy as np
from jax import lax

D = 768
H = 12
HD = 64
FF = 3072
P_SIZE = 256
NEG = 100
SPAN = 10
UTT_DEV = 3
FR_DEV = 1024
MAXLEN = 512
TOKENS = 32768
N_TM = 8
DEVICES = 32


def draw_span_starts(key, part):
    key = jax.random.fold_in(key, 11)
    rate_key, roll_key = jax.random.split(key)
    rates = jax.random.randint(rate_key, (TOKENS // 64,), 10, 131, dtype=jnp.int32)
    rolls = jax.random.randint(roll_key, (TOKENS,), 0, 1000, dtype=jnp.int32)
    limits = jnp.repeat(rates, 64, total_repeat_length=TOKENS)
    return (rolls < limits).astype(jnp.int32)


def touch_ends(entries, stream_key, low, high):
    place = [jax.random.randint(jax.random.fold_in(stream_key, axis), (), 0, length) for axis, length in enumerate(entries.shape)]
    main_axis = entries.shape.index(max(entries.shape))
    neighbour = place[:main_axis] + [(place[main_axis] + 1) % entries.shape[main_axis]] + place[main_axis + 1:]
    return entries.at[tuple(place)].set(low).at[tuple(neighbour)].set(high)


def levels(own_key, shape, shards, smallest, top_value):
    level = 1.0
    for dim, shards_of in shards:
        draws = jax.random.uniform(jax.random.fold_in(jax.random.fold_in(own_key, 6), dim), (shards_of,), jnp.float32, smallest / len(shards), top_value / len(shards))
        level = level * jnp.repeat(jnp.exp(draws), shape[dim] // shards_of).reshape((-1,) + (1,) * (len(shape) - 1 - dim))
    return level


def length_profile(count, total, reach, slope):
    loads = [(1 << 20) // math.isqrt(standing ** slope) + 1 for standing in range(2, count + 1)]
    surplus, given = total - reach - (count - 1), [1] * (count - 1)
    while surplus > 0:
        candidates = [i for i in range(count - 1) if given[i] < reach]
        whole, left = sum([loads[i] for i in candidates]), surplus
        for i in candidates:
            addition = min(reach - given[i], max(1, left * loads[i] // whole), surplus)
            given[i] = given[i] + addition
            surplus = surplus - addition
    return np.array([reach] + given)


def ragged(rng, count, total, limit, slope):
    if count == 2:
        one = jax.random.randint(rng, (), max(1, total - limit), min(limit, total - 1) + 1)
        return jnp.stack([one, total - one])
    sizes = jnp.asarray(length_profile(count, total, limit, slope), jnp.int32)
    twos = (count - 1) // 2
    giver, sink = sizes[1:1 + 2 * twos:2], sizes[2:2 + 2 * twos:2]
    slack = jnp.minimum(giver - 1, limit - sink)
    moved = jax.random.randint(jax.random.fold_in(rng, 1), (twos,), 0, 1 << 20) % (slack + 1)
    sizes = sizes.at[1:1 + 2 * twos:2].set(giver - moved).at[2:2 + 2 * twos:2].set(sink + moved)
    return sizes[jax.random.permutation(jax.random.fold_in(rng, 2), count)]


def scatter_about(own_key, dims, width, most, cuts=(), kind=jnp.bfloat16):
    level = levels(own_key, dims, cuts, -0.22, 0.18) if cuts else 1.0
    array = jax.random.normal(own_key, dims, jnp.float32) * width * level
    return jnp.minimum(jnp.maximum(array, -most), most).astype(kind)


def setup_inputs(seed: int = 0) -> dict:
    key_list = jax.random.split(jax.random.key(seed), 25)
    frames = scatter_about(key_list[0], (TOKENS, D), 1.0, 6.0, ((0, 32),), jnp.float32)
    targets = scatter_about(key_list[1], (TOKENS, P_SIZE), 1.0, 6.0, ((0, 32),), jnp.float32)
    lengths = jax.vmap(lambda own: ragged(own, UTT_DEV, FR_DEV, MAXLEN, 1))(jax.random.split(key_list[2], DEVICES)).reshape((DEVICES, UTT_DEV)).astype(jnp.int32)
    span_starts = draw_span_starts(jax.random.fold_in(key_list[24], 71), 0)
    distractors = touch_ends(jax.random.randint(key_list[4], (TOKENS, NEG), 0, FR_DEV), jax.random.fold_in(key_list[4], 1), 0, FR_DEV - 1).astype(jnp.int32)
    w_query = scatter_about(key_list[5], (D, D), D ** -0.5, 0.21875, (), jnp.float32)
    b_query = scatter_about(key_list[6], (D,), 0.3, 2.0, (), jnp.float32)
    w_key = scatter_about(key_list[7], (D, D), D ** -0.5, 0.21875, (), jnp.float32)
    w_value = scatter_about(key_list[8], (D, D), D ** -0.5, 0.21875, (), jnp.float32)
    b_value = scatter_about(key_list[9], (D,), 0.3, 2.0, (), jnp.float32)
    w_out = scatter_about(key_list[10], (D, D), (D // 64) ** -0.5, 1.75, (), jnp.float32)
    b_out = scatter_about(key_list[11], (D,), 0.3, 2.0, (), jnp.float32)
    norm_gain = jnp.clip(1.0 + 0.1 * jax.random.normal(key_list[12], (D,), jnp.float32), 0.5, 1.5)
    norm_bias = scatter_about(key_list[13], (D,), 0.3, 2.0, (), jnp.float32)
    w_up = scatter_about(key_list[14], (D, FF), D ** -0.5, 0.21875, (), jnp.float32)
    b_up = scatter_about(key_list[15], (FF,), 0.3, 2.0, (), jnp.float32)
    w_down = scatter_about(key_list[16], (FF, D), FF ** -0.5, 0.109375, (), jnp.float32)
    b_down = scatter_about(key_list[17], (D,), 0.3, 2.0, (), jnp.float32)
    final_gain = jnp.clip(1.0 + 0.1 * jax.random.normal(key_list[18], (D,), jnp.float32), 0.5, 1.5)
    final_bias = scatter_about(key_list[19], (D,), 0.3, 2.0, (), jnp.float32)
    w_final = scatter_about(key_list[20], (D, P_SIZE), D ** -0.5, 0.21875, (), jnp.float32)
    b_final = scatter_about(key_list[21], (P_SIZE,), 0.3, 2.0, (), jnp.float32)
    w_target = scatter_about(key_list[22], (P_SIZE, P_SIZE), P_SIZE ** -0.5, 0.375, (), jnp.float32)
    b_target = scatter_about(key_list[23], (P_SIZE,), 0.3, 2.0, (), jnp.float32)
    return dict(frames=frames, targets=targets, lengths=lengths, span_starts=span_starts, distractors=distractors, w_query=w_query, b_query=b_query, w_key=w_key, w_value=w_value, b_value=b_value, w_out=w_out, b_out=b_out, norm_gain=norm_gain, norm_bias=norm_bias, w_up=w_up, b_up=b_up, w_down=w_down, b_down=b_down, final_gain=final_gain, final_bias=final_bias, w_final=w_final, b_final=b_final, w_target=w_target, b_target=b_target)


@jax.custom_vjp
def low(v):
    return lax.optimization_barrier(v.astype(jnp.bfloat16)).astype(jnp.float32)

@jax.custom_vjp
def low_back(v):
    return v

def low_keep(v):
    return (low(v), None)

def low_pass(kept, grad):
    return (grad,)

def back_keep(v):
    return (v, None)

def back_low(kept, grad):
    return (low(grad),)
low.defvjp(low_keep, low_pass)
low_back.defvjp(back_keep, back_low)
careful_matrix_product = lax.Precision.HIGHEST
norm_eps = 1e-05
cosine_eps = 1e-06
similarity_softening_factor = 0.1
masked_score = -1e+30

def matmul(left, right):
    return jnp.dot(left, right, precision=careful_matrix_product, preferred_element_type=jnp.float32)

def layer_norm(values, gain, bias):
    center = values - lax.optimization_barrier(jnp.mean(values, axis=-1, keepdims=True))
    spread = lax.optimization_barrier(jnp.mean(center * center, axis=-1, keepdims=True))
    return center * lax.rsqrt(spread + norm_eps) * gain + bias

def segment_ids(lengths_row, count):
    bounds = jnp.cumsum(lengths_row).astype(jnp.int32)
    position = jnp.arange(count, dtype=jnp.int32)
    return lax.optimization_barrier(jnp.sum((position[:, None] >= bounds[None, :]).astype(jnp.int32), axis=1))

def span_mask(starts, segment, count):
    covered = jnp.zeros((count,), jnp.float32)
    for offset in range(SPAN):
        earlier = jnp.concatenate([jnp.zeros((offset,), jnp.int32), starts[:count - offset]])
        earlier_segment = jnp.concatenate([jnp.full((offset,), -1, jnp.int32), segment[:count - offset]])
        hit = jnp.where(earlier_segment == segment, earlier, 0).astype(jnp.float32)
        covered = jnp.maximum(covered, hit)
    return covered

def normalized_embeddings(values):
    return values * lax.rsqrt(lax.optimization_barrier(jnp.sum(values * values, axis=-1, keepdims=True)) + cosine_eps)

def head_loss(final, correct_quantized_goal, collected_sample_lines, masked):
    closing_heading_normal = normalized_embeddings(final)
    matching_similarity_score = lax.optimization_barrier(jnp.sum(closing_heading_normal * normalized_embeddings(correct_quantized_goal), axis=-1)) / similarity_softening_factor
    decoy_similarity_score = jnp.einsum('og,oqg->oq', closing_heading_normal, normalized_embeddings(collected_sample_lines), precision=careful_matrix_product) / similarity_softening_factor
    logits = jnp.concatenate([matching_similarity_score[:, None], decoy_similarity_score], axis=1)
    return masked * (jax.nn.logsumexp(logits, axis=1) - matching_similarity_score)

def block_terms(lowered, target_all, frames, starts, lengths_row, picks, own_start, group_start):
    query_matrix, b_query, key_matrix, value_matrix, b_value, out_matrix, b_out, norm_gain, norm_bias, up_matrix, b_up, down_matrix, b_down, final_gain, final_bias, final_matrix, b_final = lowered
    count = frames.shape[0]
    segment = segment_ids(lengths_row, count)
    masked = span_mask(starts, segment, count)
    frames_low = low(frames)
    query = low(low_back(matmul(frames_low, query_matrix) + b_query)).reshape(count, H, HD)
    key = low(low_back(matmul(frames_low, key_matrix))).reshape(count, H, HD)
    value = low(low_back(matmul(frames_low, value_matrix) + b_value)).reshape(count, H, HD)
    scores = low_back(jnp.einsum('qhd,khd->hqk', query, key, precision=careful_matrix_product) * HD ** (-0.5))
    same = segment[:, None] == segment[None, :]
    scores = jnp.where(same[None], scores, masked_score)
    prob = jax.nn.softmax(scores, axis=-1)
    attended = jnp.einsum('hqk,khd->qhd', low(prob), value, precision=careful_matrix_product).reshape(count, D)
    attended = low(low_back(attended))
    resid = frames + low_back(matmul(attended, out_matrix) + b_out)
    hidden = layer_norm(resid, norm_gain, norm_bias)
    upper = low_back(matmul(low(hidden), up_matrix) + b_up)
    active = low(jax.nn.gelu(upper, approximate=False))
    second = hidden + low_back(matmul(active, down_matrix) + b_down)
    output = layer_norm(second, final_gain, final_bias)
    final = low_back(matmul(low(output), final_matrix) + b_final)
    correct_quantized_goal = lax.dynamic_slice_in_dim(target_all, own_start.astype(jnp.int32), count, 0)
    collected_sample_lines = low_back(jnp.take(target_all, (picks + group_start).astype(jnp.int32), axis=0))
    return head_loss(final, correct_quantized_goal, collected_sample_lines, masked)

def reference(frames, targets, lengths, span_starts, distractors, w_query, b_query, w_key, w_value, b_value, w_out, b_out, norm_gain, norm_bias, w_up, b_up, w_down, b_down, final_gain, final_bias, w_final, b_final, w_target, b_target):
    block_index = jnp.arange(DEVICES, dtype=jnp.int32)
    own_starts = (block_index * FR_DEV).astype(jnp.int32)
    group_starts = (block_index // N_TM * (N_TM * FR_DEV)).astype(jnp.int32)
    slot_owner = (jnp.arange(FR_DEV * NEG, dtype=jnp.int32) % N_TM).reshape(FR_DEV, NEG)
    picks_all = (slot_owner[None] * FR_DEV + distractors.reshape(DEVICES, FR_DEV, NEG)).astype(jnp.int32)
    checked = jax.checkpoint(block_terms)

    def objective(frames, targets, *params):
        w_query, b_query, w_key, w_value, b_value, w_out, b_out, norm_gain, norm_bias, w_up, b_up, w_down, b_down, final_gain, final_bias, w_final, b_final, w_target, b_target = params
        target_all = low(low_back(matmul(low(targets), low(w_target)) + b_target))
        lowered = (low(w_query), b_query, low(w_key), low(w_value), b_value, low(w_out), b_out, norm_gain, norm_bias, low(w_up), b_up, low(w_down), b_down, final_gain, final_bias, low(w_final), b_final)
        blocks = (frames.reshape(DEVICES, FR_DEV, D), span_starts.reshape(DEVICES, FR_DEV), lengths, picks_all, own_starts, group_starts)

        def scan_step(total, inputs):
            loss = checked(lowered, target_all, *inputs)
            return (total + jnp.sum(loss), loss)
        total, losses = lax.scan(scan_step, jnp.zeros((), jnp.float32), blocks)
        return (total, losses.reshape(TOKENS))
    floats = (frames, targets, w_query, b_query, w_key, w_value, b_value, w_out, b_out, norm_gain, norm_bias, w_up, b_up, w_down, b_down, final_gain, final_bias, w_final, b_final, w_target, b_target)
    total, backward, losses = jax.vjp(objective, *floats, has_aux=True)
    grads = backward(jnp.ones_like(total))
    return (losses, grads[0], grads[1], grads[2], grads[3], grads[4], grads[5], grads[6], grads[7], grads[8], grads[9], grads[10], grads[11], grads[12], grads[13], grads[14], grads[15], grads[16], grads[17], grads[18], grads[19], grads[20])
```

```python
import functools
import math

import jax
import jax.numpy as jnp
from jax import lax
from jax.experimental import pallas as pl
from jax.experimental.pallas import tpu as pltpu
from jax.sharding import PartitionSpec as P

H = 12
HD = 64
NEG = 100
SPAN = 10


norm_eps = 1e-05
cosine_eps = 1e-06
similarity_softening_factor = 0.1
log2e = 1.4426950408889634
PAIR = 2 * HD
COLUMNS = 256
NT = (((1,), (1,)), ((), ()))
TN = (((0,), (0,)), ((), ()))
small_cost = pl.CostEstimate(flops=1, bytes_accessed=1, transcendentals=0)


def to_low(values):
    return values.astype(jnp.bfloat16)


def product(left, right):
    return jnp.dot(left, right, preferred_element_type=jnp.float32)


def product_left(left, right):
    return lax.dot_general(
        left, right, (((0,), (0,)), ((), ())), preferred_element_type=jnp.float32
    )


def product_right(left, right):
    return lax.dot_general(
        left, right, (((1,), (1,)), ((), ())), preferred_element_type=jnp.float32
    )


def column_sum(values):
    return jnp.sum(values.astype(jnp.float32), axis=0)


def exact_gelu(values):
    return jax.nn.gelu(values, approximate=False)


def layer_norm(values, gain, bias):
    center = values - jnp.mean(values, axis=-1, keepdims=True)
    scale = lax.rsqrt(jnp.mean(center * center, axis=-1, keepdims=True) + norm_eps)
    normed = center * scale
    return (normed * gain + bias, normed, scale)


def layer_norm_back(grad, normed, scale, gain):
    grad_normed = grad * gain
    inner = (
        grad_normed
        - jnp.mean(grad_normed, axis=-1, keepdims=True)
        - normed * jnp.mean(grad_normed * normed, axis=-1, keepdims=True)
    )
    return (inner * scale, jnp.sum(grad * normed, axis=0), jnp.sum(grad, axis=0))


def segment_ids(lengths_row, count):
    bounds = jnp.cumsum(lengths_row)
    position = jnp.arange(count, dtype=jnp.int32)
    return jnp.sum((position[:, None] >= bounds[None, :]).astype(jnp.int32), axis=1)


def span_mask(starts, segment, count):
    covered = jnp.zeros((count,), jnp.float32)
    for offset in range(SPAN):
        earlier = jnp.concatenate([jnp.zeros((offset,), jnp.int32), starts[: count - offset]])
        earlier_segment = jnp.concatenate(
            [jnp.full((offset,), -1, jnp.int32), segment[: count - offset]]
        )
        hit = jnp.where(earlier_segment == segment, earlier, 0).astype(jnp.float32)
        covered = jnp.maximum(covered, hit)
    return covered


def dot(a, b, dims=(((1,), (0,)), ((), ()))):
    return lax.dot_general(a, b, dims, preferred_element_type=jnp.float32)

def first_half(rows):
    return lax.broadcasted_iota(jnp.int32, (rows, PAIR), 1) < HD

def windows(span_ref, block, chunk, count, body):
    i = pl.program_id(0)
    start, chunks = span_ref[0, i], span_ref[1, i]
    total = count // chunk
    sizes = [s for s in range(2, total + 1)]
    for s in sizes:
        hit = (chunks <= s) if s == sizes[0] else (chunks == s)
        @pl.when(hit)
        def _(s=s):
            at = pl.multiple_of(jnp.minimum(start, total - s) * chunk, chunk)
            body(at, s * chunk)

def forward_kernel(pairs, chunk, unroll, span_ref, q_ref, k_ref, v_ref, hotq_ref, hotk_ref, *refs):
    casts = (len(refs) - 2) // 2
    out_ref, log_ref = refs[casts : casts + 2]
    for wide_ref, low_ref in zip(refs[:casts], refs[casts + 2 :]):
        low_ref[...] = to_low(wide_ref[...])
    block = q_ref.shape[0]
    count = k_ref.shape[0]
    c = HD ** -0.5 * log2e
    def body(at, size):
        near = pl.ds(at, size)
        lane = lax.broadcasted_iota(jnp.int32, (block, PAIR), 1)
        def pair(p, logs):
            cols = pl.ds(pl.multiple_of(p * PAIR, PAIR), PAIR)
            q, k, v = q_ref[:, cols], k_ref[near, cols], v_ref[near, cols]
            hotq, hotk = hotq_ref[...], hotk_ref[near, :]
            fq, fk = first_half(block), first_half(size)
            outs = []
            for h in range(2):
                qh = jnp.where(fq, q, hotq) if h == 0 else jnp.where(fq, hotq, q)
                kh = jnp.where(fk, k, hotk) if h == 0 else jnp.where(fk, hotk, k)
                s = dot(qh, kh, NT)
                top = jnp.max(s, axis=1, keepdims=True) * c
                e = jnp.exp2(s * c - top)
                total = jnp.sum(e, axis=1, keepdims=True)
                o = dot(e.astype(jnp.bfloat16), v)
                outs.append(o * (1.0 / total))
                logs = jnp.where(lane == 2 * p + h, top + jnp.log2(total), logs)
            out_ref[:, cols] = jnp.where(fq, outs[0], outs[1]).astype(jnp.bfloat16)
            return logs
        log_ref[...] = lax.fori_loop(0, pairs, pair, jnp.zeros((block, PAIR), jnp.float32), unroll=unroll)
    windows(span_ref, block, chunk, count, body)

def attend(span, query, key, value, hotq, hotk, casts, block, chunk, unroll):
    count, width = query.shape
    whole = lambda w: pl.BlockSpec((count, w), lambda i, *_: (0, 0))
    part = lambda w: pl.BlockSpec((block, w), lambda i, *_: (i, 0))
    steps = count // block
    slices = [pl.BlockSpec((x.shape[0] // steps, x.shape[1]), lambda i, *_: (i, 0)) for x in casts]
    return pl.pallas_call(
        functools.partial(forward_kernel, width // PAIR, chunk, unroll),
        grid_spec=pltpu.PrefetchScalarGridSpec(
            num_scalar_prefetch=1, grid=(count // block,),
            in_specs=[part(width), whole(width), whole(width), part(PAIR), whole(PAIR)] + slices,
            out_specs=[part(width), part(PAIR)] + slices,
        ),
        out_shape=[jax.ShapeDtypeStruct((count, width), jnp.bfloat16), jax.ShapeDtypeStruct((count, PAIR), jnp.float32)]
        + [jax.ShapeDtypeStruct(x.shape, jnp.bfloat16) for x in casts],
        cost_estimate=small_cost,
        compiler_params=pltpu.CompilerParams(vmem_limit_bytes=62 << 20),
    )(span, query, key, value, hotq, hotk, *casts)

def backward_kernel(
    pairs, chunk, unroll, piece, span_ref, q_ref, k_ref, v_ref, g_ref, hotq_ref, hotk_ref, log_ref, *refs
):
    dq_ref, dk_ref, dv_ref, sums_ref, dk_sum, dv_sum = refs[-6:]
    block = q_ref.shape[0]
    count = k_ref.shape[0]
    c = HD ** -0.5 * log2e
    @pl.when(pl.program_id(0) == 0)
    def _():
        dk_sum[...] = jnp.zeros_like(dk_sum)
        dv_sum[...] = jnp.zeros_like(dv_sum)
        sums_ref[...] = jnp.zeros_like(sums_ref)
    def body(at, size):
        near = pl.ds(at, size)
        lane = lax.broadcasted_iota(jnp.int32, (block, PAIR), 1)
        def pair(p, _):
            cols = pl.ds(pl.multiple_of(p * PAIR, PAIR), PAIR)
            q, k, v, g = q_ref[:, cols], k_ref[near, cols], v_ref[near, cols], g_ref[:, cols]
            hotq, hotk, logs = hotq_ref[...], hotk_ref[near, :], log_ref[...]
            fq, fk = first_half(block), first_half(size)
            zero = jnp.zeros_like(g)
            dqs, dks, dvs = [], [], []
            for h in range(2):
                qh = jnp.where(fq, q, hotq) if h == 0 else jnp.where(fq, hotq, q)
                kh = jnp.where(fk, k, hotk) if h == 0 else jnp.where(fk, hotk, k)
                gh = jnp.where(fq, g, zero) if h == 0 else jnp.where(fq, zero, g)
                s = dot(qh, kh, NT)
                log = jnp.sum(jnp.where(lane == 2 * (p + piece * pairs) + h, logs, 0.0), axis=1, keepdims=True)
                e = jnp.exp2(s * c - log)
                de = dot(gh, v, NT)
                inner = jnp.sum(de * e, axis=1, keepdims=True)
                ds = (e * (de - inner)).astype(jnp.bfloat16)
                dqs.append(dot(ds, k))
                dks.append(dot(ds, q, TN))
                dvs.append(dot(e.astype(jnp.bfloat16), g, TN))
            dq_ref[:, cols] = (jnp.where(fq, dqs[0], dqs[1]) * HD ** -0.5).astype(jnp.bfloat16)
            dk_sum[near, cols] += jnp.where(fk, dks[0], dks[1])
            dv_sum[near, cols] += jnp.where(fk, dvs[0], dvs[1])
            return 0
        lax.fori_loop(0, pairs, pair, 0, unroll=unroll)
    windows(span_ref, block, chunk, count, body)
    rounded = dq_ref[...].astype(jnp.float32)
    sums_ref[0] += jnp.sum(rounded.reshape(-1, 8, rounded.shape[1]), axis=0)
    @pl.when(pl.program_id(0) == pl.num_programs(0) - 1)
    def _():
        sums_ref[1] = jnp.sum(dv_sum[...].reshape(-1, 8, dv_sum.shape[1]), axis=0)
        dk_ref[...] = (dk_sum[...] * HD ** -0.5).astype(jnp.bfloat16)
        dv_ref[...] = dv_sum[...].astype(jnp.bfloat16)

def attend_back(
    span, query, key, value, grad, hotq, hotk, logs, block, chunk, unroll, piece, pieces, after
):
    count = query.shape[0]
    width = query.shape[1] // pieces
    whole = lambda w, j=0: pl.BlockSpec((count, w), lambda i, *_: (0, j))
    part = lambda w, j=0: pl.BlockSpec((block, w), lambda i, *_: (i, j))
    shape = jax.ShapeDtypeStruct
    return pl.pallas_call(
        functools.partial(backward_kernel, width // PAIR, chunk, unroll, piece),
        grid_spec=pltpu.PrefetchScalarGridSpec(
            num_scalar_prefetch=1,
            grid=(count // block,),
            in_specs=[
                part(width, piece),
                whole(width, piece),
                whole(width, piece),
                part(width, piece),
                part(PAIR),
                whole(PAIR),
                part(PAIR),
            ]
            + [pl.BlockSpec(memory_space=pl.ANY)] * len(after),
            out_specs=[
                part(width),
                whole(width),
                whole(width),
                pl.BlockSpec((2, 8, width), lambda i, *_: (0, 0, 0)),
            ],
            scratch_shapes=[pltpu.VMEM((count, width), jnp.float32)] * 2,
        ),
        out_shape=[shape((count, width), jnp.bfloat16)] * 3 + [shape((2, 8, width), jnp.float32)],
        cost_estimate=small_cost,
        compiler_params=pltpu.CompilerParams(vmem_limit_bytes=62 << 20),
    )(span, query, key, value, grad, hotq, hotk, logs, *after)


def attention_plan(lengths_row, segment, count, block, chunk):
    kinds = lengths_row.shape[0]
    bounds = jnp.cumsum(lengths_row)
    starts = bounds - lengths_row
    first = segment[::block]
    last = segment[block - 1 :: block]
    low = starts[first] // chunk
    high = (bounds[last] + chunk - 1) // chunk
    span = jnp.stack([low, high - low]).astype(jnp.int32)
    lane = jnp.arange(PAIR, dtype=jnp.int32)[None, :] % HD
    same = lane == segment[:, None]
    hotq = jnp.where((lane < kinds) & ~same, 1e30, 0.0).astype(jnp.bfloat16)
    hotk = jnp.where(same, -1.0, 0.0).astype(jnp.bfloat16)
    return span, hotq, hotk


def rows_of(values):
    return pl.BlockSpec((values.shape[0], values.shape[1]), lambda i, *_: (0, 0))


def gelu_and_slope(values):
    size = jnp.abs(values) * 0.7071067811865476
    near = 1.0 / (1.0 + 0.3275911 * size)
    bell = jnp.exp2(values * values * (-0.5 * log2e))
    poly = near * (
        0.254829592
        + near * (-0.284496736 + near * (1.421413741 + near * (-1.453152027 + near * 1.061405429)))
    )
    tail = 0.5 * poly * bell
    share = jnp.where(values >= 0, 1.0 - tail, tail)
    return values * share, share + values * bell * 0.3989422804014327


def normalize(values):
    center = values - jnp.mean(values, axis=-1, keepdims=True)
    scale = lax.rsqrt(jnp.mean(center * center, axis=-1, keepdims=True) + norm_eps)
    return center * scale, scale


def normalize_back(grad, normed, scale, gain):
    moved = grad * gain
    inner = (
        moved
        - jnp.mean(moved, axis=-1, keepdims=True)
        - normed * jnp.mean(moved * normed, axis=-1, keepdims=True)
    )
    return inner * scale


def feed_forward_kernel(
    parts,
    attended_ref,
    frames_ref,
    out_ref,
    up_ref,
    down_ref,
    final_ref,
    *refs,
):
    vectors, up_bias_ref, final_bias_ref = refs[:6], refs[6], refs[7]
    (
        hidden_low_ref,
        normed_one_ref,
        active_ref,
        slope_ref,
        normed_two_ref,
        output_low_ref,
        scales_ref,
        unit_ref,
        unit_scale_ref,
    ) = refs[8:]
    vector = lambda row: vectors[row][...].reshape(1, -1)
    resid = frames_ref[...] + dot(attended_ref[...], out_ref[...]) + vector(0)
    normed, scale_one = normalize(resid)
    normed_one_ref[...] = normed
    hidden = normed * vector(1) + vector(2)
    hidden_low = to_low(hidden)
    hidden_low_ref[...] = hidden_low
    second = hidden + vector(3)
    chunk = up_ref.shape[1] // parts
    for part in range(parts):
        at = pl.ds(part * chunk, chunk)
        upper = dot(hidden_low, up_ref[:, at]) + up_bias_ref[at].reshape(1, -1)
        active, slope = gelu_and_slope(upper)
        active = to_low(active)
        active_ref[:, at] = active
        slope_ref[:, at] = to_low(slope)
        second = second + dot(active, down_ref[at, :])
    normed, scale_two = normalize(second)
    normed_two_ref[...] = normed
    output_low = to_low(normed * vector(4) + vector(5))
    output_low_ref[...] = output_low
    final = dot(output_low, final_ref[...]) + final_bias_ref[...].reshape(1, -1)
    turned = final.T
    unit_scale = lax.rsqrt(jnp.sum(turned * turned, axis=0, keepdims=True) + cosine_eps)
    unit_ref[...] = turned * unit_scale
    unit_scale_ref[...] = jnp.broadcast_to(unit_scale, unit_scale_ref.shape)
    lane = lax.broadcasted_iota(jnp.int32, scales_ref.shape, 1)
    scales_ref[...] = jnp.where(lane == 0, scale_one, scale_two)


def feed_forward(attended, frames, out, up, down, final, vectors, block):
    count, model = frames.shape
    inner, width = up.shape[1], final.shape[1]
    part = lambda columns: pl.BlockSpec((block, columns), lambda i: (i, 0))
    turned = lambda rows: pl.BlockSpec((rows, block), lambda i: (0, i))
    shape = jax.ShapeDtypeStruct
    low, full = jnp.bfloat16, jnp.float32
    operands = (attended, frames, out, up, down, final)
    return pl.pallas_call(
        functools.partial(feed_forward_kernel, max(inner // model, 1)),
        grid=(count // block,),
        in_specs=[part(model), part(model)]
        + [rows_of(x) for x in operands[2:]]
        + [vector_spec(x) for x in vectors],
        out_specs=[part(model), part(model), part(inner), part(inner), part(model), part(model), part(PAIR)]
        + [turned(width), turned(8)],
        out_shape=[
            shape((count, model), low),
            shape((count, model), full),
            shape((count, inner), low),
            shape((count, inner), low),
            shape((count, model), full),
            shape((count, model), low),
            shape((count, PAIR), full),
            shape((width, count), full),
            shape((8, count), full),
        ],
        cost_estimate=small_cost,
        compiler_params=pltpu.CompilerParams(vmem_limit_bytes=62 << 20),
    )(*operands, *vectors)


def feed_forward_back_kernel(
    parts,
    d_final_ref,
    slope_ref,
    normed_one_ref,
    normed_two_ref,
    scales_ref,
    final_ref,
    up_ref,
    down_ref,
    out_ref,
    gain_one_ref,
    gain_two_ref,
    down_low_ref,
    upper_low_ref,
    resid_ref,
    branch_low_ref,
    attended_low_ref,
    sums_ref,
    up_sums_ref,
):
    @pl.when(pl.program_id(0) == 0)
    def _():
        sums_ref[...] = jnp.zeros_like(sums_ref)
        up_sums_ref[...] = jnp.zeros_like(up_sums_ref)

    def add(row, values):
        sums_ref[row] += jnp.sum(values.reshape(-1, 8, values.shape[1]), axis=0)

    grad = dot(d_final_ref[...], final_ref[...], NT)
    normed = normed_two_ref[...]
    gain = gain_two_ref[...].reshape(1, -1)
    hidden = normalize_back(grad, normed, scales_ref[:, 1:2], gain)
    down_low = to_low(hidden)
    down_low_ref[...] = down_low
    add(0, grad * normed)
    add(1, grad)
    add(2, down_low.astype(jnp.float32))
    chunk = up_ref.shape[1] // parts
    for part in range(parts):
        at = pl.ds(part * chunk, chunk)
        upper = dot(down_low, down_ref[at, :], NT) * slope_ref[:, at].astype(jnp.float32)
        upper_low = to_low(upper)
        upper_low_ref[:, at] = upper_low
        up_sums_ref[:, at] += jnp.sum(upper.reshape(-1, 8, chunk), axis=0)
        hidden = hidden + dot(upper_low, up_ref[:, at], NT)
    normed = normed_one_ref[...]
    gain = gain_one_ref[...].reshape(1, -1)
    resid = normalize_back(hidden, normed, scales_ref[:, 0:1], gain)
    resid_ref[...] = resid
    branch_low = to_low(resid)
    branch_low_ref[...] = branch_low
    attended_low_ref[...] = to_low(dot(branch_low, out_ref[...], NT))
    add(3, hidden * normed)
    add(4, hidden)
    add(5, branch_low.astype(jnp.float32))


def feed_forward_back(d_final, slope, normed_one, normed_two, scales, final, up, down, out, gains, block):
    count, model = normed_one.shape
    inner = up.shape[1]
    part = lambda columns: pl.BlockSpec((block, columns), lambda i: (i, 0))
    shape = jax.ShapeDtypeStruct
    low, full = jnp.bfloat16, jnp.float32
    return pl.pallas_call(
        functools.partial(feed_forward_back_kernel, max(inner // model, 1)),
        grid=(count // block,),
        in_specs=[part(d_final.shape[1]), part(inner), part(model), part(model), part(PAIR)]
        + [rows_of(x) for x in (final, up, down, out)]
        + [vector_spec(x) for x in gains],
        out_specs=[part(model), part(inner), part(model), part(model), part(model)]
        + [
            pl.BlockSpec((6, 8, model), lambda i: (0, 0, 0)),
            pl.BlockSpec((8, inner), lambda i: (0, 0)),
        ],
        out_shape=[
            shape((count, model), low),
            shape((count, inner), low),
            shape((count, model), full),
            shape((count, model), low),
            shape((count, model), low),
            shape((6, 8, model), full),
            shape((8, inner), full),
        ],
        cost_estimate=small_cost,
        compiler_params=pltpu.CompilerParams(vmem_limit_bytes=62 << 20),
    )(d_final, slope, normed_one, normed_two, scales, final, up, down, out, *gains)


def candidate_kernel(
    slots, owners, keep, index_ref, rows_ref, unit_ref, scale_ref, positive_ref, masked_ref,
    loss_ref, final_low_ref, positive_part_ref, rows_grad_ref,
    packed, mass, pull, total, unit_low, weighted,
):
    step = pl.program_id(0)
    frames = unit_ref.shape[1]
    own = rows_ref.shape[0]
    lanes = 128
    words = lax.broadcasted_iota(jnp.int32, (128, lanes), 0)

    def fill(at_mass):
        def count(tile, _):
            at = pl.ds(pl.multiple_of(tile * lanes, lanes), lanes)
            acc = jnp.zeros((128, lanes), jnp.int32)
            for slot in range(slots):
                index = index_ref[0, pl.ds(slot, 1), at]
                low = jnp.bitwise_and(index, 127)
                unit = jnp.where(index >= 0, jnp.left_shift(1, 4 * jnp.right_shift(index, 7)), 0)
                acc = acc + jnp.where(words == low, unit, 0)
            packed[:, at] = acc
            return 0

        lax.fori_loop(0, frames // lanes, count, 0)

        def part(nibble, _):
            at = pl.ds(pl.multiple_of(nibble * 128, 128), 128)
            cosine = dot(rows_ref[at, :], unit_low[...])
            times = jnp.bitwise_and(lax.shift_right_logical(packed[...], 4 * nibble), 15)
            value = times.astype(jnp.float32) * jnp.exp2(cosine)
            total[...] += jnp.sum(value.reshape(16, 8, frames), axis=0)
            mass[pl.ds(pl.multiple_of(at_mass + nibble * 128, 128), 128), :] = to_low(value)
            return 0

        lax.fori_loop(0, own // 128, part, 0, unroll=2)

    @pl.when(step == 0)
    def _():
        unit_low[...] = to_low(unit_ref[...])
        total[...] = jnp.zeros_like(total)
        pull[...] = jnp.zeros_like(pull)

    @pl.when(step < owners)
    def _():
        at_mass = step * own if keep else 0
        fill(at_mass)
        pull[...] += dot(rows_ref[...], mass[pl.ds(pl.multiple_of(at_mass, own), own), :], TN)

    @pl.when(step == owners - 1)
    def _():
        score_scale = log2e / similarity_softening_factor
        unit, positive, masked = unit_ref[...], positive_ref[...], masked_ref[...]
        mass_sum = jnp.sum(total[...], axis=0, keepdims=True)
        score = jnp.sum(unit * positive, axis=0, keepdims=True) * (1.0 / similarity_softening_factor)
        whole = jnp.exp(score) + mass_sum
        loss_ref[...] = jnp.broadcast_to(masked * (jnp.log(whole) - score), loss_ref.shape)
        weight = masked / whole * (1.0 / similarity_softening_factor)
        d_score = -weight * mass_sum
        d_unit = d_score * positive + weight * (1.0 / score_scale) * pull[...]
        inner = jnp.sum(d_unit * unit, axis=0, keepdims=True)
        final_low_ref[...] = to_low((scale_ref[0:1, :] * (d_unit - unit * inner)).T)
        positive_part_ref[...] = (d_score * unit).T
        weighted[...] = to_low((weight * unit).T)

    @pl.when(step >= owners)
    def _():
        at_mass = (step - owners) * own if keep else 0
        if not keep:
            fill(at_mass)
        rows_grad_ref[...] = to_low(dot(mass[pl.ds(pl.multiple_of(at_mass, own), own), :], weighted[...]))


def candidates(index, rows, unit, scale, positive, masked):
    owners, slots, frames = index.shape
    width = rows.shape[1]
    own = rows.shape[0] // owners
    keep = rows.shape[0] * frames * 2 <= 16 << 20
    again = (lambda i: jnp.minimum(i, owners - 1)) if keep else (lambda i: lax.rem(i, owners))
    shape = jax.ShapeDtypeStruct
    return pl.pallas_call(
        functools.partial(candidate_kernel, slots, owners, keep),
        grid=(2 * owners,),
        in_specs=[
            pl.BlockSpec((1, slots, frames), lambda i: (again(i), 0, 0)),
            pl.BlockSpec((own, width), lambda i: (again(i), 0)),
            rows_of(unit),
            rows_of(scale),
            rows_of(positive),
            rows_of(masked),
        ],
        out_specs=[
            pl.BlockSpec((8, frames), lambda i: (0, 0)),
            pl.BlockSpec((frames, width), lambda i: (0, 0)),
            pl.BlockSpec((frames, width), lambda i: (0, 0)),
            pl.BlockSpec((own, width), lambda i: (jnp.maximum(i - owners, 0), 0)),
        ],
        out_shape=[
            shape((8, frames), jnp.float32),
            shape((frames, width), jnp.bfloat16),
            shape((frames, width), jnp.float32),
            shape((rows.shape[0], width), jnp.bfloat16),
        ],
        scratch_shapes=[
            pltpu.VMEM((128, frames), jnp.int32),
            pltpu.VMEM((rows.shape[0] if keep else own, frames), jnp.bfloat16),
            pltpu.VMEM((width, frames), jnp.float32),
            pltpu.VMEM((8, frames), jnp.float32),
            pltpu.VMEM((width, frames), jnp.bfloat16),
            pltpu.VMEM((frames, width), jnp.bfloat16),
        ],
        cost_estimate=small_cost,
        compiler_params=pltpu.CompilerParams(vmem_limit_bytes=62 << 20),
    )(index, rows, unit, scale, positive, masked)


def down_grad_kernel(active_ref, grad_ref, *refs):
    out_ref, turned = refs[-2:]

    @pl.when(pl.program_id(0) == 0)
    def _():
        turned[...] = grad_ref[...].T

    out_ref[...] = to_low(dot(turned[...], active_ref[...])).reshape(out_ref.shape)


def down_grad(active, grad, members, groups, after):
    count, inner = active.shape
    model = grad.shape[1]
    share = inner // members
    block = (1, groups, model // groups, share)
    return pl.pallas_call(
        down_grad_kernel,
        grid=(members,),
        in_specs=[
            pl.BlockSpec((count, share), lambda i: (0, i)),
            pl.BlockSpec((count, model), lambda i: (0, 0)),
        ]
        + [pl.BlockSpec(memory_space=pl.ANY)] * len(after),
        out_specs=pl.BlockSpec(block, lambda i: (i, 0, 0, 0)),
        out_shape=jax.ShapeDtypeStruct((members, groups, model // groups, share), jnp.bfloat16),
        scratch_shapes=[pltpu.VMEM((model, count), jnp.bfloat16)],
        cost_estimate=small_cost,
        compiler_params=pltpu.CompilerParams(vmem_limit_bytes=62 << 20),
    )(active, grad, *after)


def up_grad_kernel(
    groups, core_ref, hidden_ref, upper_ref, attended_ref, branch_ref, output_ref, final_ref, *refs
):
    kept_ref, sent_ref, turned, attended_turned, held = refs[-5:]
    group = pl.program_id(0)
    core = core_ref[0]
    lines, share = kept_ref.shape[1], kept_ref.shape[2]

    @pl.when(group == 0)
    def _():
        turned[...] = hidden_ref[...].T
        attended_turned[...] = attended_ref[...].T

    wide = upper_ref.shape[1]
    side = final_ref.shape[1]
    held[:, :, :, :wide] = to_low(dot(turned[...], upper_ref[...])).reshape(lines, 2, share, wide)

    @pl.when(group < groups - 1)
    def _():
        value = dot(attended_turned[...], branch_ref[...])
        held[:, :, :, wide:] = to_low(value).reshape(lines, 2, share, side)

    @pl.when(group == groups - 1)
    def _():
        value = dot(output_ref[...], final_ref[...], TN)
        held[:, :, :, wide:] = to_low(value).reshape(lines, 2, share, side)

    kept_ref[0] = held[:, core]
    sent_ref[0] = held[:, 1 - core]


def up_grad(core, hidden, upper, attended, branch, output, final, members, groups, after):
    count, model = hidden.shape
    wide, side = upper.shape[1] // groups, final.shape[1]
    lines, share = members // 2, model // members
    whole = lambda columns: pl.BlockSpec((count, columns), lambda g, core: (0, 0))
    out = pl.BlockSpec((1, lines, share, wide + side), lambda g, core: (g, 0, 0, 0))
    shape = jax.ShapeDtypeStruct((groups, lines, share, wide + side), jnp.bfloat16)
    last = model // side - 1
    return pl.pallas_call(
        functools.partial(up_grad_kernel, groups),
        grid_spec=pltpu.PrefetchScalarGridSpec(
            num_scalar_prefetch=1,
            grid=(groups,),
            in_specs=[
                whole(model),
                pl.BlockSpec((count, wide), lambda g, core: (0, g)),
                whole(model),
                pl.BlockSpec((count, side), lambda g, core: (0, jnp.minimum(g, last))),
                whole(model),
                whole(side),
            ]
            + [pl.BlockSpec(memory_space=pl.ANY)] * len(after),
            out_specs=[out, out],
            scratch_shapes=[
                pltpu.VMEM((model, count), jnp.bfloat16),
                pltpu.VMEM((model, count), jnp.bfloat16),
                pltpu.VMEM((lines, 2, share, wide + side), jnp.bfloat16),
            ],
        ),
        out_shape=[shape, shape],
        cost_estimate=small_cost,
        compiler_params=pltpu.CompilerParams(vmem_limit_bytes=62 << 20),
    )(core, hidden, upper, attended, branch, output, final, *after)


def projection_grad_kernel(grads, core_ref, frames_ref, *refs):
    kept_ref, sent_ref, held = refs[-3:]
    core = core_ref[0]
    turned = frames_ref[...].T
    each = kept_ref.shape[3] // PAIR
    tile = 0
    for number, ref in enumerate(refs[:grads]):
        if len(ref.shape) == 2:
            held[...] = to_low(dot(turned, ref[...])).reshape(held.shape)
        else:
            held[...] = ref[...]
        for column in range(held.shape[3] // PAIR):
            group, lanes = tile // each, pl.ds(tile % each * PAIR, PAIR)
            at = pl.ds(column * PAIR, PAIR)
            kept_ref[group, :, :, lanes] = held[:, core, :, at]
            sent_ref[group, :, :, lanes] = held[:, 1 - core, :, at]
            tile += 1


def projection_grad(core, frames, grads, extra, members, groups, after):
    count, model = frames.shape
    lines, share = members // 2, model // members
    pieces = [*grads, *extra]
    width = grads[0].shape[1]
    shape = jax.ShapeDtypeStruct((groups, lines, share, len(pieces) * width // groups), jnp.bfloat16)
    vmem = pl.BlockSpec(memory_space=pltpu.VMEM)
    return pl.pallas_call(
        functools.partial(projection_grad_kernel, len(pieces)),
        in_specs=[pl.BlockSpec(memory_space=pltpu.SMEM)]
        + [vmem] * (1 + len(pieces))
        + [pl.BlockSpec(memory_space=pl.ANY)] * len(after),
        out_specs=[vmem, vmem],
        out_shape=[shape, shape],
        scratch_shapes=[pltpu.VMEM((lines, 2, share, width), jnp.bfloat16)],
        cost_estimate=small_cost,
        compiler_params=pltpu.CompilerParams(vmem_limit_bytes=62 << 20),
    )(core, frames, *pieces, *after)


def slot_rows(distractors, members):
    count, slots = distractors.shape
    turns = -(-slots // members)
    padded = jnp.pad(distractors, ((0, 0), (0, turns * members - slots)), constant_values=-1)
    padded = padded.T.reshape(turns, members, count)
    period = members // math.gcd(slots, members)
    frame = jnp.arange(count, dtype=jnp.int32) % period
    placed = padded
    for phase in range(1, period):
        turned = jnp.roll(padded, phase * slots % members, axis=1)
        placed = jnp.where(frame == phase, turned, placed)
    return placed.transpose(1, 0, 2)


def target_kernel(came_ref, part_ref, unit_ref, scale_ref, low_ref, matrix_ref, *refs):
    grad_ref, matrix_grad_ref, sums_ref = refs[-3:]
    grad_unit = part_ref[...] + came_ref[...].astype(jnp.float32)
    unit = unit_ref[...]
    inner = jnp.sum(grad_unit * unit, axis=-1, keepdims=True)
    low = to_low(scale_ref[:, 0:1] * (grad_unit - unit * inner))
    grad_ref[...] = dot(low, to_low(matrix_ref[...]), NT)
    matrix_grad_ref[...] = dot(to_low(low_ref[...]), low, TN)
    sums_ref[...] = jnp.sum(low.astype(jnp.float32).reshape(-1, 8, low.shape[1]), axis=0)


def target_back(came, part, unit, scale, low, matrix, after):
    count, width = part.shape
    vmem = pl.BlockSpec(memory_space=pltpu.VMEM)
    shape = jax.ShapeDtypeStruct
    return pl.pallas_call(
        target_kernel,
        in_specs=[vmem] * 6 + [pl.BlockSpec(memory_space=pl.ANY)] * len(after),
        out_specs=[vmem] * 3,
        out_shape=[
            shape((count, width), jnp.float32),
            shape((width, width), jnp.float32),
            shape((8, width), jnp.float32),
        ],
        cost_estimate=small_cost,
        compiler_params=pltpu.CompilerParams(vmem_limit_bytes=62 << 20),
    )(came, part, unit, scale, low, matrix, *after)


def inputs_kernel(parts, resid_ref, *refs):
    out_ref, low_ref = refs[-2:]

    @pl.when(pl.program_id(0) == 0)
    def _():
        for matrix in range(3):
            low_ref[matrix] = to_low(refs[3 * parts + matrix][...])

    total = resid_ref[...]
    for matrix in range(3):
        low = 0
        for part in range(parts):
            grad_ref = refs[matrix * parts + part]
            high = low + grad_ref.shape[1]
            total = total + dot(grad_ref[...], low_ref[matrix, :, low:high], NT)
            low = high
    out_ref[...] = total


def inputs_back(resid, grads, matrices, block, after):
    count, model = resid.shape
    part = lambda x: pl.BlockSpec((block, x.shape[1]), lambda i: (i, 0))
    flat = [g for parts in grads for g in parts]
    return pl.pallas_call(
        functools.partial(inputs_kernel, len(grads[0])),
        grid=(count // block,),
        in_specs=[part(resid)]
        + [part(g) for g in flat]
        + [rows_of(m) for m in matrices]
        + [pl.BlockSpec(memory_space=pl.ANY)] * len(after),
        out_specs=part(resid),
        out_shape=jax.ShapeDtypeStruct(resid.shape, jnp.float32),
        scratch_shapes=[pltpu.VMEM((3, model, model), jnp.bfloat16)],
        cost_estimate=small_cost,
        compiler_params=pltpu.CompilerParams(vmem_limit_bytes=62 << 20),
    )(resid, *flat, *matrices, *after)


def target_prepare_kernel(targets_ref, matrix_ref, bias_ref, rows_ref, unit_ref, turned_ref, scale_ref):
    low = to_low(dot(to_low(targets_ref[...]), to_low(matrix_ref[...])) + bias_ref[...].reshape(1, -1))
    positive = low.astype(jnp.float32)
    scale = lax.rsqrt(jnp.sum(positive * positive, axis=-1, keepdims=True) + cosine_eps)
    unit = positive * scale
    rows_ref[...] = to_low(unit * (log2e / similarity_softening_factor))
    unit_ref[...] = unit
    turned_ref[...] = unit.T
    scale_ref[...] = jnp.broadcast_to(scale, scale_ref.shape)


def target_prepare(targets, matrix, bias):
    count, width = targets.shape
    vmem = pl.BlockSpec(memory_space=pltpu.VMEM)
    shape = jax.ShapeDtypeStruct
    return pl.pallas_call(
        target_prepare_kernel,
        in_specs=[vmem] * 3,
        out_specs=[vmem] * 4,
        out_shape=[
            shape((count, width), jnp.bfloat16),
            shape((count, width), jnp.float32),
            shape((width, count), jnp.float32),
            shape((count, PAIR), jnp.float32),
        ],
        cost_estimate=small_cost,
        compiler_params=pltpu.CompilerParams(vmem_limit_bytes=62 << 20),
    )(targets, matrix, bias)


def project_kernel(frames_ref, wq_ref, wk_ref, wv_ref, bq_ref, bv_ref, *refs):
    low_ref, q_ref, k_ref, v_ref, mq, mk, mv = refs[-7:]

    @pl.when(pl.program_id(0) == 0)
    def _():
        mq[...] = to_low(wq_ref[...])
        mk[...] = to_low(wk_ref[...])
        mv[...] = to_low(wv_ref[...])

    low = to_low(frames_ref[...])
    low_ref[...] = low
    q_ref[...] = to_low(dot(low, mq[...]) + bq_ref[...].reshape(1, -1))
    k_ref[...] = to_low(dot(low, mk[...]))
    v_ref[...] = to_low(dot(low, mv[...]) + bv_ref[...].reshape(1, -1))


def vector_spec(values):
    return pl.BlockSpec(values.shape, lambda i, *_: (0,))


def project(frames, w_query, w_key, w_value, b_query, b_value, block, after):
    count, model = frames.shape
    part = pl.BlockSpec((block, model), lambda i: (i, 0))
    return pl.pallas_call(
        project_kernel,
        grid=(count // block,),
        in_specs=[part]
        + [rows_of(w) for w in (w_query, w_key, w_value)]
        + [vector_spec(b) for b in (b_query, b_value)]
        + [pl.BlockSpec(memory_space=pl.ANY)] * len(after),
        out_specs=[part] * 4,
        out_shape=[jax.ShapeDtypeStruct((count, model), jnp.bfloat16)] * 4,
        scratch_shapes=[pltpu.VMEM((model, model), jnp.bfloat16)] * 3,
        cost_estimate=small_cost,
        compiler_params=pltpu.CompilerParams(vmem_limit_bytes=62 << 20),
    )(frames, w_query, w_key, w_value, b_query, b_value, *after)


def exchange(sent):
    members = lax.axis_size("tm")
    return lax.ppermute(sent, "tm", [(i, i ^ 1) for i in range(members)])


def split_kernel(counts, pieces, choice_ref, *refs):
    out_refs = refs[-pieces:]
    number, low, lanes = 0, 0, 0
    for count in counts:
        total = refs[number][0].astype(jnp.float32)
        for term in range(1, count):
            total = total + refs[number + term][0].astype(jnp.float32)
        total = to_low(total)
        high = lanes + total.shape[-1]
        for piece in range(pieces):

            @pl.when(pl.program_id(0) == piece)
            def _(piece=piece, total=total, low=low, lanes=lanes, high=high):
                if total.ndim == 3:
                    out_refs[piece][low : low + total.shape[0]] = total
                else:
                    out_refs[piece][:, lanes:high] = total

        number, low, lanes = number + count, low + total.shape[0], high


def split_sum(choice, sums, pieces, after):
    terms = [term for group in sums for term in group]
    first = [group[0].shape[1:] for group in sums]
    if len(first[0]) == 3:
        rest = (sum(shape[0] for shape in first), *first[0][1:])
    else:
        rest = (first[0][0], sum(shape[1] for shape in first))

    def source(term):
        zeros = (0,) * (term.ndim - 1)
        return pl.BlockSpec((1, *term.shape[1:]), lambda i, choice: (choice[0] ^ i, *zeros))

    return pl.pallas_call(
        functools.partial(split_kernel, [len(group) for group in sums], pieces),
        grid_spec=pltpu.PrefetchScalarGridSpec(
            num_scalar_prefetch=1,
            grid=(pieces,),
            in_specs=[source(term) for term in terms]
            + [pl.BlockSpec(memory_space=pl.ANY)] * len(after),
            out_specs=[pl.BlockSpec(rest, lambda i, choice: (0,) * len(rest))] * pieces,
        ),
        out_shape=[jax.ShapeDtypeStruct(rest, jnp.bfloat16)] * pieces,
        cost_estimate=small_cost,
        compiler_params=pltpu.CompilerParams(vmem_limit_bytes=62 << 20),
    )(choice, *terms, *after)


def swap(pieces, axis="grp", stride=1):
    size = lax.axis_size(axis)
    return [pieces[0]] + [
        lax.ppermute(piece, axis, [(i, i ^ (k * stride)) for i in range(size)])
        for k, piece in enumerate(pieces)
        if k
    ]


def line_kernel(terms, *refs):
    total = refs[0][...].astype(jnp.float32)
    for term in range(1, terms):
        total = total + refs[term][...].astype(jnp.float32)
    refs[-1][...] = to_low(total)


def line_sum(terms, after):
    lines, rest = terms[0].shape[0], terms[0].shape[1:]
    block = pl.BlockSpec((1, *rest), lambda i: (i, *(0,) * len(rest)))
    return pl.pallas_call(
        functools.partial(line_kernel, len(terms)),
        grid=(lines,),
        in_specs=[block] * len(terms) + [pl.BlockSpec(memory_space=pl.ANY)] * len(after),
        out_specs=block,
        out_shape=jax.ShapeDtypeStruct(terms[0].shape, jnp.bfloat16),
        cost_estimate=small_cost,
        compiler_params=pltpu.CompilerParams(vmem_limit_bytes=62 << 20),
    )(*terms, *after)


def core_pairs():
    return [[2 * i, 2 * i + 1] for i in range(lax.axis_size("tm") // 2)]


def chip_lines():
    return [list(range(first, lax.axis_size("tm"), 2)) for first in range(2)]


def scatter(value, axis, among=None):
    return lax.psum_scatter(value, axis, scatter_dimension=0, axis_index_groups=among)


def over_lines(value):
    return lax.all_to_all(value, "tm", 0, 0, tiled=True, axis_index_groups=chip_lines())


def share_kernel(start, done_ref, line_ref, out_ref):
    wide = done_ref.shape[2]
    total = line_ref[0].astype(jnp.float32)
    for term in range(1, line_ref.shape[0]):
        total = total + line_ref[term].astype(jnp.float32)
    total = to_low(total)
    for copy in range(out_ref.shape[0]):
        low = 0
        for at in range(start, done_ref.shape[0]):
            out_ref[copy, :, low : low + wide] = done_ref[at]
            low += wide
        out_ref[copy, :, low:] = total


def shares(done, lines, start, groups):
    rows = done.shape[1]
    wide = (done.shape[0] - start) * done.shape[2] + lines.shape[2]
    vmem = pl.BlockSpec(memory_space=pltpu.VMEM)
    return pl.pallas_call(
        functools.partial(share_kernel, start),
        in_specs=[vmem] * 2,
        out_specs=vmem,
        out_shape=jax.ShapeDtypeStruct((groups, rows, wide), jnp.bfloat16),
        cost_estimate=small_cost,
        compiler_params=pltpu.CompilerParams(vmem_limit_bytes=62 << 20),
    )(done, lines)


def place(kernel, arrays, shapes, after, choice=None):
    vmem = pl.BlockSpec(memory_space=pltpu.VMEM)
    first = [] if choice is None else [choice]
    used = len(first) + len(arrays)
    return pl.pallas_call(
        lambda *refs: kernel(*refs[:used], *refs[used + len(after) :]),
        in_specs=[pl.BlockSpec(memory_space=pltpu.SMEM)] * len(first)
        + [vmem] * len(arrays)
        + [pl.BlockSpec(memory_space=pl.ANY)] * len(after),
        out_specs=[vmem] * len(shapes),
        out_shape=[jax.ShapeDtypeStruct(s, jnp.float32) for s in shapes],
        cost_estimate=small_cost,
        compiler_params=pltpu.CompilerParams(vmem_limit_bytes=62 << 20),
    )(*first, *arrays, *after)


def line_total(terms, after):
    vmem = pl.BlockSpec(memory_space=pltpu.VMEM)
    return pl.pallas_call(
        functools.partial(line_kernel, len(terms)),
        in_specs=[vmem] * len(terms) + [pl.BlockSpec(memory_space=pl.ANY)] * len(after),
        out_specs=vmem,
        out_shape=jax.ShapeDtypeStruct(terms[0].shape, jnp.bfloat16),
        cost_estimate=small_cost,
        compiler_params=pltpu.CompilerParams(vmem_limit_bytes=62 << 20),
    )(*terms, *after)


def on_device(
    frames,
    targets,
    lengths,
    span_starts,
    distractors,
    w_query,
    b_query,
    w_key,
    w_value,
    b_value,
    w_out,
    b_out,
    norm_gain,
    norm_bias,
    w_up,
    b_up,
    w_down,
    b_down,
    final_gain,
    final_bias,
    w_final,
    b_final,
    w_target,
    b_target,
):
    count, model = frames.shape
    width = targets.shape[1]
    inner = w_up.shape[1]
    members, groups = lax.axis_size("tm"), lax.axis_size("grp")
    block = min(count, 256)
    share = model // members
    place_in_line = lax.axis_index("tm")
    core = (place_in_line % 2)[None].astype(jnp.int32)
    line = (place_in_line // 2)[None].astype(jnp.int32)
    group = lax.axis_index("grp")[None].astype(jnp.int32)

    own_rows, positive_unit, positive_turned, positive_scale = target_prepare(targets, w_target, b_target)
    rows = lax.all_gather(own_rows, "tm", tiled=True)
    index = slot_rows(distractors, members)

    segment = segment_ids(lengths[0], count)
    masked = span_mask(span_starts, segment, count)
    span, hot_query, hot_key = attention_plan(lengths[0], segment, count, block, block)
    frames_low, query, key, value = project(
        frames, w_query, w_key, w_value, b_query, b_value, block, (own_rows,)
    )
    attended_low, log_total, out_matrix, up_matrix, down_matrix, final_matrix = attend(
        span, query, key, value, hot_query, hot_key, (w_out, w_up, w_down, w_final), block, block, 2
    )
    (
        hidden_low,
        normed_one,
        active_low,
        slope,
        normed_two,
        output_low,
        scales,
        final_unit,
        final_scale,
    ) = feed_forward(
        attended_low,
        frames,
        out_matrix,
        up_matrix,
        down_matrix,
        final_matrix,
        (b_out, norm_gain, norm_bias, b_down, final_gain, final_bias, b_up, b_final),
        block,
    )
    losses, d_final_low, positive_part, d_rows = candidates(
        index, rows, final_unit, final_scale, positive_turned, masked[None]
    )
    came = lax.psum_scatter(d_rows, "tm", scatter_dimension=0, tiled=True)

    d_down_low, d_upper_low, d_resid, d_branch_low, d_attended_low, model_sums, up_sums = feed_forward_back(
        d_final_low,
        slope,
        normed_one,
        normed_two,
        scales,
        final_matrix,
        up_matrix,
        down_matrix,
        out_matrix,
        (norm_gain, final_gain),
        block,
    )
    def attention_back(piece, pieces, after):
        return attend_back(
            span,
            query,
            key,
            value,
            d_attended_low,
            hot_query,
            hot_key,
            log_total,
            block,
            block,
            2,
            piece,
            pieces,
            after,
        )


    def total(values):
        return jnp.sum(values, axis=0)

    def vector_sums(piece_sums, target_sums):
        return (
            jnp.concatenate([total(s[0]) for s in piece_sums]),
            jnp.concatenate([total(s[1]) for s in piece_sums]),
            total(model_sums[5]),
            total(model_sums[3]),
            total(model_sums[4]),
            total(up_sums),
            total(model_sums[2]),
            total(model_sums[0]),
            total(model_sums[1]),
            column_sum(d_final_low),
            total(target_sums),
        )

    if share % 16 or (inner // members) % PAIR or model != (groups - 1) * width:
        back = [attention_back(piece, 3, ()) for piece in range(3)]
        d_query, d_key, d_value, piece_sums = ([part[k] for part in back] for k in range(4))
        target_grad, grad_w_target, target_sums = target_back(
            came, positive_part, positive_unit, positive_scale, targets, w_target, ()
        )
        input_grad = inputs_back(
            d_resid, (d_query, d_key, d_value), (w_query, w_key, w_value), block, ()
        )

        def reduced(grad):
            part = lax.psum_scatter(grad, "tm", scatter_dimension=0, tiled=True)
            return lax.psum(to_low(part), "grp").astype(jnp.float32)

        def projected(parts):
            return reduced(product_left(frames_low, jnp.concatenate(parts, axis=1)))

        small = [reduced(vector) for vector in vector_sums(piece_sums, target_sums)]
        return (
            losses[0],
            input_grad,
            target_grad,
            projected(d_query),
            small[0],
            projected(d_key),
            projected(d_value),
            small[1],
            reduced(product_left(attended_low, d_branch_low)),
            small[2],
            small[3],
            small[4],
            reduced(product_left(hidden_low, d_upper_low)),
            small[5],
            reduced(product_left(active_low, d_down_low)),
            small[6],
            small[7],
            small[8],
            reduced(product_left(output_low, d_final_low)),
            small[9],
            reduced(grad_w_target),
            small[10],
        )

    down_parts = down_grad(active_low, d_down_low, members, groups, ())
    down_part = scatter(down_parts, "tm")
    up_kept, up_sent = up_grad(
        core,
        hidden_low,
        d_upper_low,
        attended_low,
        d_branch_low,
        output_low,
        d_final_low,
        members,
        groups,
        (down_parts,),
    )
    up_came = exchange(up_sent)
    target_grad, grad_w_target, target_sums = target_back(
        came, positive_part, positive_unit, positive_scale, targets, w_target, (up_sent,)
    )
    up_group = split_sum(group, [[up_kept, up_came]], groups, (grad_w_target,))
    up_groups = swap(up_group)

    def projections(pieces, extra, after):
        grads = [back[piece][k] for k in range(3) for piece in pieces]
        return projection_grad(core, frames_low, grads, extra, members, groups, after)

    back = [attention_back(0, 3, (up_group[1],))]
    back.append(attention_back(1, 3, (back[0][0],)))
    early_kept, early_sent = projections((0, 1), [], (back[1][0],))
    early_came = exchange(early_sent)
    up_line = line_sum(up_groups, (early_sent,))
    up_lines = over_lines(up_line)
    early_group = split_sum(
        group,
        [[early_kept, early_came], [down_part.reshape(groups, -1, share, inner // members)]],
        groups,
        (up_line,),
    )
    early_groups = swap(early_group)
    back.append(attention_back(2, 3, (early_group[1],)))
    early_line = line_sum(early_groups, (back[2][0],))
    most_shares = shares(early_line, up_lines, members // 2, groups)
    most = lax.all_to_all(most_shares, "grp", 0, 0, tiled=True)
    d_query, d_key, d_value, piece_sums = ([part[k] for part in back] for k in range(4))
    summed = vector_sums(piece_sums, target_sums)
    lines_of = []
    for vector in summed:
        part = vector.reshape(members, -1)
        lanes = -(-part.shape[1] // PAIR) * PAIR
        part = jnp.pad(part, ((0, 0), (0, lanes - part.shape[1])))
        lines_of.append(part.reshape(members, -1, PAIR))
    counts = [part.shape[1] for part in lines_of]
    joined = jnp.concatenate(lines_of, axis=1)
    square = grad_w_target.reshape(members, width // members, width // PAIR, PAIR)
    square = square.transpose(0, 2, 1, 3).reshape(members, -1, PAIR)
    extra = jnp.concatenate(
        [jnp.pad(x, ((0, 0), (0, share - x.shape[1]), (0, 0))) for x in (joined, square)], axis=2
    )
    extra = to_low(extra).reshape(members // 2, 2, share, 2 * PAIR)
    late_kept, late_sent = projections((2,), [extra], (most_shares,))
    late_came = exchange(late_sent)
    late_group = split_sum(group, [[late_kept, late_came]], groups, (most,))
    late_groups = swap(late_group)
    input_grad = inputs_back(
        d_resid, (d_query, d_key, d_value), (w_query, w_key, w_value), block, (late_group[1],)
    )
    own_line = split_sum(line, [[early_line], late_groups], members // 2, (input_grad,))
    own_lines = swap(own_line, "tm", 2)
    up_at = inner // members * (model // groups // share)
    side_at = up_at + inner // groups

    def put_most(most_ref, down_ref, up_ref, out_ref, final_ref):
        rows = model // groups
        for at in range(groups):
            part = lambda low, high: most_ref[at, :, low:high].astype(jnp.float32)
            for top in range(rows // share):
                low = at * rows + top * share
                wide = inner // members
                down_ref[:, low : low + share] = part(top * wide, (top + 1) * wide).T
            wide = inner // groups
            up_ref[:, at * wide : (at + 1) * wide] = part(up_at, side_at)
            if at < groups - 1:
                out_ref[:, at * width : (at + 1) * width] = part(side_at, side_at + width)
            else:
                final_ref[...] = part(side_at, side_at + width)

    grad_down, grad_up, grad_out, grad_final = place(
        put_most,
        [most],
        [(inner // members, model), (share, inner), (share, model), (share, width)],
        (own_line[1],),
    )
    last = swap([line_total(own_lines, (grad_down,))] * groups)
    third = model // 3
    early = [(k, piece * third + at) for k in range(3) for piece in (0, 1) for at in range(0, third, PAIR)]
    late = [(k, 2 * third + at) for k in range(3) for at in range(0, third, PAIR)]
    late += [(3, at) for at in range(0, 2 * PAIR, PAIR)]

    def put_last(choice_ref, *refs):
        outs = refs[groups:]
        for piece in range(groups):
            at = choice_ref[0] ^ piece
            for number in range(groups):

                @pl.when(at == number)
                def _(piece=piece, number=number):
                    low = 0
                    for tiles in (early, late):
                        each = len(tiles) // groups
                        for k, lanes in tiles[number * each : (number + 1) * each]:
                            value = refs[piece][:, low : low + PAIR].astype(jnp.float32)
                            low += PAIR
                            if k < 3:
                                outs[k][:, lanes : lanes + PAIR] = value
                            elif lanes:
                                rows = width // members
                                for half in range(width // PAIR):
                                    part = value[half * rows : (half + 1) * rows]
                                    outs[3][:, half * PAIR : (half + 1) * PAIR] = part
                            else:
                                row = 0
                                for count_rows, out in zip(counts, outs[4:]):
                                    for start in range(0, out.shape[0], PAIR):
                                        size = min(PAIR, out.shape[0] - start)
                                        out[start : start + size] = value[row, :size]
                                        row += 1

    grad_query, grad_key, grad_value, grad_target, *small = place(
        put_last,
        last,
        [(share, model)] * 3
        + [(width // members, width)]
        + [(vector.shape[0] // members,) for vector in summed],
        (),
        group,
    )
    return (
        losses[0],
        input_grad,
        target_grad,
        grad_query,
        small[0],
        grad_key,
        grad_value,
        small[1],
        grad_out,
        small[2],
        small[3],
        small[4],
        grad_up,
        small[5],
        grad_down,
        small[6],
        small[7],
        small[8],
        grad_final,
        small[9],
        grad_target,
        small[10],
    )


def solution(mesh):
    placed = (
        P(("grp", "tm"), None),
        P(("grp", "tm"), None),
        P(("grp", "tm"), None),
        P(("grp", "tm")),
        P(("grp", "tm"), None),
        P(),
        P(),
        P(),
        P(),
        P(),
        P(),
        P(),
        P(),
        P(),
        P(),
        P(),
        P(),
        P(),
        P(),
        P(),
        P(),
        P(),
        P(),
        P(),
    )
    return jax.shard_map(
        on_device,
        mesh=mesh,
        in_specs=placed,
        out_specs=(
            P(("grp", "tm")),
            P(("grp", "tm"), None),
            P(("grp", "tm"), None),
            P("tm", None),
            P("tm"),
            P("tm", None),
            P("tm", None),
            P("tm"),
            P("tm", None),
            P("tm"),
            P("tm"),
            P("tm"),
            P("tm", None),
            P("tm"),
            P("tm", None),
            P("tm"),
            P("tm"),
            P("tm"),
            P("tm", None),
            P("tm"),
            P("tm", None),
            P("tm"),
        ),
        check_vma=False,
    )
```

```python
import functools
import math

import jax
import jax.numpy as jnp
from jax import lax
from jax.experimental import pallas as pl
from jax.experimental.pallas import tpu as pltpu
from jax.sharding import PartitionSpec as P

H = 12
HD = 64
NEG = 100
SPAN = 10


norm_eps = 1e-05
cosine_eps = 1e-06
similarity_softening_factor = 0.1
log2e = 1.4426950408889634
PAIR = 2 * HD
COLUMNS = 256
NT = (((1,), (1,)), ((), ()))
TN = (((0,), (0,)), ((), ()))
large_cost = pl.CostEstimate(flops=23_000_000_000, bytes_accessed=1, transcendentals=0)
small_cost = pl.CostEstimate(flops=1, bytes_accessed=1, transcendentals=0)


def to_low(values):
    return values.astype(jnp.bfloat16)


def product(left, right):
    return jnp.dot(left, right, preferred_element_type=jnp.float32)


def product_left(left, right):
    return lax.dot_general(
        left, right, (((0,), (0,)), ((), ())), preferred_element_type=jnp.float32
    )


def product_right(left, right):
    return lax.dot_general(
        left, right, (((1,), (1,)), ((), ())), preferred_element_type=jnp.float32
    )


def column_sum(values):
    return jnp.sum(values.astype(jnp.float32), axis=0)


def exact_gelu(values):
    return jax.nn.gelu(values, approximate=False)


def layer_norm(values, gain, bias):
    center = values - jnp.mean(values, axis=-1, keepdims=True)
    scale = lax.rsqrt(jnp.mean(center * center, axis=-1, keepdims=True) + norm_eps)
    normed = center * scale
    return (normed * gain + bias, normed, scale)


def layer_norm_back(grad, normed, scale, gain):
    grad_normed = grad * gain
    inner = (
        grad_normed
        - jnp.mean(grad_normed, axis=-1, keepdims=True)
        - normed * jnp.mean(grad_normed * normed, axis=-1, keepdims=True)
    )
    return (inner * scale, jnp.sum(grad * normed, axis=0), jnp.sum(grad, axis=0))


def segment_ids(lengths_row, count):
    bounds = jnp.cumsum(lengths_row)
    position = jnp.arange(count, dtype=jnp.int32)
    return jnp.sum((position[:, None] >= bounds[None, :]).astype(jnp.int32), axis=1)


def span_mask(starts, segment, count):
    covered = jnp.zeros((count,), jnp.float32)
    for offset in range(SPAN):
        earlier = jnp.concatenate([jnp.zeros((offset,), jnp.int32), starts[: count - offset]])
        earlier_segment = jnp.concatenate(
            [jnp.full((offset,), -1, jnp.int32), segment[: count - offset]]
        )
        hit = jnp.where(earlier_segment == segment, earlier, 0).astype(jnp.float32)
        covered = jnp.maximum(covered, hit)
    return covered


def dot(a, b, dims=(((1,), (0,)), ((), ()))):
    return lax.dot_general(a, b, dims, preferred_element_type=jnp.float32)

def first_half(rows):
    return lax.broadcasted_iota(jnp.int32, (rows, PAIR), 1) < HD


def windows(span_ref, block, chunk, count, body):
    i = pl.program_id(0)
    start, chunks = span_ref[0, i], span_ref[1, i]
    total = count // chunk
    sizes = list(range(2, total + 1))
    for size in sizes:
        hit = (chunks <= size) if size == sizes[0] else (chunks == size)

        @pl.when(hit)
        def _(size=size):
            at = pl.multiple_of(jnp.minimum(start, total - size) * chunk, chunk)
            body(at, size * chunk)


def either(first, one, other, half):
    return jnp.where(first, one, other) if half == 0 else jnp.where(first, other, one)


def forward_kernel(casts, pairs, chunk, unroll, span_ref, q_ref, k_ref, v_ref, hotq_ref, hotk_ref, *refs):
    sources, out_ref, log_ref = refs[:casts], refs[casts], refs[casts + 1]
    results = refs[casts + 2 : 2 * casts + 2]
    wides, lows = refs[2 * casts + 2 : 3 * casts + 2], refs[3 * casts + 2 : 4 * casts + 2]
    in_sems, out_sems = refs[-2:]
    step = pl.program_id(0)

    def copies(pairs_of, sems):
        return [
            pltpu.make_async_copy(source, target, sems.at[number])
            for number, (source, target) in enumerate(pairs_of)
        ]

    @pl.when(step == 0)
    def _():
        for copy in copies(zip(sources, wides), in_sems):
            copy.start()

    block = q_ref.shape[0]
    count = k_ref.shape[0]
    scale = HD**-0.5 * log2e

    def body(at, size):
        near = pl.ds(at, size)
        lane = lax.broadcasted_iota(jnp.int32, (block, PAIR), 1)
        first_q, first_k = first_half(block), first_half(size)
        ones = jnp.ones((size, PAIR), jnp.bfloat16)

        def pair(p, logs):
            cols = pl.ds(pl.multiple_of(p * PAIR, PAIR), PAIR)
            q, k, v = q_ref[:, cols], k_ref[near, cols], v_ref[near, cols]
            hotq, hotk = hotq_ref[...], hotk_ref[near, :]
            outs = []
            for half in range(2):
                scores = dot(either(first_q, q, hotq, half), either(first_k, k, hotk, half), NT)
                top = jnp.max(scores, axis=1, keepdims=True) * scale
                raised = to_low(jnp.exp2(scores * scale - top))
                result = dot(raised, either(first_k, v, ones, half))
                spare = HD * (1 - half)
                total = result[:, spare : spare + 1]
                outs.append(result * (1.0 / total))
                logs = jnp.where(lane == 2 * p + half, top + jnp.log2(total), logs)
            out_ref[:, cols] = to_low(jnp.where(first_q, outs[0], outs[1]))
            return logs

        empty = jnp.zeros((block, PAIR), jnp.float32)
        log_ref[...] = lax.fori_loop(0, pairs, pair, empty, unroll=unroll)

    windows(span_ref, block, chunk, count, body)

    @pl.when(step == 0)
    def _():
        for copy, wide, low in zip(copies(zip(sources, wides), in_sems), wides, lows):
            copy.wait()
            low[...] = to_low(wide[...])
        for copy in copies(zip(lows, results), out_sems):
            copy.start()

    @pl.when(step == pl.num_programs(0) - 1)
    def _():
        for copy in copies(zip(lows, results), out_sems):
            copy.wait()


def attend(span, query, key, value, hotq, hotk, casts, block, chunk, unroll):
    count, width = query.shape
    whole = lambda w: pl.BlockSpec((count, w), lambda i, *_: (0, 0))
    part = lambda w: pl.BlockSpec((block, w), lambda i, *_: (i, 0))
    anywhere = [pl.BlockSpec(memory_space=pl.ANY)] * len(casts)
    shape = jax.ShapeDtypeStruct
    return pl.pallas_call(
        functools.partial(forward_kernel, len(casts), width // PAIR, chunk, unroll),
        grid_spec=pltpu.PrefetchScalarGridSpec(
            num_scalar_prefetch=1,
            grid=(count // block,),
            in_specs=[part(width), whole(width), whole(width), part(PAIR), whole(PAIR)] + anywhere,
            out_specs=[part(width), part(PAIR)] + anywhere,
            scratch_shapes=[pltpu.VMEM(x.shape, jnp.float32) for x in casts]
            + [pltpu.VMEM(x.shape, jnp.bfloat16) for x in casts]
            + [pltpu.SemaphoreType.DMA((len(casts),))] * 2,
        ),
        out_shape=[shape((count, width), jnp.bfloat16), shape((count, PAIR), jnp.float32)]
        + [shape(x.shape, jnp.bfloat16) for x in casts],
        cost_estimate=small_cost,
        compiler_params=pltpu.CompilerParams(vmem_limit_bytes=62 << 20),
    )(span, query, key, value, hotq, hotk, *casts)


def thirds(values):
    high = to_low(values)
    rest = values - high.astype(jnp.float32)
    middle = to_low(rest)
    return high, middle, to_low(rest - middle.astype(jnp.float32))


def backward_kernel(
    kinds,
    pairs,
    chunk,
    unroll,
    piece,
    span_ref,
    q_ref,
    k_ref,
    v_ref,
    g_ref,
    o_ref,
    hotq_ref,
    hotk_ref,
    log_ref,
    *refs,
):
    dq_ref, dk_ref, dv_ref, sums_ref, dk_sum, dv_sum = refs[-6:]
    block = q_ref.shape[0]
    count = k_ref.shape[0]
    scale = HD**-0.5 * log2e

    @pl.when(pl.program_id(0) == 0)
    def _():
        dk_sum[...] = jnp.zeros_like(dk_sum)
        dv_sum[...] = jnp.zeros_like(dv_sum)
        sums_ref[...] = jnp.zeros_like(sums_ref)

    def body(at, size):
        near = pl.ds(at, size)
        lane = lax.broadcasted_iota(jnp.int32, (block, PAIR), 1)
        first_q, first_k = first_half(block), first_half(size)
        spare = lax.rem(lane, HD) - kinds

        def affine(values, rest):
            for number, part in enumerate(thirds(values)):
                rest = jnp.where(spare == number, part, rest)
            return rest

        def pair(p, _):
            cols = pl.ds(pl.multiple_of(p * PAIR, PAIR), PAIR)
            q, k, v, g = q_ref[:, cols], k_ref[near, cols], v_ref[near, cols], g_ref[:, cols]
            hotq, hotk, logs = hotq_ref[...], hotk_ref[near, :], log_ref[...]
            products = g.astype(jnp.float32) * o_ref[:, cols].astype(jnp.float32)
            zero = jnp.zeros_like(g)
            dqs, dks, dvs = [], [], []
            for half in range(2):
                mine = lane == 2 * (p + piece * pairs) + half
                log = jnp.sum(jnp.where(mine, logs, 0.0), axis=1, keepdims=True)
                inner = jnp.sum(either(first_q, products, 0.0, half), axis=1, keepdims=True)
                qh = either(first_q, q, affine(log * (-1.0 / scale), hotq), half)
                gh = either(first_q, g, affine(-inner, zero), half)
                kh = either(first_k, k, hotk, half)
                vh = either(first_k, v, hotk, half)
                prob = jnp.exp2(dot(qh, kh, NT) * scale)
                d_scores = to_low(prob * dot(gh, vh, NT))
                dqs.append(dot(d_scores, k))
                dks.append(dot(d_scores, q, TN))
                dvs.append(dot(to_low(prob), g, TN))
            dq_ref[:, cols] = to_low(jnp.where(first_q, dqs[0], dqs[1]) * HD**-0.5)
            dk_sum[near, cols] += jnp.where(first_k, dks[0], dks[1])
            dv_sum[near, cols] += jnp.where(first_k, dvs[0], dvs[1])
            return 0

        lax.fori_loop(0, pairs, pair, 0, unroll=unroll)

    windows(span_ref, block, chunk, count, body)
    rounded = dq_ref[...].astype(jnp.float32)
    sums_ref[0] += jnp.sum(rounded.reshape(-1, 8, rounded.shape[1]), axis=0)

    @pl.when(pl.program_id(0) == pl.num_programs(0) - 1)
    def _():
        sums_ref[1] = jnp.sum(dv_sum[...].reshape(-1, 8, dv_sum.shape[1]), axis=0)
        dk_ref[...] = to_low(dk_sum[...] * HD**-0.5)
        dv_ref[...] = to_low(dv_sum[...])


def attend_back(
    span, query, key, value, grad, result, hotq, hotk, logs, kinds, block, chunk, unroll, piece, pieces, after
):
    count = query.shape[0]
    width = query.shape[1] // pieces
    whole = lambda w, j=0: pl.BlockSpec((count, w), lambda i, *_: (0, j))
    part = lambda w, j=0: pl.BlockSpec((block, w), lambda i, *_: (i, j))
    shape = jax.ShapeDtypeStruct
    return pl.pallas_call(
        functools.partial(backward_kernel, kinds, width // PAIR, chunk, unroll, piece),
        grid_spec=pltpu.PrefetchScalarGridSpec(
            num_scalar_prefetch=1,
            grid=(count // block,),
            in_specs=[
                part(width, piece),
                whole(width, piece),
                whole(width, piece),
                part(width, piece),
                part(width, piece),
                part(PAIR),
                whole(PAIR),
                part(PAIR),
            ]
            + [pl.BlockSpec(memory_space=pl.ANY)] * len(after),
            out_specs=[
                part(width),
                whole(width),
                whole(width),
                pl.BlockSpec((2, 8, width), lambda i, *_: (0, 0, 0)),
            ],
            scratch_shapes=[pltpu.VMEM((count, width), jnp.float32)] * 2,
        ),
        out_shape=[shape((count, width), jnp.bfloat16)] * 3 + [shape((2, 8, width), jnp.float32)],
        cost_estimate=small_cost,
        compiler_params=pltpu.CompilerParams(vmem_limit_bytes=62 << 20),
    )(span, query, key, value, grad, result, hotq, hotk, logs, *after)


def attention_plan(lengths_row, segment, count, block, chunk):
    kinds = lengths_row.shape[0]
    row = jnp.arange(count // block, dtype=jnp.int32) * block
    low = jnp.zeros_like(row)
    high = jnp.full_like(row, count)
    bound = jnp.zeros((), jnp.int32)
    for kind in range(kinds):
        low = jnp.where(row >= bound, bound, low)
        bound = bound + lengths_row[kind]
    for kind in reversed(range(kinds)):
        high = jnp.where(row + block <= bound, bound, high)
        bound = bound - lengths_row[kind]
    low = low // chunk
    high = (high + chunk - 1) // chunk
    span = jnp.stack([low, high - low]).astype(jnp.int32)
    lane = jnp.arange(PAIR, dtype=jnp.int32)[None, :] % HD
    same = lane == segment[:, None]
    hot_query = to_low(jnp.where((lane < kinds) & ~same, 1e30, 0.0))
    hot_key = to_low(jnp.where((lane >= kinds) & (lane < kinds + 3), 1.0, jnp.where(same, -1.0, 0.0)))
    return span, hot_query, hot_key


def rows_of(values):
    return pl.BlockSpec((values.shape[0], values.shape[1]), lambda i, *_: (0, 0))


def gelu_and_slope(values):
    size = jnp.abs(values) * 0.7071067811865476
    near = 1.0 / (1.0 + 0.3275911 * size)
    bell = jnp.exp2(values * values * (-0.5 * log2e))
    poly = near * (
        0.254829592
        + near * (-0.284496736 + near * (1.421413741 + near * (-1.453152027 + near * 1.061405429)))
    )
    tail = 0.5 * poly * bell
    share = jnp.where(values >= 0, 1.0 - tail, tail)
    return values * share, share + values * bell * 0.3989422804014327


def normalize(values):
    center = values - jnp.mean(values, axis=-1, keepdims=True)
    scale = lax.rsqrt(jnp.mean(center * center, axis=-1, keepdims=True) + norm_eps)
    return center * scale, scale


def normalize_back(grad, normed, scale, gain):
    moved = grad * gain
    inner = (
        moved
        - jnp.mean(moved, axis=-1, keepdims=True)
        - normed * jnp.mean(moved * normed, axis=-1, keepdims=True)
    )
    return inner * scale


def feed_forward_kernel(
    parts,
    attended_ref,
    frames_ref,
    out_ref,
    up_ref,
    down_ref,
    final_ref,
    *refs,
):
    vectors, up_bias_ref, final_bias_ref = refs[:6], refs[6], refs[7]
    (
        hidden_low_ref,
        normed_one_ref,
        active_ref,
        slope_ref,
        normed_two_ref,
        output_low_ref,
        scales_ref,
        unit_ref,
        unit_scale_ref,
    ) = refs[8:]
    vector = lambda row: vectors[row][...].reshape(1, -1)
    resid = frames_ref[...] + dot(attended_ref[...], out_ref[...]) + vector(0)
    normed, scale_one = normalize(resid)
    normed_one_ref[...] = to_low(normed)
    hidden = normed * vector(1) + vector(2)
    hidden_low = to_low(hidden)
    hidden_low_ref[...] = hidden_low
    second = hidden + vector(3)
    chunk = up_ref.shape[1] // parts
    for part in range(parts):
        at = pl.ds(part * chunk, chunk)
        upper = dot(hidden_low, up_ref[:, at]) + up_bias_ref[at].reshape(1, -1)
        active, slope = gelu_and_slope(upper)
        active = to_low(active)
        active_ref[:, at] = active
        slope_ref[:, at] = to_low(slope)
        second = second + dot(active, down_ref[at, :])
    normed, scale_two = normalize(second)
    normed_two_ref[...] = to_low(normed)
    output_low = to_low(normed * vector(4) + vector(5))
    output_low_ref[...] = output_low
    final = dot(output_low, final_ref[...]) + final_bias_ref[...].reshape(1, -1)
    turned = final.T
    unit_scale = lax.rsqrt(jnp.sum(turned * turned, axis=0, keepdims=True) + cosine_eps)
    unit_ref[...] = turned * unit_scale
    unit_scale_ref[...] = jnp.broadcast_to(unit_scale, unit_scale_ref.shape)
    lane = lax.broadcasted_iota(jnp.int32, scales_ref.shape, 1)
    scales_ref[...] = jnp.where(lane == 0, scale_one, scale_two)


def feed_forward(attended, frames, out, up, down, final, vectors, block):
    count, model = frames.shape
    inner, width = up.shape[1], final.shape[1]
    part = lambda columns: pl.BlockSpec((block, columns), lambda i: (i, 0))
    turned = lambda rows: pl.BlockSpec((rows, block), lambda i: (0, i))
    shape = jax.ShapeDtypeStruct
    low, full = jnp.bfloat16, jnp.float32
    operands = (attended, frames, out, up, down, final)
    return pl.pallas_call(
        functools.partial(feed_forward_kernel, max(inner // model, 1)),
        grid=(count // block,),
        in_specs=[part(model), part(model)]
        + [rows_of(x) for x in operands[2:]]
        + [vector_spec(x) for x in vectors],
        out_specs=[part(model), part(model), part(inner), part(inner), part(model), part(model), part(PAIR)]
        + [turned(width), turned(8)],
        out_shape=[
            shape((count, model), low),
            shape((count, model), low),
            shape((count, inner), low),
            shape((count, inner), low),
            shape((count, model), low),
            shape((count, model), low),
            shape((count, PAIR), full),
            shape((width, count), full),
            shape((8, count), full),
        ],
        cost_estimate=small_cost,
        compiler_params=pltpu.CompilerParams(vmem_limit_bytes=62 << 20),
    )(*operands, *vectors)


def feed_forward_back_kernel(
    parts,
    d_final_ref,
    slope_ref,
    normed_one_ref,
    normed_two_ref,
    scales_ref,
    final_ref,
    up_ref,
    down_ref,
    out_ref,
    gain_one_ref,
    gain_two_ref,
    down_low_ref,
    upper_low_ref,
    resid_ref,
    branch_low_ref,
    attended_low_ref,
    sums_ref,
    up_sums_ref,
    final_sums_ref,
):
    @pl.when(pl.program_id(0) == 0)
    def _():
        sums_ref[...] = jnp.zeros_like(sums_ref)
        up_sums_ref[...] = jnp.zeros_like(up_sums_ref)
        final_sums_ref[...] = jnp.zeros_like(final_sums_ref)

    def add(row, values):
        sums_ref[row] += jnp.sum(values.reshape(-1, 8, values.shape[1]), axis=0)

    d_final = d_final_ref[...]
    final_sums_ref[...] += jnp.sum(d_final.astype(jnp.float32).reshape(-1, 8, d_final.shape[1]), axis=0)
    grad = dot(d_final, final_ref[...], NT)
    normed = normed_two_ref[...].astype(jnp.float32)
    gain = gain_two_ref[...].reshape(1, -1)
    hidden = normalize_back(grad, normed, scales_ref[:, 1:2], gain)
    down_low = to_low(hidden)
    down_low_ref[...] = down_low
    add(0, grad * normed)
    add(1, grad)
    add(2, down_low.astype(jnp.float32))
    chunk = up_ref.shape[1] // parts
    for part in range(parts):
        at = pl.ds(part * chunk, chunk)
        upper = dot(down_low, down_ref[at, :], NT) * slope_ref[:, at].astype(jnp.float32)
        upper_low = to_low(upper)
        upper_low_ref[:, at] = upper_low
        up_sums_ref[:, at] += jnp.sum(upper.reshape(-1, 8, chunk), axis=0)
        hidden = hidden + dot(upper_low, up_ref[:, at], NT)
    normed = normed_one_ref[...].astype(jnp.float32)
    gain = gain_one_ref[...].reshape(1, -1)
    resid = normalize_back(hidden, normed, scales_ref[:, 0:1], gain)
    resid_ref[...] = resid
    branch_low = to_low(resid)
    branch_low_ref[...] = branch_low
    attended_low_ref[...] = to_low(dot(branch_low, out_ref[...], NT))
    add(3, hidden * normed)
    add(4, hidden)
    add(5, branch_low.astype(jnp.float32))


def feed_forward_back(d_final, slope, normed_one, normed_two, scales, final, up, down, out, gains, block):
    count, model = normed_one.shape
    inner = up.shape[1]
    part = lambda columns: pl.BlockSpec((block, columns), lambda i: (i, 0))
    shape = jax.ShapeDtypeStruct
    low, full = jnp.bfloat16, jnp.float32
    return pl.pallas_call(
        functools.partial(feed_forward_back_kernel, max(inner // model, 1)),
        grid=(count // block,),
        in_specs=[part(d_final.shape[1]), part(inner), part(model), part(model), part(PAIR)]
        + [rows_of(x) for x in (final, up, down, out)]
        + [vector_spec(x) for x in gains],
        out_specs=[part(model), part(inner), part(model), part(model), part(model)]
        + [
            pl.BlockSpec((6, 8, model), lambda i: (0, 0, 0)),
            pl.BlockSpec((8, inner), lambda i: (0, 0)),
            pl.BlockSpec((8, d_final.shape[1]), lambda i: (0, 0)),
        ],
        out_shape=[
            shape((count, model), low),
            shape((count, inner), low),
            shape((count, model), full),
            shape((count, model), low),
            shape((count, model), low),
            shape((6, 8, model), full),
            shape((8, inner), full),
            shape((8, d_final.shape[1]), full),
        ],
        cost_estimate=small_cost,
        compiler_params=pltpu.CompilerParams(vmem_limit_bytes=62 << 20),
    )(d_final, slope, normed_one, normed_two, scales, final, up, down, out, *gains)


def candidate_kernel(
    slots, owners, keep, index_ref, rows_ref, unit_ref, scale_ref, positive_ref, masked_ref,
    loss_ref, final_low_ref, positive_part_ref, rows_grad_ref,
    packed, mass, pull, total, unit_low, weighted,
):
    step = pl.program_id(0)
    frames = unit_ref.shape[1]
    own = rows_ref.shape[0]
    lanes = 128
    words = lax.broadcasted_iota(jnp.int32, (128, lanes), 0)

    def fill(at_mass):
        def count(tile, _):
            at = pl.ds(pl.multiple_of(tile * lanes, lanes), lanes)
            acc = jnp.zeros((128, lanes), jnp.int32)
            for slot in range(slots):
                index = index_ref[0, pl.ds(slot, 1), at]
                low = jnp.bitwise_and(index, 127)
                unit = jnp.where(index >= 0, jnp.left_shift(1, 4 * jnp.right_shift(index, 7)), 0)
                acc = acc + jnp.where(words == low, unit, 0)
            packed[:, at] = acc
            return 0

        lax.fori_loop(0, frames // lanes, count, 0)

        def part(nibble, _):
            at = pl.ds(pl.multiple_of(nibble * 128, 128), 128)
            cosine = dot(rows_ref[at, :], unit_low[...])
            times = jnp.bitwise_and(lax.shift_right_logical(packed[...], 4 * nibble), 15)
            value = times.astype(jnp.float32) * jnp.exp2(cosine)
            total[...] += jnp.sum(value.reshape(16, 8, frames), axis=0)
            mass[pl.ds(pl.multiple_of(at_mass + nibble * 128, 128), 128), :] = to_low(value)
            return 0

        lax.fori_loop(0, own // 128, part, 0, unroll=2)

    @pl.when(step == 0)
    def _():
        unit_low[...] = to_low(unit_ref[...])
        total[...] = jnp.zeros_like(total)
        pull[...] = jnp.zeros_like(pull)

    @pl.when(step < owners)
    def _():
        at_mass = step * own if keep else 0
        fill(at_mass)
        pull[...] += dot(rows_ref[...], mass[pl.ds(pl.multiple_of(at_mass, own), own), :], TN)

    @pl.when(step == owners - 1)
    def _():
        score_scale = log2e / similarity_softening_factor
        unit, positive, masked = unit_ref[...], positive_ref[...], masked_ref[...]
        mass_sum = jnp.sum(total[...], axis=0, keepdims=True)
        score = jnp.sum(unit * positive, axis=0, keepdims=True) * (1.0 / similarity_softening_factor)
        whole = jnp.exp(score) + mass_sum
        loss_ref[...] = jnp.broadcast_to(masked * (jnp.log(whole) - score), loss_ref.shape)
        weight = masked / whole * (1.0 / similarity_softening_factor)
        d_score = -weight * mass_sum
        d_unit = d_score * positive + weight * (1.0 / score_scale) * pull[...]
        inner = jnp.sum(d_unit * unit, axis=0, keepdims=True)
        final_low_ref[...] = to_low((scale_ref[0:1, :] * (d_unit - unit * inner)).T)
        positive_part_ref[...] = (d_score * unit).T
        weighted[...] = to_low((weight * unit).T)

    @pl.when(step >= owners)
    def _():
        at_mass = (step - owners) * own if keep else 0
        if not keep:
            fill(at_mass)
        rows_grad_ref[...] = to_low(dot(mass[pl.ds(pl.multiple_of(at_mass, own), own), :], weighted[...]))


def candidates(index, rows, unit, scale, positive, masked):
    owners, slots, frames = index.shape
    width = rows.shape[1]
    own = rows.shape[0] // owners
    keep = rows.shape[0] * frames * 2 <= 16 << 20
    again = (lambda i: jnp.minimum(i, owners - 1)) if keep else (lambda i: lax.rem(i, owners))
    shape = jax.ShapeDtypeStruct
    return pl.pallas_call(
        functools.partial(candidate_kernel, slots, owners, keep),
        grid=(2 * owners,),
        in_specs=[
            pl.BlockSpec((1, slots, frames), lambda i: (again(i), 0, 0)),
            pl.BlockSpec((own, width), lambda i: (again(i), 0)),
            rows_of(unit),
            rows_of(scale),
            rows_of(positive),
            rows_of(masked),
        ],
        out_specs=[
            pl.BlockSpec((8, frames), lambda i: (0, 0)),
            pl.BlockSpec((frames, width), lambda i: (0, 0)),
            pl.BlockSpec((frames, width), lambda i: (0, 0)),
            pl.BlockSpec((own, width), lambda i: (jnp.maximum(i - owners, 0), 0)),
        ],
        out_shape=[
            shape((8, frames), jnp.float32),
            shape((frames, width), jnp.bfloat16),
            shape((frames, width), jnp.float32),
            shape((rows.shape[0], width), jnp.bfloat16),
        ],
        scratch_shapes=[
            pltpu.VMEM((128, frames), jnp.int32),
            pltpu.VMEM((rows.shape[0] if keep else own, frames), jnp.bfloat16),
            pltpu.VMEM((width, frames), jnp.float32),
            pltpu.VMEM((8, frames), jnp.float32),
            pltpu.VMEM((width, frames), jnp.bfloat16),
            pltpu.VMEM((frames, width), jnp.bfloat16),
        ],
        cost_estimate=small_cost,
        compiler_params=pltpu.CompilerParams(vmem_limit_bytes=62 << 20),
    )(index, rows, unit, scale, positive, masked)


def down_grad_kernel(active_ref, grad_ref, *refs):
    out_ref, turned = refs[-2:]

    @pl.when(pl.program_id(0) == 0)
    def _():
        turned[...] = grad_ref[...].T

    out_ref[...] = to_low(dot(turned[...], active_ref[...])).reshape(out_ref.shape)


def down_grad(active, grad, members, groups, after):
    count, inner = active.shape
    model = grad.shape[1]
    share = inner // members
    block = (1, groups, model // groups, share)
    return pl.pallas_call(
        down_grad_kernel,
        grid=(members,),
        in_specs=[
            pl.BlockSpec((count, share), lambda i: (0, i)),
            pl.BlockSpec((count, model), lambda i: (0, 0)),
        ]
        + [pl.BlockSpec(memory_space=pl.ANY)] * len(after),
        out_specs=pl.BlockSpec(block, lambda i: (i, 0, 0, 0)),
        out_shape=jax.ShapeDtypeStruct((members, groups, model // groups, share), jnp.bfloat16),
        scratch_shapes=[pltpu.VMEM((model, count), jnp.bfloat16)],
        cost_estimate=small_cost,
        compiler_params=pltpu.CompilerParams(vmem_limit_bytes=62 << 20),
    )(active, grad, *after)


def up_grad_kernel(
    groups, core_ref, hidden_ref, upper_ref, attended_ref, branch_ref, output_ref, final_ref, *refs
):
    kept_ref, sent_ref, turned, attended_turned, held = refs[-5:]
    group = pl.program_id(0)
    core = core_ref[0]
    lines, share = kept_ref.shape[1], kept_ref.shape[2]

    @pl.when(group == 0)
    def _():
        turned[...] = hidden_ref[...].T
        attended_turned[...] = attended_ref[...].T

    wide = upper_ref.shape[1]
    side = final_ref.shape[1]
    held[:, :, :, :wide] = to_low(dot(turned[...], upper_ref[...])).reshape(lines, 2, share, wide)

    @pl.when(group < groups - 1)
    def _():
        value = dot(attended_turned[...], branch_ref[...])
        held[:, :, :, wide:] = to_low(value).reshape(lines, 2, share, side)

    @pl.when(group == groups - 1)
    def _():
        value = dot(output_ref[...], final_ref[...], TN)
        held[:, :, :, wide:] = to_low(value).reshape(lines, 2, share, side)

    kept_ref[0] = held[:, core]
    sent_ref[0] = held[:, 1 - core]


def up_grad(core, hidden, upper, attended, branch, output, final, members, groups, after):
    count, model = hidden.shape
    wide, side = upper.shape[1] // groups, final.shape[1]
    lines, share = members // 2, model // members
    whole = lambda columns: pl.BlockSpec((count, columns), lambda g, core: (0, 0))
    out = pl.BlockSpec((1, lines, share, wide + side), lambda g, core: (g, 0, 0, 0))
    shape = jax.ShapeDtypeStruct((groups, lines, share, wide + side), jnp.bfloat16)
    last = model // side - 1
    return pl.pallas_call(
        functools.partial(up_grad_kernel, groups),
        grid_spec=pltpu.PrefetchScalarGridSpec(
            num_scalar_prefetch=1,
            grid=(groups,),
            in_specs=[
                whole(model),
                pl.BlockSpec((count, wide), lambda g, core: (0, g)),
                whole(model),
                pl.BlockSpec((count, side), lambda g, core: (0, jnp.minimum(g, last))),
                whole(model),
                whole(side),
            ]
            + [pl.BlockSpec(memory_space=pl.ANY)] * len(after),
            out_specs=[out, out],
            scratch_shapes=[
                pltpu.VMEM((model, count), jnp.bfloat16),
                pltpu.VMEM((model, count), jnp.bfloat16),
                pltpu.VMEM((lines, 2, share, wide + side), jnp.bfloat16),
            ],
        ),
        out_shape=[shape, shape],
        cost_estimate=small_cost,
        compiler_params=pltpu.CompilerParams(vmem_limit_bytes=62 << 20),
    )(core, hidden, upper, attended, branch, output, final, *after)


def projection_grad_kernel(grads, pieces, core_ref, frames_ref, *refs):
    kept_ref, sent_ref, held = refs[-3:]
    core = core_ref[0]
    turned = frames_ref[...].T
    each = kept_ref.shape[3] // PAIR
    lines, share = kept_ref.shape[1], kept_ref.shape[2]
    members = 2 * lines

    def put(number):
        for column in range(held.shape[3] // PAIR):
            tile = number * (held.shape[3] // PAIR) + column
            group, lanes = tile // each, pl.ds(tile % each * PAIR, PAIR)
            at = pl.ds(column * PAIR, PAIR)
            kept_ref[group, :, :, lanes] = held[:, core, :, at]
            sent_ref[group, :, :, lanes] = held[:, 1 - core, :, at]

    for number, ref in enumerate(refs[:grads]):
        held[...] = to_low(dot(turned, ref[...])).reshape(held.shape)
        put(number)
    if len(refs) == grads + 3:
        return
    piece_refs = refs[grads : grads + pieces]
    model_ref, up_ref, final_ref, target_ref, square_ref = refs[grads + pieces : -3]

    def total(values):
        return jnp.sum(values, axis=0, keepdims=True)

    vectors = (
        jnp.concatenate([total(ref[0]) for ref in piece_refs], axis=1),
        jnp.concatenate([total(ref[1]) for ref in piece_refs], axis=1),
        total(model_ref[5]),
        total(model_ref[3]),
        total(model_ref[4]),
        total(up_ref[...]),
        total(model_ref[2]),
        total(model_ref[0]),
        total(model_ref[1]),
        total(final_ref[...]),
        total(target_ref[...]),
    )
    square = square_ref[...]
    rows = square.shape[0] // members
    held[...] = jnp.zeros_like(held)
    for member in range(members):
        line, side = member // 2, member % 2
        parts = []
        for vector in vectors:
            size = vector.shape[1] // members
            for low in range(member * size, (member + 1) * size, PAIR):
                part = vector[:, low : min(low + PAIR, (member + 1) * size)]
                parts.append(jnp.pad(part, ((0, 0), (0, PAIR - part.shape[1]))))
        parts.append(jnp.zeros((share - len(parts), PAIR), jnp.float32))
        held[line, side, :, :PAIR] = to_low(jnp.concatenate(parts, axis=0))
        own = square[member * rows : (member + 1) * rows]
        for half in range(square.shape[1] // PAIR):
            part = own[:, half * PAIR : (half + 1) * PAIR]
            held[line, side, half * rows : (half + 1) * rows, PAIR:] = to_low(part)
    put(grads)


def projection_grad(core, frames, grads, pieces, sums, members, groups, after):
    count, model = frames.shape
    lines, share = members // 2, model // members
    width = grads[0].shape[1]
    wide = (len(grads) + bool(sums)) * width // groups
    shape = jax.ShapeDtypeStruct((groups, lines, share, wide), jnp.bfloat16)
    vmem = pl.BlockSpec(memory_space=pltpu.VMEM)

    def kernel(*refs):
        used = 2 + len(grads) + len(pieces) + len(sums)
        projection_grad_kernel(len(grads), len(pieces), *refs[:used], *refs[used + len(after) :])

    return pl.pallas_call(
        kernel,
        in_specs=[pl.BlockSpec(memory_space=pltpu.SMEM)]
        + [vmem] * (1 + len(grads) + len(pieces) + len(sums))
        + [pl.BlockSpec(memory_space=pl.ANY)] * len(after),
        out_specs=[vmem, vmem],
        out_shape=[shape, shape],
        scratch_shapes=[pltpu.VMEM((lines, 2, share, width), jnp.bfloat16)],
        cost_estimate=small_cost,
        compiler_params=pltpu.CompilerParams(vmem_limit_bytes=62 << 20),
    )(core, frames, *grads, *pieces, *sums, *after)


def slot_rows(distractors, members):
    count, slots = distractors.shape
    turns = -(-slots // members)
    padded = jnp.pad(distractors, ((0, 0), (0, turns * members - slots)), constant_values=-1)
    padded = padded.T.reshape(turns, members, count)
    period = members // math.gcd(slots, members)
    frame = jnp.arange(count, dtype=jnp.int32) % period
    placed = padded
    for phase in range(1, period):
        turned = jnp.roll(padded, phase * slots % members, axis=1)
        placed = jnp.where(frame == phase, turned, placed)
    return placed.transpose(1, 0, 2)


def target_kernel(came_ref, part_ref, unit_ref, scale_ref, low_ref, matrix_ref, *refs):
    grad_ref, matrix_grad_ref, sums_ref = refs[-3:]
    grad_unit = part_ref[...] + came_ref[...].astype(jnp.float32)
    unit = unit_ref[...]
    inner = jnp.sum(grad_unit * unit, axis=-1, keepdims=True)
    low = to_low(scale_ref[:, 0:1] * (grad_unit - unit * inner))
    grad_ref[...] = dot(low, to_low(matrix_ref[...]), NT)
    matrix_grad_ref[...] = dot(to_low(low_ref[...]), low, TN)
    sums_ref[...] = jnp.sum(low.astype(jnp.float32).reshape(-1, 8, low.shape[1]), axis=0)


def target_back(came, part, unit, scale, low, matrix, after):
    count, width = part.shape
    vmem = pl.BlockSpec(memory_space=pltpu.VMEM)
    shape = jax.ShapeDtypeStruct
    return pl.pallas_call(
        target_kernel,
        in_specs=[vmem] * 6 + [pl.BlockSpec(memory_space=pl.ANY)] * len(after),
        out_specs=[vmem] * 3,
        out_shape=[
            shape((count, width), jnp.float32),
            shape((width, width), jnp.float32),
            shape((8, width), jnp.float32),
        ],
        cost_estimate=small_cost,
        compiler_params=pltpu.CompilerParams(vmem_limit_bytes=62 << 20),
    )(came, part, unit, scale, low, matrix, *after)


def inputs_kernel(parts, resid_ref, *refs):
    out_ref = refs[-1]
    total = resid_ref[...]
    for matrix in range(3):
        low = 0
        for part in range(parts):
            grad_ref = refs[matrix * parts + part]
            high = low + grad_ref.shape[1]
            total = total + dot(grad_ref[...], refs[3 * parts + matrix][:, low:high], NT)
            low = high
    out_ref[...] = total


def inputs_back(resid, grads, matrices, block, after):
    count, model = resid.shape
    part = lambda x: pl.BlockSpec((block, x.shape[1]), lambda i: (i, 0))
    flat = [g for parts in grads for g in parts]
    return pl.pallas_call(
        functools.partial(inputs_kernel, len(grads[0])),
        grid=(count // block,),
        in_specs=[part(resid)]
        + [part(g) for g in flat]
        + [rows_of(m) for m in matrices]
        + [pl.BlockSpec(memory_space=pl.ANY)] * len(after),
        out_specs=part(resid),
        out_shape=jax.ShapeDtypeStruct(resid.shape, jnp.float32),
        cost_estimate=small_cost,
        compiler_params=pltpu.CompilerParams(vmem_limit_bytes=62 << 20),
    )(resid, *flat, *matrices, *after)


def target_prepare_kernel(targets_ref, matrix_ref, bias_ref, rows_ref, unit_ref, turned_ref, scale_ref):
    low = to_low(dot(to_low(targets_ref[...]), to_low(matrix_ref[...])) + bias_ref[...].reshape(1, -1))
    positive = low.astype(jnp.float32)
    scale = lax.rsqrt(jnp.sum(positive * positive, axis=-1, keepdims=True) + cosine_eps)
    unit = positive * scale
    rows_ref[...] = to_low(unit * (log2e / similarity_softening_factor))
    unit_ref[...] = unit
    turned_ref[...] = unit.T
    scale_ref[...] = jnp.broadcast_to(scale, scale_ref.shape)


def target_prepare(targets, matrix, bias):
    count, width = targets.shape
    vmem = pl.BlockSpec(memory_space=pltpu.VMEM)
    shape = jax.ShapeDtypeStruct
    return pl.pallas_call(
        target_prepare_kernel,
        in_specs=[vmem] * 3,
        out_specs=[vmem] * 4,
        out_shape=[
            shape((count, width), jnp.bfloat16),
            shape((count, width), jnp.float32),
            shape((width, count), jnp.float32),
            shape((count, PAIR), jnp.float32),
        ],
        cost_estimate=small_cost,
        compiler_params=pltpu.CompilerParams(vmem_limit_bytes=62 << 20),
    )(targets, matrix, bias)


def project_kernel(frames_ref, wq_ref, wk_ref, wv_ref, bq_ref, bv_ref, *refs):
    low_ref, q_ref, k_ref, v_ref, mq, mk, mv = refs[-7:]


    @pl.when(pl.program_id(0) == 0)
    def _():
        mq[...] = to_low(wq_ref[...])
        mk[...] = to_low(wk_ref[...])
        mv[...] = to_low(wv_ref[...])

    low = to_low(frames_ref[...])
    low_ref[...] = low
    q_ref[...] = to_low(dot(low, mq[...]) + bq_ref[...].reshape(1, -1))
    k_ref[...] = to_low(dot(low, mk[...]))
    v_ref[...] = to_low(dot(low, mv[...]) + bv_ref[...].reshape(1, -1))


def vector_spec(values):
    return pl.BlockSpec(values.shape, lambda i, *_: (0,))


def project(frames, w_query, w_key, w_value, b_query, b_value, block, after):
    count, model = frames.shape
    part = pl.BlockSpec((block, model), lambda i: (i, 0))
    return pl.pallas_call(
        project_kernel,
        grid=(count // block,),
        in_specs=[part]
        + [rows_of(w) for w in (w_query, w_key, w_value)]
        + [vector_spec(b) for b in (b_query, b_value)]
        + [pl.BlockSpec(memory_space=pl.ANY)] * len(after),
        out_specs=[part] * 4 + [rows_of(w_query)] * 3,
        out_shape=[jax.ShapeDtypeStruct((count, model), jnp.bfloat16)] * 4
        + [jax.ShapeDtypeStruct((model, model), jnp.bfloat16)] * 3,
        cost_estimate=small_cost,
        compiler_params=pltpu.CompilerParams(vmem_limit_bytes=62 << 20),
    )(frames, w_query, w_key, w_value, b_query, b_value, *after)


def exchange(sent):
    members = lax.axis_size("tm")
    return lax.ppermute(sent, "tm", [(i, i ^ 1) for i in range(members)])


def split_kernel(counts, pieces, choice_ref, *refs):
    out_refs = refs[-pieces:]
    number, low, lanes = 0, 0, 0
    for count in counts:
        total = refs[number][0].astype(jnp.float32)
        for term in range(1, count):
            total = total + refs[number + term][0].astype(jnp.float32)
        total = to_low(total)
        high = lanes + total.shape[-1]
        for piece in range(pieces):

            @pl.when(pl.program_id(0) == piece)
            def _(piece=piece, total=total, low=low, lanes=lanes, high=high):
                if total.ndim == 3:
                    out_refs[piece][low : low + total.shape[0]] = total
                else:
                    out_refs[piece][:, lanes:high] = total

        number, low, lanes = number + count, low + total.shape[0], high


def split_sum(choice, sums, pieces, after):
    terms = [term for group in sums for term in group]
    first = [group[0].shape[1:] for group in sums]
    if len(first[0]) == 3:
        rest = (sum(shape[0] for shape in first), *first[0][1:])
    else:
        rest = (first[0][0], sum(shape[1] for shape in first))

    def source(term):
        zeros = (0,) * (term.ndim - 1)
        return pl.BlockSpec((1, *term.shape[1:]), lambda i, choice: (choice[0] ^ i, *zeros))

    return pl.pallas_call(
        functools.partial(split_kernel, [len(group) for group in sums], pieces),
        grid_spec=pltpu.PrefetchScalarGridSpec(
            num_scalar_prefetch=1,
            grid=(pieces,),
            in_specs=[source(term) for term in terms]
            + [pl.BlockSpec(memory_space=pl.ANY)] * len(after),
            out_specs=[pl.BlockSpec(rest, lambda i, choice: (0,) * len(rest))] * pieces,
        ),
        out_shape=[jax.ShapeDtypeStruct(rest, jnp.bfloat16)] * pieces,
        cost_estimate=small_cost,
        compiler_params=pltpu.CompilerParams(vmem_limit_bytes=62 << 20),
    )(choice, *terms, *after)


def swap(pieces, axis="grp", stride=1):
    size = lax.axis_size(axis)
    return [pieces[0]] + [
        lax.ppermute(piece, axis, [(i, i ^ (k * stride)) for i in range(size)])
        for k, piece in enumerate(pieces)
        if k
    ]


def line_kernel(terms, *refs):
    total = refs[0][...].astype(jnp.float32)
    for term in range(1, terms):
        total = total + refs[term][...].astype(jnp.float32)
    refs[-1][...] = to_low(total)


def line_sum(terms, after):
    lines, rest = terms[0].shape[0], terms[0].shape[1:]
    block = pl.BlockSpec((1, *rest), lambda i: (i, *(0,) * len(rest)))
    return pl.pallas_call(
        functools.partial(line_kernel, len(terms)),
        grid=(lines,),
        in_specs=[block] * len(terms) + [pl.BlockSpec(memory_space=pl.ANY)] * len(after),
        out_specs=block,
        out_shape=jax.ShapeDtypeStruct(terms[0].shape, jnp.bfloat16),
        cost_estimate=large_cost,
        compiler_params=pltpu.CompilerParams(vmem_limit_bytes=62 << 20),
    )(*terms, *after)


def core_pairs():
    return [[2 * i, 2 * i + 1] for i in range(lax.axis_size("tm") // 2)]


def chip_lines():
    return [list(range(first, lax.axis_size("tm"), 2)) for first in range(2)]


def scatter(value, axis, among=None):
    return lax.psum_scatter(value, axis, scatter_dimension=0, axis_index_groups=among)


def over_lines(value):
    return lax.all_to_all(value, "tm", 0, 0, tiled=True, axis_index_groups=chip_lines())


def share_kernel(start, done_ref, line_ref, out_ref):
    wide = done_ref.shape[2]
    for copy in range(out_ref.shape[0]):
        low = 0
        for at in range(start, done_ref.shape[0]):
            out_ref[copy, :, low : low + wide] = done_ref[at]
            low += wide
        out_ref[copy, :, low:] = line_ref[...]


def shares(done, lines, start, groups, after):
    rows = done.shape[1]
    wide = (done.shape[0] - start) * done.shape[2] + lines.shape[1]
    vmem = pl.BlockSpec(memory_space=pltpu.VMEM)
    return pl.pallas_call(
        lambda *refs: share_kernel(start, refs[0], refs[1], refs[-1]),
        in_specs=[vmem] * 2 + [pl.BlockSpec(memory_space=pl.ANY)] * len(after),
        out_specs=vmem,
        out_shape=jax.ShapeDtypeStruct((groups, rows, wide), jnp.bfloat16),
        cost_estimate=large_cost,
        compiler_params=pltpu.CompilerParams(vmem_limit_bytes=62 << 20),
    )(done, lines, *after)


def place(kernel, arrays, shapes, after, choice=None):
    vmem = pl.BlockSpec(memory_space=pltpu.VMEM)
    first = [] if choice is None else [choice]
    used = len(first) + len(arrays)
    return pl.pallas_call(
        lambda *refs: kernel(*refs[:used], *refs[used + len(after) :]),
        in_specs=[pl.BlockSpec(memory_space=pltpu.SMEM)] * len(first)
        + [vmem] * len(arrays)
        + [pl.BlockSpec(memory_space=pl.ANY)] * len(after),
        out_specs=[vmem] * len(shapes),
        out_shape=[jax.ShapeDtypeStruct(s, jnp.float32) for s in shapes],
        cost_estimate=small_cost,
        compiler_params=pltpu.CompilerParams(vmem_limit_bytes=62 << 20),
    )(*first, *arrays, *after)


def line_total(terms, after):
    vmem = pl.BlockSpec(memory_space=pltpu.VMEM)
    return pl.pallas_call(
        functools.partial(line_kernel, len(terms)),
        in_specs=[vmem] * len(terms) + [pl.BlockSpec(memory_space=pl.ANY)] * len(after),
        out_specs=vmem,
        out_shape=jax.ShapeDtypeStruct(terms[0].shape, jnp.bfloat16),
        cost_estimate=small_cost,
        compiler_params=pltpu.CompilerParams(vmem_limit_bytes=62 << 20),
    )(*terms, *after)


def on_device(
    frames,
    targets,
    lengths,
    span_starts,
    distractors,
    w_query,
    b_query,
    w_key,
    w_value,
    b_value,
    w_out,
    b_out,
    norm_gain,
    norm_bias,
    w_up,
    b_up,
    w_down,
    b_down,
    final_gain,
    final_bias,
    w_final,
    b_final,
    w_target,
    b_target,
):
    count, model = frames.shape
    width = targets.shape[1]
    inner = w_up.shape[1]
    members, groups = lax.axis_size("tm"), lax.axis_size("grp")
    block = min(count, 256)
    share = model // members
    place_in_line = lax.axis_index("tm")
    core = (place_in_line % 2)[None].astype(jnp.int32)
    line = (place_in_line // 2)[None].astype(jnp.int32)
    group = lax.axis_index("grp")[None].astype(jnp.int32)

    own_rows, positive_unit, positive_turned, positive_scale = target_prepare(targets, w_target, b_target)
    rows = lax.all_gather(own_rows, "tm", tiled=True)
    index = slot_rows(distractors, members)

    segment = segment_ids(lengths[0], count)
    masked = span_mask(span_starts, segment, count)
    span, hot_query, hot_key = attention_plan(lengths[0], segment, count, 2 * block, block)
    span_back, _, _ = attention_plan(lengths[0], segment, count, block, block // 2)
    frames_low, query, key, value, *own_matrices = project(
        frames, w_query, w_key, w_value, b_query, b_value, block, (own_rows,)
    )
    attended_low, log_total, out_matrix, up_matrix, down_matrix, final_matrix = attend(
        span, query, key, value, hot_query, hot_key, (w_out, w_up, w_down, w_final), 2 * block, block, 2
    )
    (
        hidden_low,
        normed_one,
        active_low,
        slope,
        normed_two,
        output_low,
        scales,
        final_unit,
        final_scale,
    ) = feed_forward(
        attended_low,
        frames,
        out_matrix,
        up_matrix,
        down_matrix,
        final_matrix,
        (b_out, norm_gain, norm_bias, b_down, final_gain, final_bias, b_up, b_final),
        block,
    )
    losses, d_final_low, positive_part, d_rows = candidates(
        index, rows, final_unit, final_scale, positive_turned, masked[None]
    )
    came = lax.psum_scatter(d_rows, "tm", scatter_dimension=0, tiled=True)

    (
        d_down_low,
        d_upper_low,
        d_resid,
        d_branch_low,
        d_attended_low,
        model_sums,
        up_sums,
        final_sums,
    ) = feed_forward_back(
        d_final_low,
        slope,
        normed_one,
        normed_two,
        scales,
        final_matrix,
        up_matrix,
        down_matrix,
        out_matrix,
        (norm_gain, final_gain),
        block,
    )
    def attention_back(piece, pieces, after):
        return attend_back(
            span_back,
            query,
            key,
            value,
            d_attended_low,
            attended_low,
            hot_query,
            hot_key,
            log_total,
            lengths.shape[1],
            block,
            block // 2,
            2,
            piece,
            pieces,
            after,
        )


    def total(values):
        return jnp.sum(values, axis=0)

    def vector_sums(piece_sums, target_sums):
        return (
            jnp.concatenate([total(s[0]) for s in piece_sums]),
            jnp.concatenate([total(s[1]) for s in piece_sums]),
            total(model_sums[5]),
            total(model_sums[3]),
            total(model_sums[4]),
            total(up_sums),
            total(model_sums[2]),
            total(model_sums[0]),
            total(model_sums[1]),
            total(final_sums),
            total(target_sums),
        )

    if share % 16 or (inner // members) % PAIR or model != (groups - 1) * width:
        back = [attention_back(piece, 3, ()) for piece in range(3)]
        d_query, d_key, d_value, piece_sums = ([part[k] for part in back] for k in range(4))
        target_grad, grad_w_target, target_sums = target_back(
            came, positive_part, positive_unit, positive_scale, targets, w_target, ()
        )
        input_grad = inputs_back(
            d_resid, (d_query, d_key, d_value), own_matrices, block, ()
        )

        def reduced(grad):
            part = lax.psum_scatter(grad, "tm", scatter_dimension=0, tiled=True)
            return lax.psum(to_low(part), "grp").astype(jnp.float32)

        def projected(parts):
            return reduced(product_left(frames_low, jnp.concatenate(parts, axis=1)))

        small = [reduced(vector) for vector in vector_sums(piece_sums, target_sums)]
        return (
            losses[0],
            input_grad,
            target_grad,
            projected(d_query),
            small[0],
            projected(d_key),
            projected(d_value),
            small[1],
            reduced(product_left(attended_low, d_branch_low)),
            small[2],
            small[3],
            small[4],
            reduced(product_left(hidden_low, d_upper_low)),
            small[5],
            reduced(product_left(active_low, d_down_low)),
            small[6],
            small[7],
            small[8],
            reduced(product_left(output_low, d_final_low)),
            small[9],
            reduced(grad_w_target),
            small[10],
        )

    down_parts = down_grad(active_low, d_down_low, members, groups, ())
    down_part = scatter(down_parts, "tm")
    up_kept, up_sent = up_grad(
        core,
        hidden_low,
        d_upper_low,
        attended_low,
        d_branch_low,
        output_low,
        d_final_low,
        members,
        groups,
        (down_parts,),
    )
    up_came = exchange(up_sent)
    target_grad, grad_w_target, target_sums = target_back(
        came, positive_part, positive_unit, positive_scale, targets, w_target, (up_sent,)
    )
    up_group = split_sum(group, [[up_kept, up_came]], groups, (grad_w_target,))
    up_groups = swap(up_group)

    def projections(pieces, sums, after):
        grads = [back[piece][k] for k in range(3) for piece in pieces]
        sums_of = [part[3] for part in back] if sums else []
        return projection_grad(core, frames_low, grads, sums_of, sums, members, groups, after)

    back = [attention_back(0, 3, (up_group[1],))]
    back.append(attention_back(1, 3, (back[0][0],)))
    early_kept, early_sent = projections((0, 1), (), ())
    early_came = exchange(early_sent)
    up_line = line_sum(up_groups, (early_sent,))
    up_share = scatter(up_line, "tm", chip_lines())
    early_group = split_sum(
        group,
        [[early_kept, early_came], [down_part.reshape(groups, -1, share, inner // members)]],
        groups,
        (up_line,),
    )
    early_groups = swap(early_group)
    back.append(attention_back(2, 3, (early_group[1],)))
    d_query, d_key, d_value, piece_sums = ([part[k] for part in back] for k in range(4))
    late_kept, late_sent = projections(
        (2,), (model_sums, up_sums, final_sums, target_sums, grad_w_target), ()
    )
    late_came = exchange(late_sent)
    early_line = line_sum(early_groups, (late_sent,))
    late_group = split_sum(group, [[late_kept, late_came]], groups, (early_line,))
    late_groups = swap(late_group)
    input_grad = inputs_back(
        d_resid, (d_query, d_key, d_value), own_matrices, block, (late_group[1],)
    )
    own_line = split_sum(line, [[early_line], late_groups], members // 2, (input_grad,))
    own_lines = swap(own_line, "tm", 2)
    most_shares = shares(early_line, up_share, members // 2, groups, (own_line[1],))
    most = lax.all_to_all(most_shares, "grp", 0, 0, tiled=True)

    def by_group(choice_ref, refs, put):
        for piece in range(groups):
            for number in range(groups):

                @pl.when(choice_ref[0] ^ piece == number)
                def _(piece=piece, number=number):
                    put(number, refs[piece], refs[groups:])

    last = swap([line_total(own_lines, (most_shares,))] * groups)
    up_at = inner // members * (model // groups // share)
    side_at = up_at + inner // groups

    def put_most(most_ref, down_ref, up_ref, out_ref, final_ref):
        rows = model // groups
        for at in range(groups):
            part = lambda low, high: most_ref[at, :, low:high].astype(jnp.float32)
            for top in range(rows // share):
                low = at * rows + top * share
                wide = inner // members
                down_ref[:, low : low + share] = part(top * wide, (top + 1) * wide).T
            wide = inner // groups
            up_ref[:, at * wide : (at + 1) * wide] = part(up_at, side_at)
            if at < groups - 1:
                out_ref[:, at * width : (at + 1) * width] = part(side_at, side_at + width)
            else:
                final_ref[...] = part(side_at, side_at + width)

    grad_down, grad_up, grad_out, grad_final = place(
        put_most,
        [most],
        [(inner // members, model), (share, inner), (share, model), (share, width)],
        (last[0],),
    )
    third = model // 3
    early = [(k, piece * third + at) for k in range(3) for piece in (0, 1) for at in range(0, third, PAIR)]
    late = [(k, 2 * third + at) for k in range(3) for at in range(0, third, PAIR)]
    late += [(3, at) for at in range(0, 2 * PAIR, PAIR)]

    def put_last(number, ref, outs):
        low = 0
        for tiles in (early, late):
            each = len(tiles) // groups
            for k, lanes in tiles[number * each : (number + 1) * each]:
                value = ref[:, low : low + PAIR].astype(jnp.float32)
                low += PAIR
                if k < 3:
                    outs[k][:, lanes : lanes + PAIR] = value
                elif lanes:
                    rows = width // members
                    for half in range(width // PAIR):
                        part = value[half * rows : (half + 1) * rows]
                        outs[3][:, half * PAIR : (half + 1) * PAIR] = part
                else:
                    row = 0
                    for out in outs[4:]:
                        for start in range(0, out.shape[0], PAIR):
                            size = min(PAIR, out.shape[0] - start)
                            out[start : start + size] = value[row, :size]
                            row += 1

    sizes = [model] * 5 + [inner] + [model] * 3 + [width] * 2
    grad_query, grad_key, grad_value, grad_target, *small = place(
        lambda choice_ref, *refs: by_group(choice_ref, refs, put_last),
        last,
        [(share, model)] * 3
        + [(width // members, width)]
        + [(size // members,) for size in sizes],
        (grad_up,),
        group,
    )
    return (
        losses[0],
        input_grad,
        target_grad,
        grad_query,
        small[0],
        grad_key,
        grad_value,
        small[1],
        grad_out,
        small[2],
        small[3],
        small[4],
        grad_up,
        small[5],
        grad_down,
        small[6],
        small[7],
        small[8],
        grad_final,
        small[9],
        grad_target,
        small[10],
    )


def solution(mesh):
    placed = (
        P(("grp", "tm"), None),
        P(("grp", "tm"), None),
        P(("grp", "tm"), None),
        P(("grp", "tm")),
        P(("grp", "tm"), None),
        P(),
        P(),
        P(),
        P(),
        P(),
        P(),
        P(),
        P(),
        P(),
        P(),
        P(),
        P(),
        P(),
        P(),
        P(),
        P(),
        P(),
        P(),
        P(),
    )
    return jax.shard_map(
        on_device,
        mesh=mesh,
        in_specs=placed,
        out_specs=(
            P(("grp", "tm")),
            P(("grp", "tm"), None),
            P(("grp", "tm"), None),
            P("tm", None),
            P("tm"),
            P("tm", None),
            P("tm", None),
            P("tm"),
            P("tm", None),
            P("tm"),
            P("tm"),
            P("tm"),
            P("tm", None),
            P("tm"),
            P("tm", None),
            P("tm"),
            P("tm"),
            P("tm"),
            P("tm", None),
            P("tm"),
            P("tm", None),
            P("tm"),
        ),
        check_vma=False,
    )
```

```python
import functools
import math

import jax
import jax.numpy as jnp
from jax import lax
from jax.experimental import pallas as pl
from jax.experimental.pallas import tpu as pltpu
from jax.sharding import PartitionSpec as P

H = 12
HD = 64
NEG = 100
SPAN = 10


norm_eps = 1e-05
cosine_eps = 1e-06
similarity_softening_factor = 0.1
log2e = 1.4426950408889634
PAIR = 2 * HD
COLUMNS = 256
NT = (((1,), (1,)), ((), ()))
TN = (((0,), (0,)), ((), ()))
large_cost = pl.CostEstimate(flops=230_000_000_000, bytes_accessed=1, transcendentals=0)
small_cost = pl.CostEstimate(flops=1, bytes_accessed=1, transcendentals=0)


def to_low(values):
    return values.astype(jnp.bfloat16)


def product(left, right):
    return jnp.dot(left, right, preferred_element_type=jnp.float32)


def product_left(left, right):
    return lax.dot_general(
        left, right, (((0,), (0,)), ((), ())), preferred_element_type=jnp.float32
    )


def product_right(left, right):
    return lax.dot_general(
        left, right, (((1,), (1,)), ((), ())), preferred_element_type=jnp.float32
    )


def column_sum(values):
    return jnp.sum(values.astype(jnp.float32), axis=0)


def exact_gelu(values):
    return jax.nn.gelu(values, approximate=False)


def layer_norm(values, gain, bias):
    center = values - jnp.mean(values, axis=-1, keepdims=True)
    scale = lax.rsqrt(jnp.mean(center * center, axis=-1, keepdims=True) + norm_eps)
    normed = center * scale
    return (normed * gain + bias, normed, scale)


def layer_norm_back(grad, normed, scale, gain):
    grad_normed = grad * gain
    inner = (
        grad_normed
        - jnp.mean(grad_normed, axis=-1, keepdims=True)
        - normed * jnp.mean(grad_normed * normed, axis=-1, keepdims=True)
    )
    return (inner * scale, jnp.sum(grad * normed, axis=0), jnp.sum(grad, axis=0))


def utterances(lengths_row, count):
    position = jnp.arange(count, dtype=jnp.int32)
    segment = jnp.zeros((count,), jnp.int32)
    begin = jnp.zeros((count,), jnp.int32)
    bound = jnp.zeros((), jnp.int32)
    for kind in range(lengths_row.shape[0]):
        bound = bound + lengths_row[kind]
        later = position >= bound
        segment = segment + later.astype(jnp.int32)
        begin = jnp.where(later, bound, begin)
    return segment, position - begin


def span_mask(starts, age, count):
    covered = starts
    for offset in range(1, SPAN):
        earlier = jnp.pad(starts[: count - offset], (offset, 0))
        covered = jnp.maximum(covered, jnp.where(age >= offset, earlier, 0))
    return covered.astype(jnp.float32)


def dot(a, b, dims=(((1,), (0,)), ((), ()))):
    return lax.dot_general(a, b, dims, preferred_element_type=jnp.float32)

def first_half(rows):
    return lax.broadcasted_iota(jnp.int32, (rows, PAIR), 1) < HD


def windows(span_ref, block, chunk, count, body):
    i = pl.program_id(0)
    start, chunks = span_ref[0, i], span_ref[1, i]
    total = count // chunk
    sizes = list(range(2, total + 1))
    for size in sizes:
        hit = (chunks <= size) if size == sizes[0] else (chunks == size)

        @pl.when(hit)
        def _(size=size):
            at = pl.multiple_of(jnp.minimum(start, total - size) * chunk, chunk)
            body(at, size * chunk)


def either(first, one, other, half):
    return jnp.where(first, one, other) if half == 0 else jnp.where(first, other, one)


def forward_kernel(casts, pairs, chunk, unroll, span_ref, q_ref, k_ref, v_ref, hotq_ref, hotk_ref, *refs):
    sources, out_ref, log_ref = refs[:casts], refs[casts], refs[casts + 1]
    results = refs[casts + 2 : 2 * casts + 2]
    wides, lows = refs[2 * casts + 2 : 3 * casts + 2], refs[3 * casts + 2 : 4 * casts + 2]
    in_sems, out_sems = refs[-2:]
    step = pl.program_id(0)

    def copies(pairs_of, sems):
        return [
            pltpu.make_async_copy(source, target, sems.at[number])
            for number, (source, target) in enumerate(pairs_of)
        ]

    @pl.when(step == 0)
    def _():
        for copy in copies(zip(sources, wides), in_sems):
            copy.start()

    block = q_ref.shape[0]
    count = k_ref.shape[0]
    scale = HD**-0.5 * log2e

    def body(at, size):
        near = pl.ds(at, size)
        lane = lax.broadcasted_iota(jnp.int32, (block, PAIR), 1)
        first_q, first_k = first_half(block), first_half(size)
        ones = jnp.ones((size, PAIR), jnp.bfloat16)

        def pair(p, logs):
            cols = pl.ds(pl.multiple_of(p * PAIR, PAIR), PAIR)
            q, k, v = q_ref[:, cols], k_ref[near, cols], v_ref[near, cols]
            hotq, hotk = hotq_ref[...], hotk_ref[near, :]
            outs = []
            for half in range(2):
                scores = dot(either(first_q, q, hotq, half), either(first_k, k, hotk, half), NT)
                top = jnp.max(scores, axis=1, keepdims=True) * scale
                raised = to_low(jnp.exp2(scores * scale - top))
                result = dot(raised, either(first_k, v, ones, half))
                spare = HD * (1 - half)
                total = result[:, spare : spare + 1]
                outs.append(result * (1.0 / total))
                logs = jnp.where(lane == 2 * p + half, top + jnp.log2(total), logs)
            out_ref[:, cols] = to_low(jnp.where(first_q, outs[0], outs[1]))
            return logs

        empty = jnp.zeros((block, PAIR), jnp.float32)
        log_ref[...] = lax.fori_loop(0, pairs, pair, empty, unroll=unroll)

    windows(span_ref, block, chunk, count, body)

    @pl.when(step == 0)
    def _():
        for copy, wide, low in zip(copies(zip(sources, wides), in_sems), wides, lows):
            copy.wait()
            low[...] = to_low(wide[...])
        for copy in copies(zip(lows, results), out_sems):
            copy.start()

    @pl.when(step == pl.num_programs(0) - 1)
    def _():
        for copy in copies(zip(lows, results), out_sems):
            copy.wait()


def attend(span, query, key, value, hotq, hotk, casts, block, chunk, unroll):
    count, width = query.shape
    whole = lambda w: pl.BlockSpec((count, w), lambda i, *_: (0, 0))
    part = lambda w: pl.BlockSpec((block, w), lambda i, *_: (i, 0))
    anywhere = [pl.BlockSpec(memory_space=pl.ANY)] * len(casts)
    shape = jax.ShapeDtypeStruct
    return pl.pallas_call(
        functools.partial(forward_kernel, len(casts), width // PAIR, chunk, unroll),
        grid_spec=pltpu.PrefetchScalarGridSpec(
            num_scalar_prefetch=1,
            grid=(count // block,),
            in_specs=[part(width), whole(width), whole(width), part(PAIR), whole(PAIR)] + anywhere,
            out_specs=[part(width), part(PAIR)] + anywhere,
            scratch_shapes=[pltpu.VMEM(x.shape, jnp.float32) for x in casts]
            + [pltpu.VMEM(x.shape, jnp.bfloat16) for x in casts]
            + [pltpu.SemaphoreType.DMA((len(casts),))] * 2,
        ),
        out_shape=[shape((count, width), jnp.bfloat16), shape((count, PAIR), jnp.float32)]
        + [shape(x.shape, jnp.bfloat16) for x in casts],
        cost_estimate=small_cost,
        compiler_params=pltpu.CompilerParams(vmem_limit_bytes=62 << 20),
    )(span, query, key, value, hotq, hotk, *casts)


def thirds(values):
    high = to_low(values)
    rest = values - high.astype(jnp.float32)
    middle = to_low(rest)
    return high, middle, to_low(rest - middle.astype(jnp.float32))


def backward_kernel(
    kinds,
    pairs,
    chunk,
    unroll,
    piece,
    span_ref,
    q_ref,
    k_ref,
    v_ref,
    g_ref,
    o_ref,
    hotq_ref,
    hotk_ref,
    log_ref,
    *refs,
):
    dq_ref, dk_ref, dv_ref, sums_ref, dk_sum, dv_sum = refs[-6:]
    block = q_ref.shape[0]
    count = k_ref.shape[0]
    scale = HD**-0.5 * log2e

    @pl.when(pl.program_id(0) == 0)
    def _():
        dk_sum[...] = jnp.zeros_like(dk_sum)
        dv_sum[...] = jnp.zeros_like(dv_sum)
        sums_ref[...] = jnp.zeros_like(sums_ref)

    def body(at, size):
        near = pl.ds(at, size)
        lane = lax.broadcasted_iota(jnp.int32, (block, PAIR), 1)
        first_q, first_k = first_half(block), first_half(size)
        spare = lax.rem(lane, HD) - kinds

        def affine(values, rest):
            for number, part in enumerate(thirds(values)):
                rest = jnp.where(spare == number, part, rest)
            return rest

        def pair(p, _):
            cols = pl.ds(pl.multiple_of(p * PAIR, PAIR), PAIR)
            q, k, v, g = q_ref[:, cols], k_ref[near, cols], v_ref[near, cols], g_ref[:, cols]
            hotq, hotk, logs = hotq_ref[...], hotk_ref[near, :], log_ref[...]
            products = g.astype(jnp.float32) * o_ref[:, cols].astype(jnp.float32)
            zero = jnp.zeros_like(g)
            dqs, dks, dvs = [], [], []
            for half in range(2):
                mine = lane == 2 * (p + piece * pairs) + half
                log = jnp.sum(jnp.where(mine, logs, 0.0), axis=1, keepdims=True)
                inner = jnp.sum(either(first_q, products, 0.0, half), axis=1, keepdims=True)
                qh = either(first_q, q, affine(log * (-1.0 / scale), hotq), half)
                gh = either(first_q, g, affine(-inner, zero), half)
                kh = either(first_k, k, hotk, half)
                vh = either(first_k, v, hotk, half)
                prob = jnp.exp2(dot(qh, kh, NT) * scale)
                d_scores = to_low(prob * dot(gh, vh, NT))
                dqs.append(dot(d_scores, k))
                dks.append(dot(d_scores, q, TN))
                dvs.append(dot(to_low(prob), g, TN))
            dq_ref[:, cols] = to_low(jnp.where(first_q, dqs[0], dqs[1]) * HD**-0.5)
            dk_sum[near, cols] += jnp.where(first_k, dks[0], dks[1])
            dv_sum[near, cols] += jnp.where(first_k, dvs[0], dvs[1])
            return 0

        lax.fori_loop(0, pairs, pair, 0, unroll=unroll)

    windows(span_ref, block, chunk, count, body)
    rounded = dq_ref[...].astype(jnp.float32)
    sums_ref[0] += jnp.sum(rounded.reshape(-1, 8, rounded.shape[1]), axis=0)

    @pl.when(pl.program_id(0) == pl.num_programs(0) - 1)
    def _():
        sums_ref[1] = jnp.sum(dv_sum[...].reshape(-1, 8, dv_sum.shape[1]), axis=0)
        dk_ref[...] = to_low(dk_sum[...] * HD**-0.5)
        dv_ref[...] = to_low(dv_sum[...])


def attend_back(
    span, query, key, value, grad, result, hotq, hotk, logs, kinds, block, chunk, unroll, piece, pieces, after
):
    count = query.shape[0]
    width = query.shape[1] // pieces
    whole = lambda w, j=0: pl.BlockSpec((count, w), lambda i, *_: (0, j))
    part = lambda w, j=0: pl.BlockSpec((block, w), lambda i, *_: (i, j))
    shape = jax.ShapeDtypeStruct
    return pl.pallas_call(
        functools.partial(backward_kernel, kinds, width // PAIR, chunk, unroll, piece),
        grid_spec=pltpu.PrefetchScalarGridSpec(
            num_scalar_prefetch=1,
            grid=(count // block,),
            in_specs=[
                part(width, piece),
                whole(width, piece),
                whole(width, piece),
                part(width, piece),
                part(width, piece),
                part(PAIR),
                whole(PAIR),
                part(PAIR),
            ]
            + [pl.BlockSpec(memory_space=pl.ANY)] * len(after),
            out_specs=[
                part(width),
                whole(width),
                whole(width),
                pl.BlockSpec((2, 8, width), lambda i, *_: (0, 0, 0)),
            ],
            scratch_shapes=[pltpu.VMEM((count, width), jnp.float32)] * 2,
        ),
        out_shape=[shape((count, width), jnp.bfloat16)] * 3 + [shape((2, 8, width), jnp.float32)],
        cost_estimate=small_cost,
        compiler_params=pltpu.CompilerParams(vmem_limit_bytes=62 << 20),
    )(span, query, key, value, grad, result, hotq, hotk, logs, *after)


def attention_plan(lengths_row, segment, count, block, chunk):
    kinds = lengths_row.shape[0]
    row = jnp.arange(count // block, dtype=jnp.int32) * block
    low = jnp.zeros_like(row)
    high = jnp.full_like(row, count)
    bound = jnp.zeros((), jnp.int32)
    for kind in range(kinds):
        low = jnp.where(row >= bound, bound, low)
        bound = bound + lengths_row[kind]
    for kind in reversed(range(kinds)):
        high = jnp.where(row + block <= bound, bound, high)
        bound = bound - lengths_row[kind]
    low = low // chunk
    high = (high + chunk - 1) // chunk
    span = jnp.stack([low, high - low]).astype(jnp.int32)
    lane = jnp.arange(PAIR, dtype=jnp.int32)[None, :] % HD
    same = lane == segment[:, None]
    hot_query = to_low(jnp.where((lane < kinds) & ~same, 1e30, 0.0))
    hot_key = to_low(jnp.where((lane >= kinds) & (lane < kinds + 3), 1.0, jnp.where(same, -1.0, 0.0)))
    return span, hot_query, hot_key


def rows_of(values):
    return pl.BlockSpec((values.shape[0], values.shape[1]), lambda i, *_: (0, 0))


def gelu_and_slope(values):
    size = jnp.abs(values) * 0.7071067811865476
    near = 1.0 / (1.0 + 0.3275911 * size)
    bell = jnp.exp2(values * values * (-0.5 * log2e))
    poly = near * (
        0.254829592
        + near * (-0.284496736 + near * (1.421413741 + near * (-1.453152027 + near * 1.061405429)))
    )
    tail = 0.5 * poly * bell
    share = jnp.where(values >= 0, 1.0 - tail, tail)
    return values * share, share + values * bell * 0.3989422804014327


def normalize(values):
    center = values - jnp.mean(values, axis=-1, keepdims=True)
    scale = lax.rsqrt(jnp.mean(center * center, axis=-1, keepdims=True) + norm_eps)
    return center * scale, scale


def normalize_back(grad, normed, scale, gain):
    moved = grad * gain
    inner = (
        moved
        - jnp.mean(moved, axis=-1, keepdims=True)
        - normed * jnp.mean(moved * normed, axis=-1, keepdims=True)
    )
    return inner * scale


def feed_forward_kernel(
    parts,
    attended_ref,
    frames_ref,
    out_ref,
    up_ref,
    down_ref,
    final_ref,
    *refs,
):
    vectors, up_bias_ref, final_bias_ref = refs[:6], refs[6], refs[7]
    (
        hidden_turned_ref,
        normed_one_ref,
        active_ref,
        slope_ref,
        normed_two_ref,
        output_turned_ref,
        scales_ref,
        unit_ref,
        unit_scale_ref,
    ) = refs[8:]
    vector = lambda row: vectors[row][...].reshape(1, -1)
    resid = frames_ref[...] + dot(attended_ref[...], out_ref[...]) + vector(0)
    normed, scale_one = normalize(resid)
    normed_one_ref[...] = to_low(normed)
    hidden = normed * vector(1) + vector(2)
    hidden_low = to_low(hidden)
    hidden_turned_ref[...] = hidden_low.T
    second = hidden + vector(3)
    chunk = up_ref.shape[1] // parts
    for part in range(parts):
        at = pl.ds(part * chunk, chunk)
        upper = dot(hidden_low, up_ref[:, at]) + up_bias_ref[at].reshape(1, -1)
        active, slope = gelu_and_slope(upper)
        active = to_low(active)
        active_ref[:, at] = active
        slope_ref[:, at] = to_low(slope)
        second = second + dot(active, down_ref[at, :])
    normed, scale_two = normalize(second)
    normed_two_ref[...] = to_low(normed)
    output_low = to_low(normed * vector(4) + vector(5))
    output_turned_ref[...] = output_low.T
    final = dot(output_low, final_ref[...]) + final_bias_ref[...].reshape(1, -1)
    turned = final.T
    unit_scale = lax.rsqrt(jnp.sum(turned * turned, axis=0, keepdims=True) + cosine_eps)
    unit_ref[...] = turned * unit_scale
    unit_scale_ref[...] = jnp.broadcast_to(unit_scale, unit_scale_ref.shape)
    lane = lax.broadcasted_iota(jnp.int32, scales_ref.shape, 1)
    scales_ref[...] = jnp.where(lane == 0, scale_one, scale_two)


def feed_forward(attended, frames, out, up, down, final, vectors, block):
    count, model = frames.shape
    inner, width = up.shape[1], final.shape[1]
    part = lambda columns: pl.BlockSpec((block, columns), lambda i: (i, 0))
    turned = lambda rows: pl.BlockSpec((rows, block), lambda i: (0, i))
    shape = jax.ShapeDtypeStruct
    low, full = jnp.bfloat16, jnp.float32
    operands = (attended, frames, out, up, down, final)
    return pl.pallas_call(
        functools.partial(feed_forward_kernel, max(inner // model, 1)),
        grid=(count // block,),
        in_specs=[part(model), part(model)]
        + [rows_of(x) for x in operands[2:]]
        + [vector_spec(x) for x in vectors],
        out_specs=[turned(model), part(model), part(inner), part(inner), part(model), turned(model), part(PAIR)]
        + [turned(width), turned(8)],
        out_shape=[
            shape((model, count), low),
            shape((count, model), low),
            shape((count, inner), low),
            shape((count, inner), low),
            shape((count, model), low),
            shape((model, count), low),
            shape((count, PAIR), full),
            shape((width, count), full),
            shape((8, count), full),
        ],
        cost_estimate=small_cost,
        compiler_params=pltpu.CompilerParams(vmem_limit_bytes=62 << 20),
    )(*operands, *vectors)


def feed_forward_back_kernel(
    parts,
    d_final_ref,
    slope_ref,
    normed_one_ref,
    normed_two_ref,
    scales_ref,
    final_ref,
    up_ref,
    down_ref,
    out_ref,
    gain_one_ref,
    gain_two_ref,
    down_turned_ref,
    upper_low_ref,
    resid_ref,
    branch_low_ref,
    attended_low_ref,
    sums_ref,
    up_sums_ref,
    final_sums_ref,
):
    @pl.when(pl.program_id(0) == 0)
    def _():
        sums_ref[...] = jnp.zeros_like(sums_ref)
        up_sums_ref[...] = jnp.zeros_like(up_sums_ref)
        final_sums_ref[...] = jnp.zeros_like(final_sums_ref)

    def add(row, values):
        sums_ref[row] += jnp.sum(values.reshape(-1, 8, values.shape[1]), axis=0)

    d_final = d_final_ref[...]
    final_sums_ref[...] += jnp.sum(d_final.astype(jnp.float32).reshape(-1, 8, d_final.shape[1]), axis=0)
    grad = dot(d_final, final_ref[...], NT)
    normed = normed_two_ref[...].astype(jnp.float32)
    gain = gain_two_ref[...].reshape(1, -1)
    hidden = normalize_back(grad, normed, scales_ref[:, 1:2], gain)
    down_low = to_low(hidden)
    down_turned_ref[...] = down_low.T
    add(0, grad * normed)
    add(1, grad)
    add(2, down_low.astype(jnp.float32))
    chunk = up_ref.shape[1] // parts
    for part in range(parts):
        at = pl.ds(part * chunk, chunk)
        upper = dot(down_low, down_ref[at, :], NT) * slope_ref[:, at].astype(jnp.float32)
        upper_low = to_low(upper)
        upper_low_ref[:, at] = upper_low
        up_sums_ref[:, at] += jnp.sum(upper.reshape(-1, 8, chunk), axis=0)
        hidden = hidden + dot(upper_low, up_ref[:, at], NT)
    normed = normed_one_ref[...].astype(jnp.float32)
    gain = gain_one_ref[...].reshape(1, -1)
    resid = normalize_back(hidden, normed, scales_ref[:, 0:1], gain)
    resid_ref[...] = resid
    branch_low = to_low(resid)
    branch_low_ref[...] = branch_low
    attended_low_ref[...] = to_low(dot(branch_low, out_ref[...], NT))
    add(3, hidden * normed)
    add(4, hidden)
    add(5, branch_low.astype(jnp.float32))


def feed_forward_back(d_final, slope, normed_one, normed_two, scales, final, up, down, out, gains, block):
    count, model = normed_one.shape
    inner = up.shape[1]
    part = lambda columns: pl.BlockSpec((block, columns), lambda i: (i, 0))
    shape = jax.ShapeDtypeStruct
    low, full = jnp.bfloat16, jnp.float32
    return pl.pallas_call(
        functools.partial(feed_forward_back_kernel, max(inner // model, 1)),
        grid=(count // block,),
        in_specs=[part(d_final.shape[1]), part(inner), part(model), part(model), part(PAIR)]
        + [rows_of(x) for x in (final, up, down, out)]
        + [vector_spec(x) for x in gains],
        out_specs=[pl.BlockSpec((model, block), lambda i: (0, i))]
        + [part(inner), part(model), part(model), part(model)]
        + [
            pl.BlockSpec((6, 8, model), lambda i: (0, 0, 0)),
            pl.BlockSpec((8, inner), lambda i: (0, 0)),
            pl.BlockSpec((8, d_final.shape[1]), lambda i: (0, 0)),
        ],
        out_shape=[
            shape((model, count), low),
            shape((count, inner), low),
            shape((count, model), full),
            shape((count, model), low),
            shape((count, model), low),
            shape((6, 8, model), full),
            shape((8, inner), full),
            shape((8, d_final.shape[1]), full),
        ],
        cost_estimate=small_cost,
        compiler_params=pltpu.CompilerParams(vmem_limit_bytes=62 << 20),
    )(d_final, slope, normed_one, normed_two, scales, final, up, down, out, *gains)


def candidate_kernel(
    slots, owners, keep, index_ref, rows_ref, unit_ref, scale_ref, positive_ref, masked_ref,
    loss_ref, final_low_ref, positive_part_ref, rows_grad_ref,
    packed, mass, pull, total, unit_low, weighted,
):
    step = pl.program_id(0)
    frames = unit_ref.shape[1]
    own = rows_ref.shape[0]
    lanes = 128
    words = lax.broadcasted_iota(jnp.int32, (128, lanes), 0)

    def fill(at_mass):
        def count(tile, _):
            at = pl.ds(pl.multiple_of(tile * lanes, lanes), lanes)
            acc = jnp.zeros((128, lanes), jnp.int32)
            for slot in range(slots):
                index = index_ref[0, pl.ds(slot, 1), at]
                low = jnp.bitwise_and(index, 127)
                unit = jnp.where(index >= 0, jnp.left_shift(1, 4 * jnp.right_shift(index, 7)), 0)
                acc = acc + jnp.where(words == low, unit, 0)
            packed[:, at] = acc
            return 0

        lax.fori_loop(0, frames // lanes, count, 0)

        wide = 4

        def part(number, _):
            first = number * (128 * wide)
            at = pl.ds(pl.multiple_of(first, 128 * wide), 128 * wide)
            cosines = dot(rows_ref[at, :], unit_low[...])
            for piece in range(wide):
                cosine = cosines[piece * 128 : (piece + 1) * 128]
                shift = 4 * (number * wide + piece)
                times = jnp.bitwise_and(lax.shift_right_logical(packed[...], shift), 15)
                value = times.astype(jnp.float32) * jnp.exp2(cosine)
                total[...] += jnp.sum(value.reshape(16, 8, frames), axis=0)
                low = pl.multiple_of(at_mass + first + piece * 128, 128)
                mass[pl.ds(low, 128), :] = to_low(value)
            return 0

        lax.fori_loop(0, own // (128 * wide), part, 0, unroll=1)

    @pl.when(step == 0)
    def _():
        unit_low[...] = to_low(unit_ref[...])
        total[...] = jnp.zeros_like(total)
        pull[...] = jnp.zeros_like(pull)

    @pl.when(step < owners)
    def _():
        at_mass = step * own if keep else 0
        fill(at_mass)
        pull[...] += dot(rows_ref[...], mass[pl.ds(pl.multiple_of(at_mass, own), own), :], TN)

    @pl.when(step == owners - 1)
    def _():
        score_scale = log2e / similarity_softening_factor
        unit, positive, masked = unit_ref[...], positive_ref[...], masked_ref[...]
        mass_sum = jnp.sum(total[...], axis=0, keepdims=True)
        score = jnp.sum(unit * positive, axis=0, keepdims=True) * (1.0 / similarity_softening_factor)
        whole = jnp.exp(score) + mass_sum
        loss_ref[...] = (masked * (jnp.log(whole) - score))[0]
        weight = masked / whole * (1.0 / similarity_softening_factor)
        d_score = -weight * mass_sum
        d_unit = d_score * positive + weight * (1.0 / score_scale) * pull[...]
        inner = jnp.sum(d_unit * unit, axis=0, keepdims=True)
        final_low_ref[...] = to_low((scale_ref[0:1, :] * (d_unit - unit * inner)).T)
        positive_part_ref[...] = (d_score * unit).T
        weighted[...] = to_low((weight * unit).T)

    @pl.when(step >= owners)
    def _():
        at_mass = (step - owners) * own if keep else 0
        if not keep:
            fill(at_mass)
        rows_grad_ref[...] = to_low(dot(mass[pl.ds(pl.multiple_of(at_mass, own), own), :], weighted[...]))


def candidates(index, rows, unit, scale, positive, masked):
    owners, slots, frames = index.shape
    width = rows.shape[1]
    own = rows.shape[0] // owners
    keep = rows.shape[0] * frames * 2 <= 16 << 20
    again = (lambda i: jnp.minimum(i, owners - 1)) if keep else (lambda i: lax.rem(i, owners))
    shape = jax.ShapeDtypeStruct
    return pl.pallas_call(
        functools.partial(candidate_kernel, slots, owners, keep),
        grid=(2 * owners,),
        in_specs=[
            pl.BlockSpec((1, slots, frames), lambda i: (again(i), 0, 0)),
            pl.BlockSpec((own, width), lambda i: (again(i), 0)),
            rows_of(unit),
            rows_of(scale),
            rows_of(positive),
            rows_of(masked),
        ],
        out_specs=[
            pl.BlockSpec((frames,), lambda i: (0,)),
            pl.BlockSpec((frames, width), lambda i: (0, 0)),
            pl.BlockSpec((frames, width), lambda i: (0, 0)),
            pl.BlockSpec((own, width), lambda i: (jnp.maximum(i - owners, 0), 0)),
        ],
        out_shape=[
            shape((frames,), jnp.float32),
            shape((frames, width), jnp.bfloat16),
            shape((frames, width), jnp.float32),
            shape((rows.shape[0], width), jnp.bfloat16),
        ],
        scratch_shapes=[
            pltpu.VMEM((128, frames), jnp.int32),
            pltpu.VMEM((rows.shape[0] if keep else own, frames), jnp.bfloat16),
            pltpu.VMEM((width, frames), jnp.float32),
            pltpu.VMEM((8, frames), jnp.float32),
            pltpu.VMEM((width, frames), jnp.bfloat16),
            pltpu.VMEM((frames, width), jnp.bfloat16),
        ],
        cost_estimate=small_cost,
        compiler_params=pltpu.CompilerParams(vmem_limit_bytes=62 << 20),
    )(index, rows, unit, scale, positive, masked)


def down_grad_kernel(active_ref, turned_ref, *refs):
    out_ref = refs[-1]
    _, groups, blocks, rows, wide = out_ref.shape
    value = to_low(dot(turned_ref[...], active_ref[...]))
    each = value.shape[0] // groups
    across = value.shape[1] // PAIR
    for group in range(groups):
        for tile in range(each // rows * across):
            top = group * each + tile // across * rows
            part = value[top : top + rows, tile % across * PAIR : (tile % across + 1) * PAIR]
            lanes = pl.ds(tile * PAIR % wide, PAIR)
            out_ref[0, group, tile * PAIR // wide, :, lanes] = part


def down_grad(active, turned, members, groups, width, after):
    count, inner = active.shape
    model = turned.shape[0]
    share, rows = inner // members, model // members
    block = (1, groups, model * share // (groups * rows * width), rows, width)
    return pl.pallas_call(
        down_grad_kernel,
        grid=(members,),
        in_specs=[pl.BlockSpec((count, share), lambda i: (0, i)), rows_of(turned)]
        + [pl.BlockSpec(memory_space=pl.ANY)] * len(after),
        out_specs=pl.BlockSpec(block, lambda i: (i, 0, 0, 0, 0)),
        out_shape=jax.ShapeDtypeStruct((members, *block[1:]), jnp.bfloat16),
        cost_estimate=small_cost,
        compiler_params=pltpu.CompilerParams(vmem_limit_bytes=62 << 20),
    )(active, turned, *after)


def up_grad_kernel(
    groups, core_ref, hidden_ref, upper_ref, attended_ref, branch_ref, output_ref, final_ref, *refs
):
    kept_ref, sent_ref, attended_turned, held = refs[-4:]
    group = pl.program_id(0)
    core = core_ref[0]
    lines, share = kept_ref.shape[1], kept_ref.shape[2]

    @pl.when(group == 0)
    def _():
        attended_turned[...] = attended_ref[...].T

    wide = upper_ref.shape[1]
    side = final_ref.shape[1]
    held[:, :, :, :wide] = to_low(dot(hidden_ref[...], upper_ref[...])).reshape(lines, 2, share, wide)

    @pl.when(group < groups - 1)
    def _():
        value = dot(attended_turned[...], branch_ref[...])
        held[:, :, :, wide:] = to_low(value).reshape(lines, 2, share, side)

    @pl.when(group == groups - 1)
    def _():
        value = dot(output_ref[...], final_ref[...])
        held[:, :, :, wide:] = to_low(value).reshape(lines, 2, share, side)

    kept_ref[0] = held[:, core]
    sent_ref[0] = held[:, 1 - core]


def up_grad(core, hidden, upper, attended, branch, output, final, members, groups, after):
    model, count = hidden.shape
    wide, side = upper.shape[1] // groups, final.shape[1]
    lines, share = members // 2, model // members
    whole = lambda columns: pl.BlockSpec((count, columns), lambda g, core: (0, 0))
    out = pl.BlockSpec((1, lines, share, wide + side), lambda g, core: (g, 0, 0, 0))
    shape = jax.ShapeDtypeStruct((groups, lines, share, wide + side), jnp.bfloat16)
    last = model // side - 1
    return pl.pallas_call(
        functools.partial(up_grad_kernel, groups),
        grid_spec=pltpu.PrefetchScalarGridSpec(
            num_scalar_prefetch=1,
            grid=(groups,),
            in_specs=[
                rows_of(hidden),
                pl.BlockSpec((count, wide), lambda g, core: (0, g)),
                whole(model),
                pl.BlockSpec((count, side), lambda g, core: (0, jnp.minimum(g, last))),
                rows_of(output),
                whole(side),
            ]
            + [pl.BlockSpec(memory_space=pl.ANY)] * len(after),
            out_specs=[out, out],
            scratch_shapes=[
                pltpu.VMEM((model, count), jnp.bfloat16),
                pltpu.VMEM((lines, 2, share, wide + side), jnp.bfloat16),
            ],
        ),
        out_shape=[shape, shape],
        cost_estimate=small_cost,
        compiler_params=pltpu.CompilerParams(vmem_limit_bytes=62 << 20),
    )(core, hidden, upper, attended, branch, output, final, *after)


def projection_grad_kernel(grads, pieces, core_ref, frames_ref, *refs):
    kept_ref, sent_ref, held = refs[-3:]
    core = core_ref[0]
    turned = frames_ref[...].T
    each = kept_ref.shape[3] // PAIR
    lines, share = kept_ref.shape[1], kept_ref.shape[2]
    members = 2 * lines

    def put(number):
        for column in range(held.shape[3] // PAIR):
            tile = number * (held.shape[3] // PAIR) + column
            group, lanes = tile // each, pl.ds(tile % each * PAIR, PAIR)
            at = pl.ds(column * PAIR, PAIR)
            kept_ref[group, :, :, lanes] = held[:, core, :, at]
            sent_ref[group, :, :, lanes] = held[:, 1 - core, :, at]

    for number, ref in enumerate(refs[:grads]):
        held[...] = to_low(dot(turned, ref[...])).reshape(held.shape)
        put(number)
    if len(refs) == grads + 3:
        return
    piece_refs = refs[grads : grads + pieces]
    model_ref, up_ref, final_ref, target_ref, square_ref = refs[grads + pieces : -3]

    def total(values):
        return jnp.sum(values, axis=0, keepdims=True)

    vectors = (
        jnp.concatenate([total(ref[0]) for ref in piece_refs], axis=1),
        jnp.concatenate([total(ref[1]) for ref in piece_refs], axis=1),
        total(model_ref[5]),
        total(model_ref[3]),
        total(model_ref[4]),
        total(up_ref[...]),
        total(model_ref[2]),
        total(model_ref[0]),
        total(model_ref[1]),
        total(final_ref[...]),
        total(target_ref[...]),
    )
    square = square_ref[...]
    rows = square.shape[0] // members
    held[...] = jnp.zeros_like(held)
    for member in range(members):
        line, side = member // 2, member % 2
        parts = []
        for vector in vectors:
            size = vector.shape[1] // members
            for low in range(member * size, (member + 1) * size, PAIR):
                part = vector[:, low : min(low + PAIR, (member + 1) * size)]
                parts.append(jnp.pad(part, ((0, 0), (0, PAIR - part.shape[1]))))
        parts.append(jnp.zeros((share - len(parts), PAIR), jnp.float32))
        held[line, side, :, :PAIR] = to_low(jnp.concatenate(parts, axis=0))
        own = square[member * rows : (member + 1) * rows]
        for half in range(square.shape[1] // PAIR):
            part = own[:, half * PAIR : (half + 1) * PAIR]
            held[line, side, half * rows : (half + 1) * rows, PAIR:] = to_low(part)
    put(grads)


def projection_grad(core, frames, grads, pieces, sums, members, groups, after):
    count, model = frames.shape
    lines, share = members // 2, model // members
    width = grads[0].shape[1]
    wide = (len(grads) + bool(sums)) * width // groups
    shape = jax.ShapeDtypeStruct((groups, lines, share, wide), jnp.bfloat16)
    vmem = pl.BlockSpec(memory_space=pltpu.VMEM)

    def kernel(*refs):
        used = 2 + len(grads) + len(pieces) + len(sums)
        projection_grad_kernel(len(grads), len(pieces), *refs[:used], *refs[used + len(after) :])

    return pl.pallas_call(
        kernel,
        in_specs=[pl.BlockSpec(memory_space=pltpu.SMEM)]
        + [vmem] * (1 + len(grads) + len(pieces) + len(sums))
        + [pl.BlockSpec(memory_space=pl.ANY)] * len(after),
        out_specs=[vmem, vmem],
        out_shape=[shape, shape],
        scratch_shapes=[pltpu.VMEM((lines, 2, share, width), jnp.bfloat16)],
        cost_estimate=small_cost,
        compiler_params=pltpu.CompilerParams(vmem_limit_bytes=62 << 20),
    )(core, frames, *grads, *pieces, *sums, *after)


def slot_rows(distractors, members):
    count, slots = distractors.shape
    turns = -(-slots // members)
    padded = jnp.pad(distractors, ((0, 0), (0, turns * members - slots)), constant_values=-1)
    padded = padded.T.reshape(turns, members, count)
    period = members // math.gcd(slots, members)
    frame = jnp.arange(count, dtype=jnp.int32) % period
    placed = padded
    for phase in range(1, period):
        turned = jnp.roll(padded, phase * slots % members, axis=1)
        placed = jnp.where(frame == phase, turned, placed)
    return placed.transpose(1, 0, 2)


def target_kernel(came_ref, part_ref, unit_ref, scale_ref, low_ref, matrix_ref, *refs):
    grad_ref, matrix_grad_ref, sums_ref = refs[-3:]
    grad_unit = part_ref[...] + came_ref[...].astype(jnp.float32)
    unit = unit_ref[...]
    inner = jnp.sum(grad_unit * unit, axis=-1, keepdims=True)
    low = to_low(scale_ref[:, 0:1] * (grad_unit - unit * inner))
    grad_ref[...] = dot(low, to_low(matrix_ref[...]), NT)
    matrix_grad_ref[...] = dot(to_low(low_ref[...]), low, TN)
    sums_ref[...] = jnp.sum(low.astype(jnp.float32).reshape(-1, 8, low.shape[1]), axis=0)


def target_back(came, part, unit, scale, low, matrix, after):
    count, width = part.shape
    vmem = pl.BlockSpec(memory_space=pltpu.VMEM)
    shape = jax.ShapeDtypeStruct
    return pl.pallas_call(
        target_kernel,
        in_specs=[vmem] * 6 + [pl.BlockSpec(memory_space=pl.ANY)] * len(after),
        out_specs=[vmem] * 3,
        out_shape=[
            shape((count, width), jnp.float32),
            shape((width, width), jnp.float32),
            shape((8, width), jnp.float32),
        ],
        cost_estimate=small_cost,
        compiler_params=pltpu.CompilerParams(vmem_limit_bytes=62 << 20),
    )(came, part, unit, scale, low, matrix, *after)


def inputs_kernel(parts, resid_ref, *refs):
    out_ref = refs[-1]
    total = resid_ref[...]
    for matrix in range(3):
        low = 0
        for part in range(parts):
            grad_ref = refs[matrix * parts + part]
            high = low + grad_ref.shape[1]
            total = total + dot(grad_ref[...], refs[3 * parts + matrix][:, low:high], NT)
            low = high
    out_ref[...] = total


def inputs_back(resid, grads, matrices, block, after):
    count, model = resid.shape
    part = lambda x: pl.BlockSpec((block, x.shape[1]), lambda i: (i, 0))
    flat = [g for parts in grads for g in parts]
    return pl.pallas_call(
        functools.partial(inputs_kernel, len(grads[0])),
        grid=(count // block,),
        in_specs=[part(resid)]
        + [part(g) for g in flat]
        + [rows_of(m) for m in matrices]
        + [pl.BlockSpec(memory_space=pl.ANY)] * len(after),
        out_specs=part(resid),
        out_shape=jax.ShapeDtypeStruct(resid.shape, jnp.float32),
        cost_estimate=small_cost,
        compiler_params=pltpu.CompilerParams(vmem_limit_bytes=62 << 20),
    )(resid, *flat, *matrices, *after)


def target_prepare_kernel(targets_ref, matrix_ref, bias_ref, rows_ref, unit_ref, turned_ref, scale_ref):
    low = to_low(dot(to_low(targets_ref[...]), to_low(matrix_ref[...])) + bias_ref[...].reshape(1, -1))
    positive = low.astype(jnp.float32)
    scale = lax.rsqrt(jnp.sum(positive * positive, axis=-1, keepdims=True) + cosine_eps)
    unit = positive * scale
    rows_ref[...] = to_low(unit * (log2e / similarity_softening_factor))
    unit_ref[...] = unit
    turned_ref[...] = unit.T
    scale_ref[...] = jnp.broadcast_to(scale, scale_ref.shape)


def target_prepare(targets, matrix, bias):
    count, width = targets.shape
    vmem = pl.BlockSpec(memory_space=pltpu.VMEM)
    shape = jax.ShapeDtypeStruct
    return pl.pallas_call(
        target_prepare_kernel,
        in_specs=[vmem] * 3,
        out_specs=[vmem] * 4,
        out_shape=[
            shape((count, width), jnp.bfloat16),
            shape((count, width), jnp.float32),
            shape((width, count), jnp.float32),
            shape((count, PAIR), jnp.float32),
        ],
        cost_estimate=small_cost,
        compiler_params=pltpu.CompilerParams(vmem_limit_bytes=62 << 20),
    )(targets, matrix, bias)


def project_kernel(frames_ref, wq_ref, wk_ref, wv_ref, bq_ref, bv_ref, *refs):
    low_ref, q_ref, k_ref, v_ref, mq, mk, mv = refs[-7:]


    @pl.when(pl.program_id(0) == 0)
    def _():
        mq[...] = to_low(wq_ref[...])
        mk[...] = to_low(wk_ref[...])
        mv[...] = to_low(wv_ref[...])

    low = to_low(frames_ref[...])
    low_ref[...] = low
    q_ref[...] = to_low(dot(low, mq[...]) + bq_ref[...].reshape(1, -1))
    k_ref[...] = to_low(dot(low, mk[...]))
    v_ref[...] = to_low(dot(low, mv[...]) + bv_ref[...].reshape(1, -1))


def vector_spec(values):
    return pl.BlockSpec(values.shape, lambda i, *_: (0,))


def project(frames, w_query, w_key, w_value, b_query, b_value, block, after):
    count, model = frames.shape
    part = pl.BlockSpec((block, model), lambda i: (i, 0))
    return pl.pallas_call(
        project_kernel,
        grid=(count // block,),
        in_specs=[part]
        + [rows_of(w) for w in (w_query, w_key, w_value)]
        + [vector_spec(b) for b in (b_query, b_value)]
        + [pl.BlockSpec(memory_space=pl.ANY)] * len(after),
        out_specs=[part] * 4 + [rows_of(w_query)] * 3,
        out_shape=[jax.ShapeDtypeStruct((count, model), jnp.bfloat16)] * 4
        + [jax.ShapeDtypeStruct((model, model), jnp.bfloat16)] * 3,
        cost_estimate=small_cost,
        compiler_params=pltpu.CompilerParams(vmem_limit_bytes=62 << 20),
    )(frames, w_query, w_key, w_value, b_query, b_value, *after)


def exchange(sent):
    members = lax.axis_size("tm")
    return lax.ppermute(sent, "tm", [(i, i ^ 1) for i in range(members)])


def split_kernel(counts, pieces, choice_ref, *refs):
    out_refs = refs[-pieces:]
    number, low, lanes = 0, 0, 0
    for count in counts:
        if count < 3:
            total = sum((refs[number + term][0] for term in range(1, count)), refs[number][0])
        else:
            total = to_low(sum(refs[number + term][0].astype(jnp.float32) for term in range(count)))
        high = lanes + total.shape[-1]
        for piece in range(pieces):

            @pl.when(pl.program_id(0) == piece)
            def _(piece=piece, total=total, low=low, lanes=lanes, high=high):
                if total.ndim == 3:
                    out_refs[piece][low : low + total.shape[0]] = total
                else:
                    out_refs[piece][:, lanes:high] = total

        number, low, lanes = number + count, low + total.shape[0], high


def split_sum(choice, sums, pieces, after):
    terms = [term for group in sums for term in group]
    first = [group[0].shape[1:] for group in sums]
    if len(first[0]) == 3:
        rest = (sum(shape[0] for shape in first), *first[0][1:])
    else:
        rest = (first[0][0], sum(shape[1] for shape in first))

    def source(term):
        zeros = (0,) * (term.ndim - 1)
        return pl.BlockSpec((1, *term.shape[1:]), lambda i, choice: (choice[0] ^ i, *zeros))

    return pl.pallas_call(
        functools.partial(split_kernel, [len(group) for group in sums], pieces),
        grid_spec=pltpu.PrefetchScalarGridSpec(
            num_scalar_prefetch=1,
            grid=(pieces,),
            in_specs=[source(term) for term in terms]
            + [pl.BlockSpec(memory_space=pl.ANY)] * len(after),
            out_specs=[pl.BlockSpec(rest, lambda i, choice: (0,) * len(rest))] * pieces,
        ),
        out_shape=[jax.ShapeDtypeStruct(rest, jnp.bfloat16)] * pieces,
        cost_estimate=small_cost,
        compiler_params=pltpu.CompilerParams(vmem_limit_bytes=62 << 20),
    )(choice, *terms, *after)


def swap(pieces, axis="grp", stride=1):
    size = lax.axis_size(axis)
    return [pieces[0]] + [
        lax.ppermute(piece, axis, [(i, i ^ (k * stride)) for i in range(size)])
        for k, piece in enumerate(pieces)
        if k
    ]


def line_kernel(terms, *refs):
    total = refs[0][...].astype(jnp.float32)
    for term in range(1, terms):
        total = total + refs[term][...].astype(jnp.float32)
    refs[-1][...] = to_low(total)


def line_sum(terms, after):
    lines, rest = terms[0].shape[0], terms[0].shape[1:]
    block = pl.BlockSpec((lines // 2, *rest), lambda i: (i, *(0,) * len(rest)))
    return pl.pallas_call(
        functools.partial(line_kernel, len(terms)),
        grid=(2,),
        in_specs=[block] * len(terms) + [pl.BlockSpec(memory_space=pl.ANY)] * len(after),
        out_specs=block,
        out_shape=jax.ShapeDtypeStruct(terms[0].shape, jnp.bfloat16),
        cost_estimate=large_cost,
        compiler_params=pltpu.CompilerParams(vmem_limit_bytes=62 << 20),
    )(*terms, *after)


def core_pairs():
    return [[2 * i, 2 * i + 1] for i in range(lax.axis_size("tm") // 2)]


def chip_lines():
    return [list(range(first, lax.axis_size("tm"), 2)) for first in range(2)]


def scatter(value, axis, among=None):
    return lax.psum_scatter(value, axis, scatter_dimension=0, axis_index_groups=among)


def over_lines(value):
    return lax.all_to_all(value, "tm", 0, 0, tiled=True, axis_index_groups=chip_lines())


def share_kernel(terms, start, *refs):
    out_ref, share_ref = refs[-1], refs[terms]
    wide = refs[0].shape[2]
    for copy in range(out_ref.shape[0]):
        low = 0
        for at in range(start, refs[0].shape[0]):
            total = sum(ref[at].astype(jnp.float32) for ref in refs[:terms])
            out_ref[copy, :, low : low + wide] = to_low(total)
            low += wide
        out_ref[copy, :, low:] = share_ref[...]


def shares(terms, start, share, groups, after):
    blocks, rows, wide = terms[0].shape
    wide = (blocks - start) * wide + share.shape[1]
    vmem = pl.BlockSpec(memory_space=pltpu.VMEM)
    return pl.pallas_call(
        functools.partial(share_kernel, len(terms), start),
        in_specs=[vmem] * (len(terms) + 1) + [pl.BlockSpec(memory_space=pl.ANY)] * len(after),
        out_specs=vmem,
        out_shape=jax.ShapeDtypeStruct((groups, rows, wide), jnp.bfloat16),
        cost_estimate=small_cost,
        compiler_params=pltpu.CompilerParams(vmem_limit_bytes=62 << 20),
    )(*terms, share, *after)


def place(kernel, arrays, shapes, after, choice=None):
    vmem = pl.BlockSpec(memory_space=pltpu.VMEM)
    first = [] if choice is None else [choice]
    used = len(first) + len(arrays)
    return pl.pallas_call(
        lambda *refs: kernel(*refs[:used], *refs[used + len(after) :]),
        in_specs=[pl.BlockSpec(memory_space=pltpu.SMEM)] * len(first)
        + [vmem] * len(arrays)
        + [pl.BlockSpec(memory_space=pl.ANY)] * len(after),
        out_specs=[vmem] * len(shapes),
        out_shape=[jax.ShapeDtypeStruct(s, jnp.float32) for s in shapes],
        cost_estimate=small_cost,
        compiler_params=pltpu.CompilerParams(vmem_limit_bytes=62 << 20),
    )(*first, *arrays, *after)


def line_total(terms, after):
    vmem = pl.BlockSpec(memory_space=pltpu.VMEM)
    return pl.pallas_call(
        functools.partial(line_kernel, len(terms)),
        in_specs=[vmem] * len(terms) + [pl.BlockSpec(memory_space=pl.ANY)] * len(after),
        out_specs=vmem,
        out_shape=jax.ShapeDtypeStruct(terms[0].shape, jnp.bfloat16),
        cost_estimate=small_cost,
        compiler_params=pltpu.CompilerParams(vmem_limit_bytes=62 << 20),
    )(*terms, *after)


def on_device(
    frames,
    targets,
    lengths,
    span_starts,
    distractors,
    w_query,
    b_query,
    w_key,
    w_value,
    b_value,
    w_out,
    b_out,
    norm_gain,
    norm_bias,
    w_up,
    b_up,
    w_down,
    b_down,
    final_gain,
    final_bias,
    w_final,
    b_final,
    w_target,
    b_target,
):
    count, model = frames.shape
    width = targets.shape[1]
    inner = w_up.shape[1]
    members, groups = lax.axis_size("tm"), lax.axis_size("grp")
    block = min(count, 256)
    share = model // members
    place_in_line = lax.axis_index("tm")
    core = (place_in_line % 2)[None].astype(jnp.int32)
    line = (place_in_line // 2)[None].astype(jnp.int32)
    group = lax.axis_index("grp")[None].astype(jnp.int32)

    own_rows, positive_unit, positive_turned, positive_scale = target_prepare(targets, w_target, b_target)
    rows = lax.all_gather(own_rows, "tm", tiled=True)
    index = slot_rows(distractors, members)

    segment, age = utterances(lengths[0], count)
    masked = span_mask(span_starts, age, count)
    span, hot_query, hot_key = attention_plan(lengths[0], segment, count, 2 * block, block)
    span_back, _, _ = attention_plan(lengths[0], segment, count, block, block)
    frames_low, query, key, value, *own_matrices = project(
        frames, w_query, w_key, w_value, b_query, b_value, block, (own_rows,)
    )
    attended_low, log_total, out_matrix, up_matrix, down_matrix, final_matrix = attend(
        span, query, key, value, hot_query, hot_key, (w_out, w_up, w_down, w_final), 2 * block, block, 2
    )
    (
        hidden_turned,
        normed_one,
        active_low,
        slope,
        normed_two,
        output_turned,
        scales,
        final_unit,
        final_scale,
    ) = feed_forward(
        attended_low,
        frames,
        out_matrix,
        up_matrix,
        down_matrix,
        final_matrix,
        (b_out, norm_gain, norm_bias, b_down, final_gain, final_bias, b_up, b_final),
        block,
    )
    losses, d_final_low, positive_part, d_rows = candidates(
        index, rows, final_unit, final_scale, positive_turned, masked[None]
    )
    came = lax.psum_scatter(d_rows, "tm", scatter_dimension=0, tiled=True)

    (
        d_down_turned,
        d_upper_low,
        d_resid,
        d_branch_low,
        d_attended_low,
        model_sums,
        up_sums,
        final_sums,
    ) = feed_forward_back(
        d_final_low,
        slope,
        normed_one,
        normed_two,
        scales,
        final_matrix,
        up_matrix,
        down_matrix,
        out_matrix,
        (norm_gain, final_gain),
        block,
    )
    def attention_back(piece, pieces, after):
        return attend_back(
            span_back,
            query,
            key,
            value,
            d_attended_low,
            attended_low,
            hot_query,
            hot_key,
            log_total,
            lengths.shape[1],
            block,
            block,
            2,
            piece,
            pieces,
            after,
        )


    def total(values):
        return jnp.sum(values, axis=0)

    def vector_sums(piece_sums, target_sums):
        return (
            jnp.concatenate([total(s[0]) for s in piece_sums]),
            jnp.concatenate([total(s[1]) for s in piece_sums]),
            total(model_sums[5]),
            total(model_sums[3]),
            total(model_sums[4]),
            total(up_sums),
            total(model_sums[2]),
            total(model_sums[0]),
            total(model_sums[1]),
            total(final_sums),
            total(target_sums),
        )

    if share % 16 or (inner // members) % PAIR or model != (groups - 1) * width:
        back = [attention_back(piece, 3, ()) for piece in range(3)]
        d_query, d_key, d_value, piece_sums = ([part[k] for part in back] for k in range(4))
        target_grad, grad_w_target, target_sums = target_back(
            came, positive_part, positive_unit, positive_scale, targets, w_target, ()
        )
        input_grad = inputs_back(
            d_resid, (d_query, d_key, d_value), own_matrices, block, ()
        )

        def reduced(grad):
            part = lax.psum_scatter(grad, "tm", scatter_dimension=0, tiled=True)
            return lax.psum(to_low(part), "grp").astype(jnp.float32)

        def projected(parts):
            return reduced(product_left(frames_low, jnp.concatenate(parts, axis=1)))

        small = [reduced(vector) for vector in vector_sums(piece_sums, target_sums)]
        return (
            losses,
            input_grad,
            target_grad,
            projected(d_query),
            small[0],
            projected(d_key),
            projected(d_value),
            small[1],
            reduced(product_left(attended_low, d_branch_low)),
            small[2],
            small[3],
            small[4],
            reduced(product(hidden_turned, d_upper_low)),
            small[5],
            reduced(product(d_down_turned, active_low).T),
            small[6],
            small[7],
            small[8],
            reduced(product(output_turned, d_final_low)),
            small[9],
            reduced(grad_w_target),
            small[10],
        )

    up_kept, up_sent = up_grad(
        core,
        hidden_turned,
        d_upper_low,
        attended_low,
        d_branch_low,
        output_turned,
        d_final_low,
        members,
        groups,
        (),
    )
    up_came = exchange(up_sent)
    down_parts = down_grad(active_low, d_down_turned, members, groups, width, (up_sent,))
    down_part = scatter(down_parts, "tm")
    up_group = split_sum(group, [[up_kept, up_came]], groups, (down_parts,))
    up_groups = swap(up_group)

    def projections(pieces, sums, after):
        grads = [back[piece][k] for k in range(3) for piece in pieces]
        sums_of = [part[3] for part in back] if sums else []
        return projection_grad(core, frames_low, grads, sums_of, sums, members, groups, after)

    back = [attention_back(0, 3, (up_group[1],))]
    target_grad, grad_w_target, target_sums = target_back(
        came, positive_part, positive_unit, positive_scale, targets, w_target, (back[0][0],)
    )
    back.append(attention_back(1, 3, (grad_w_target,)))
    early_kept, early_sent = projections((0, 1), (), ())
    early_came = exchange(early_sent)
    up_line = line_sum(up_groups, (early_sent,))
    up_share = scatter(up_line, "tm", chip_lines())
    early_group = split_sum(group, [[early_kept, early_came]], groups, (up_line,))
    early_groups = swap(early_group)
    back.append(attention_back(2, 3, (early_group[1],)))
    d_query, d_key, d_value, piece_sums = ([part[k] for part in back] for k in range(4))
    late_kept, late_sent = projections(
        (2,), (model_sums, up_sums, final_sums, target_sums, grad_w_target), ()
    )
    late_came = exchange(late_sent)
    early_line = line_sum(early_groups, (late_sent,))
    late_group = split_sum(group, [[late_kept, late_came], [down_part]], groups, (early_line,))
    late_groups = swap(late_group)
    input_grad = inputs_back(
        d_resid, (d_query, d_key, d_value), own_matrices, block, (late_group[1],)
    )
    own_line = split_sum(line, [[early_line], late_groups], members // 2, (input_grad,))
    own_lines = swap(own_line, "tm", 2)
    most_shares = shares(late_groups, members // 2, up_share, groups, (own_line[1],))
    most = lax.all_to_all(most_shares, "grp", 0, 0, tiled=True)

    def by_group(choice_ref, refs, put):
        for piece in range(groups):
            for number in range(groups):

                @pl.when(choice_ref[0] ^ piece == number)
                def _(piece=piece, number=number):
                    put(number, refs[piece], refs[groups:])

    last = swap([line_total(own_lines, (most_shares,))] * groups)
    up_at = inner // members * (model // groups // share)
    side_at = up_at + inner // groups

    def put_most(most_ref, down_ref, up_ref, out_ref, final_ref):
        rows = model // groups
        across = inner // members // PAIR
        for at in range(groups):
            part = lambda low, high: most_ref[at, :, low:high].astype(jnp.float32)
            for tile in range(up_at // PAIR):
                top = at * rows + tile // across * share
                low = tile % across * PAIR
                down_ref[low : low + PAIR, top : top + share] = part(tile * PAIR, (tile + 1) * PAIR).T
            wide = inner // groups
            up_ref[:, at * wide : (at + 1) * wide] = part(up_at, side_at)
            if at < groups - 1:
                out_ref[:, at * width : (at + 1) * width] = part(side_at, side_at + width)
            else:
                final_ref[...] = part(side_at, side_at + width)

    grad_down, grad_up, grad_out, grad_final = place(
        put_most,
        [most],
        [(inner // members, model), (share, inner), (share, model), (share, width)],
        (last[0],),
    )
    third = model // 3
    early = [(k, piece * third + at) for k in range(3) for piece in (0, 1) for at in range(0, third, PAIR)]
    late = [(k, 2 * third + at) for k in range(3) for at in range(0, third, PAIR)]
    late += [(3, at) for at in range(0, 2 * PAIR, PAIR)]

    def put_last(number, ref, outs):
        low = 0
        for tiles in (early, late):
            each = len(tiles) // groups
            for k, lanes in tiles[number * each : (number + 1) * each]:
                value = ref[:, low : low + PAIR].astype(jnp.float32)
                low += PAIR
                if k < 3:
                    outs[k][:, lanes : lanes + PAIR] = value
                elif lanes:
                    rows = width // members
                    for half in range(width // PAIR):
                        part = value[half * rows : (half + 1) * rows]
                        outs[3][:, half * PAIR : (half + 1) * PAIR] = part
                else:
                    row = 0
                    for out in outs[4:]:
                        for start in range(0, out.shape[0], PAIR):
                            size = min(PAIR, out.shape[0] - start)
                            out[start : start + size] = value[row, :size]
                            row += 1

    sizes = [model] * 5 + [inner] + [model] * 3 + [width] * 2
    grad_query, grad_key, grad_value, grad_target, *small = place(
        lambda choice_ref, *refs: by_group(choice_ref, refs, put_last),
        last,
        [(share, model)] * 3
        + [(width // members, width)]
        + [(size // members,) for size in sizes],
        (grad_up,),
        group,
    )
    return (
        losses,
        input_grad,
        target_grad,
        grad_query,
        small[0],
        grad_key,
        grad_value,
        small[1],
        grad_out,
        small[2],
        small[3],
        small[4],
        grad_up,
        small[5],
        grad_down,
        small[6],
        small[7],
        small[8],
        grad_final,
        small[9],
        grad_target,
        small[10],
    )


def solution(mesh):
    placed = (
        P(("grp", "tm"), None),
        P(("grp", "tm"), None),
        P(("grp", "tm"), None),
        P(("grp", "tm")),
        P(("grp", "tm"), None),
        P(),
        P(),
        P(),
        P(),
        P(),
        P(),
        P(),
        P(),
        P(),
        P(),
        P(),
        P(),
        P(),
        P(),
        P(),
        P(),
        P(),
        P(),
        P(),
    )
    return jax.shard_map(
        on_device,
        mesh=mesh,
        in_specs=placed,
        out_specs=(
            P(("grp", "tm")),
            P(("grp", "tm"), None),
            P(("grp", "tm"), None),
            P("tm", None),
            P("tm"),
            P("tm", None),
            P("tm", None),
            P("tm"),
            P("tm", None),
            P("tm"),
            P("tm"),
            P("tm"),
            P("tm", None),
            P("tm"),
            P("tm", None),
            P("tm"),
            P("tm"),
            P("tm"),
            P("tm", None),
            P("tm"),
            P("tm", None),
            P("tm"),
        ),
        check_vma=False,
    )
```

```python
import functools
import math

import jax
import jax.numpy as jnp
from jax import lax
from jax.experimental import pallas as pl
from jax.experimental.pallas import tpu as pltpu
from jax.sharding import PartitionSpec as P

H = 12
HD = 64
NEG = 100
SPAN = 10


norm_eps = 1e-05
cosine_eps = 1e-06
similarity_softening_factor = 0.1
log2e = 1.4426950408889634
PAIR = 2 * HD
COLUMNS = 256
NT = (((1,), (1,)), ((), ()))
TN = (((0,), (0,)), ((), ()))
large_cost = pl.CostEstimate(flops=230_000_000_000, bytes_accessed=1, transcendentals=0)
small_cost = pl.CostEstimate(flops=1, bytes_accessed=1, transcendentals=0)


def to_low(values):
    return values.astype(jnp.bfloat16)


def product(left, right):
    return jnp.dot(left, right, preferred_element_type=jnp.float32)


def product_left(left, right):
    return lax.dot_general(
        left, right, (((0,), (0,)), ((), ())), preferred_element_type=jnp.float32
    )


def dot(a, b, dims=(((1,), (0,)), ((), ()))):
    return lax.dot_general(a, b, dims, preferred_element_type=jnp.float32)

def first_half(rows):
    return lax.broadcasted_iota(jnp.int32, (rows, PAIR), 1) < HD


def windows(span_ref, block, chunk, count, body):
    i = pl.program_id(0)
    start, chunks = span_ref[0, i], span_ref[1, i]
    total = count // chunk
    sizes = list(range(2, total + 1))
    for size in sizes:
        hit = (chunks <= size) if size == sizes[0] else (chunks == size)

        @pl.when(hit)
        def _(size=size):
            at = pl.multiple_of(jnp.minimum(start, total - size) * chunk, chunk)
            body(at, size * chunk)


def either(first, one, other, half):
    return jnp.where(first, one, other) if half == 0 else jnp.where(first, other, one)


def forward_kernel(casts, pairs, chunk, unroll, span_ref, q_ref, k_ref, v_ref, hotq_ref, hotk_ref, *refs):
    sources, out_ref, log_ref = refs[:casts], refs[casts], refs[casts + 1]
    results = refs[casts + 2 : 2 * casts + 2]
    wides, lows = refs[2 * casts + 2 : 3 * casts + 2], refs[3 * casts + 2 : 4 * casts + 2]
    in_sems, out_sems = refs[-2:]
    step = pl.program_id(0)

    def copies(pairs_of, sems):
        return [
            pltpu.make_async_copy(source, target, sems.at[number])
            for number, (source, target) in enumerate(pairs_of)
        ]

    @pl.when(step == 0)
    def _():
        for copy in copies(zip(sources, wides), in_sems):
            copy.start()

    block = q_ref.shape[0]
    count = k_ref.shape[0]
    scale = HD**-0.5 * log2e

    def body(at, size):
        near = pl.ds(at, size)
        lane = lax.broadcasted_iota(jnp.int32, (block, PAIR), 1)
        first_q, first_k = first_half(block), first_half(size)
        ones = jnp.ones((size, PAIR), jnp.bfloat16)

        def pair(p, logs):
            cols = pl.ds(pl.multiple_of(p * PAIR, PAIR), PAIR)
            q, k, v = q_ref[:, cols], k_ref[near, cols], v_ref[near, cols]
            hotq, hotk = hotq_ref[...], hotk_ref[near, :]
            outs = []
            for half in range(2):
                scores = dot(either(first_q, q, hotq, half), either(first_k, k, hotk, half), NT)
                top = jnp.max(scores, axis=1, keepdims=True) * scale
                raised = to_low(jnp.exp2(scores * scale - top))
                result = dot(raised, either(first_k, v, ones, half))
                spare = HD * (1 - half)
                total = result[:, spare : spare + 1]
                outs.append(result * (1.0 / total))
                logs = jnp.where(lane == 2 * p + half, top + jnp.log2(total), logs)
            out_ref[:, cols] = to_low(jnp.where(first_q, outs[0], outs[1]))
            return logs

        empty = jnp.zeros((block, PAIR), jnp.float32)
        log_ref[...] = lax.fori_loop(0, pairs, pair, empty, unroll=unroll)

    windows(span_ref, block, chunk, count, body)

    @pl.when(step == 0)
    def _():
        for copy, wide, low in zip(copies(zip(sources, wides), in_sems), wides, lows):
            copy.wait()
            low[...] = to_low(wide[...])
        for copy in copies(zip(lows, results), out_sems):
            copy.start()

    @pl.when(step == pl.num_programs(0) - 1)
    def _():
        for copy in copies(zip(lows, results), out_sems):
            copy.wait()


def attend(span, query, key, value, hotq, hotk, casts, block, chunk, unroll):
    count, width = query.shape
    whole = lambda w: pl.BlockSpec((count, w), lambda i, *_: (0, 0))
    part = lambda w: pl.BlockSpec((block, w), lambda i, *_: (i, 0))
    anywhere = [pl.BlockSpec(memory_space=pl.ANY)] * len(casts)
    shape = jax.ShapeDtypeStruct
    return pl.pallas_call(
        functools.partial(forward_kernel, len(casts), width // PAIR, chunk, unroll),
        grid_spec=pltpu.PrefetchScalarGridSpec(
            num_scalar_prefetch=1,
            grid=(count // block,),
            in_specs=[part(width), whole(width), whole(width), part(PAIR), whole(PAIR)] + anywhere,
            out_specs=[part(width), part(PAIR)] + anywhere,
            scratch_shapes=[pltpu.VMEM(x.shape, jnp.float32) for x in casts]
            + [pltpu.VMEM(x.shape, jnp.bfloat16) for x in casts]
            + [pltpu.SemaphoreType.DMA((len(casts),))] * 2,
        ),
        out_shape=[shape((count, width), jnp.bfloat16), shape((count, PAIR), jnp.float32)]
        + [shape(x.shape, jnp.bfloat16) for x in casts],
        cost_estimate=small_cost,
        compiler_params=pltpu.CompilerParams(vmem_limit_bytes=62 << 20),
    )(span, query, key, value, hotq, hotk, *casts)


def thirds(values):
    high = to_low(values)
    rest = values - high.astype(jnp.float32)
    middle = to_low(rest)
    return high, middle, to_low(rest - middle.astype(jnp.float32))


def backward_kernel(
    kinds,
    pairs,
    chunk,
    unroll,
    piece,
    span_ref,
    q_ref,
    k_ref,
    v_ref,
    g_ref,
    o_ref,
    hotq_ref,
    hotk_ref,
    log_ref,
    *refs,
):
    dq_ref, dk_ref, dv_ref, sums_ref, dk_sum, dv_sum = refs[-6:]
    block = q_ref.shape[0]
    count = k_ref.shape[0]
    scale = HD**-0.5 * log2e

    @pl.when(pl.program_id(0) == 0)
    def _():
        dk_sum[...] = jnp.zeros_like(dk_sum)
        dv_sum[...] = jnp.zeros_like(dv_sum)
        sums_ref[...] = jnp.zeros_like(sums_ref)

    def body(at, size):
        near = pl.ds(at, size)
        lane = lax.broadcasted_iota(jnp.int32, (block, PAIR), 1)
        first_q, first_k = first_half(block), first_half(size)
        spare = lax.rem(lane, HD) - kinds

        def affine(values, rest):
            for number, part in enumerate(thirds(values)):
                rest = jnp.where(spare == number, part, rest)
            return rest

        def pair(p, _):
            cols = pl.ds(pl.multiple_of(p * PAIR, PAIR), PAIR)
            q, k, v, g = q_ref[:, cols], k_ref[near, cols], v_ref[near, cols], g_ref[:, cols]
            hotq, hotk, logs = hotq_ref[...], hotk_ref[near, :], log_ref[...]
            products = g.astype(jnp.float32) * o_ref[:, cols].astype(jnp.float32)
            zero = jnp.zeros_like(g)
            dqs, dks, dvs = [], [], []
            for half in range(2):
                mine = lane == 2 * (p + piece * pairs) + half
                log = jnp.sum(jnp.where(mine, logs, 0.0), axis=1, keepdims=True)
                inner = jnp.sum(either(first_q, products, 0.0, half), axis=1, keepdims=True)
                qh = either(first_q, q, affine(log * (-1.0 / scale), hotq), half)
                gh = either(first_q, g, affine(-inner, zero), half)
                kh = either(first_k, k, hotk, half)
                vh = either(first_k, v, hotk, half)
                prob = jnp.exp2(dot(qh, kh, NT) * scale)
                d_scores = to_low(prob * dot(gh, vh, NT))
                dqs.append(dot(d_scores, k))
                dks.append(dot(d_scores, q, TN))
                dvs.append(dot(to_low(prob), g, TN))
            dq_ref[:, cols] = to_low(jnp.where(first_q, dqs[0], dqs[1]) * HD**-0.5)
            dk_sum[near, cols] += jnp.where(first_k, dks[0], dks[1])
            dv_sum[near, cols] += jnp.where(first_k, dvs[0], dvs[1])
            return 0

        lax.fori_loop(0, pairs, pair, 0, unroll=unroll)

    windows(span_ref, block, chunk, count, body)
    rounded = dq_ref[...].astype(jnp.float32)
    sums_ref[0] += jnp.sum(rounded.reshape(-1, 8, rounded.shape[1]), axis=0)

    @pl.when(pl.program_id(0) == pl.num_programs(0) - 1)
    def _():
        sums_ref[1] = jnp.sum(dv_sum[...].reshape(-1, 8, dv_sum.shape[1]), axis=0)
        dk_ref[...] = to_low(dk_sum[...] * HD**-0.5)
        dv_ref[...] = to_low(dv_sum[...])


def attend_back(
    span, query, key, value, grad, result, hotq, hotk, logs, kinds, block, chunk, unroll, piece, pieces, after
):
    count = query.shape[0]
    width = query.shape[1] // pieces
    whole = lambda w, j=0: pl.BlockSpec((count, w), lambda i, *_: (0, j))
    part = lambda w, j=0: pl.BlockSpec((block, w), lambda i, *_: (i, j))
    shape = jax.ShapeDtypeStruct
    return pl.pallas_call(
        functools.partial(backward_kernel, kinds, width // PAIR, chunk, unroll, piece),
        grid_spec=pltpu.PrefetchScalarGridSpec(
            num_scalar_prefetch=1,
            grid=(count // block,),
            in_specs=[
                part(width, piece),
                whole(width, piece),
                whole(width, piece),
                part(width, piece),
                part(width, piece),
                part(PAIR),
                whole(PAIR),
                part(PAIR),
            ]
            + [pl.BlockSpec(memory_space=pl.ANY)] * len(after),
            out_specs=[
                part(width),
                whole(width),
                whole(width),
                pl.BlockSpec((2, 8, width), lambda i, *_: (0, 0, 0)),
            ],
            scratch_shapes=[pltpu.VMEM((count, width), jnp.float32)] * 2,
        ),
        out_shape=[shape((count, width), jnp.bfloat16)] * 3 + [shape((2, 8, width), jnp.float32)],
        cost_estimate=small_cost,
        compiler_params=pltpu.CompilerParams(vmem_limit_bytes=62 << 20),
    )(span, query, key, value, grad, result, hotq, hotk, logs, *after)


def rows_of(values):
    return pl.BlockSpec((values.shape[0], values.shape[1]), lambda i, *_: (0, 0))


def gelu_and_slope(values):
    size = jnp.abs(values) * 0.7071067811865476
    near = 1.0 / (1.0 + 0.3275911 * size)
    bell = jnp.exp2(values * values * (-0.5 * log2e))
    poly = near * (
        0.254829592
        + near * (-0.284496736 + near * (1.421413741 + near * (-1.453152027 + near * 1.061405429)))
    )
    tail = 0.5 * poly * bell
    share = jnp.where(values >= 0, 1.0 - tail, tail)
    return values * share, share + values * bell * 0.3989422804014327


def normalize(values):
    center = values - jnp.mean(values, axis=-1, keepdims=True)
    scale = lax.rsqrt(jnp.mean(center * center, axis=-1, keepdims=True) + norm_eps)
    return center * scale, scale


def normalize_back(grad, normed, scale, gain):
    moved = grad * gain
    inner = (
        moved
        - jnp.mean(moved, axis=-1, keepdims=True)
        - normed * jnp.mean(moved * normed, axis=-1, keepdims=True)
    )
    return inner * scale


def feed_forward_kernel(
    parts,
    attended_ref,
    frames_ref,
    out_ref,
    up_ref,
    down_ref,
    final_ref,
    *refs,
):
    vectors, up_bias_ref, final_bias_ref = refs[:6], refs[6], refs[7]
    (
        hidden_turned_ref,
        normed_one_ref,
        active_ref,
        slope_ref,
        normed_two_ref,
        output_turned_ref,
        scales_ref,
        unit_ref,
        unit_scale_ref,
    ) = refs[8:]
    vector = lambda row: vectors[row][...].reshape(1, -1)
    resid = frames_ref[...] + dot(attended_ref[...], out_ref[...]) + vector(0)
    normed, scale_one = normalize(resid)
    normed_one_ref[...] = to_low(normed)
    hidden = normed * vector(1) + vector(2)
    hidden_low = to_low(hidden)
    hidden_turned_ref[...] = hidden_low.T
    second = hidden + vector(3)
    chunk = up_ref.shape[1] // parts
    for part in range(parts):
        at = pl.ds(part * chunk, chunk)
        upper = dot(hidden_low, up_ref[:, at]) + up_bias_ref[at].reshape(1, -1)
        active, slope = gelu_and_slope(upper)
        active = to_low(active)
        active_ref[:, at] = active
        slope_ref[:, at] = to_low(slope)
        second = second + dot(active, down_ref[at, :])
    normed, scale_two = normalize(second)
    normed_two_ref[...] = to_low(normed)
    output_low = to_low(normed * vector(4) + vector(5))
    output_turned_ref[...] = output_low.T
    final = dot(output_low, final_ref[...]) + final_bias_ref[...].reshape(1, -1)
    turned = final.T
    unit_scale = lax.rsqrt(jnp.sum(turned * turned, axis=0, keepdims=True) + cosine_eps)
    unit_ref[...] = turned * unit_scale
    unit_scale_ref[...] = jnp.broadcast_to(unit_scale, unit_scale_ref.shape)
    lane = lax.broadcasted_iota(jnp.int32, scales_ref.shape, 1)
    scales_ref[...] = jnp.where(lane == 0, scale_one, scale_two)


def feed_forward(attended, frames, out, up, down, final, vectors, block):
    count, model = frames.shape
    inner, width = up.shape[1], final.shape[1]
    part = lambda columns: pl.BlockSpec((block, columns), lambda i: (i, 0))
    turned = lambda rows: pl.BlockSpec((rows, block), lambda i: (0, i))
    shape = jax.ShapeDtypeStruct
    low, full = jnp.bfloat16, jnp.float32
    operands = (attended, frames, out, up, down, final)
    return pl.pallas_call(
        functools.partial(feed_forward_kernel, max(inner // model, 1)),
        grid=(count // block,),
        in_specs=[part(model), part(model)]
        + [rows_of(x) for x in operands[2:]]
        + [vector_spec(x) for x in vectors],
        out_specs=[turned(model), part(model), part(inner), part(inner), part(model), turned(model), part(PAIR)]
        + [turned(width), turned(8)],
        out_shape=[
            shape((model, count), low),
            shape((count, model), low),
            shape((count, inner), low),
            shape((count, inner), low),
            shape((count, model), low),
            shape((model, count), low),
            shape((count, PAIR), full),
            shape((width, count), full),
            shape((8, count), full),
        ],
        cost_estimate=small_cost,
        compiler_params=pltpu.CompilerParams(vmem_limit_bytes=62 << 20),
    )(*operands, *vectors)


def feed_forward_back_kernel(
    parts,
    d_final_ref,
    slope_ref,
    normed_one_ref,
    normed_two_ref,
    scales_ref,
    final_ref,
    up_ref,
    down_ref,
    out_ref,
    gain_one_ref,
    gain_two_ref,
    down_turned_ref,
    upper_low_ref,
    resid_ref,
    branch_low_ref,
    attended_low_ref,
    sums_ref,
    up_sums_ref,
    final_sums_ref,
):
    @pl.when(pl.program_id(0) == 0)
    def _():
        sums_ref[...] = jnp.zeros_like(sums_ref)
        up_sums_ref[...] = jnp.zeros_like(up_sums_ref)
        final_sums_ref[...] = jnp.zeros_like(final_sums_ref)

    def add(row, values):
        sums_ref[row] += jnp.sum(values.reshape(-1, 8, values.shape[1]), axis=0)

    d_final = d_final_ref[...]
    final_sums_ref[...] += jnp.sum(d_final.astype(jnp.float32).reshape(-1, 8, d_final.shape[1]), axis=0)
    grad = dot(d_final, final_ref[...], NT)
    normed = normed_two_ref[...].astype(jnp.float32)
    gain = gain_two_ref[...].reshape(1, -1)
    hidden = normalize_back(grad, normed, scales_ref[:, 1:2], gain)
    down_low = to_low(hidden)
    down_turned_ref[...] = down_low.T
    add(0, grad * normed)
    add(1, grad)
    add(2, down_low.astype(jnp.float32))
    chunk = up_ref.shape[1] // parts
    for part in range(parts):
        at = pl.ds(part * chunk, chunk)
        upper = dot(down_low, down_ref[at, :], NT) * slope_ref[:, at].astype(jnp.float32)
        upper_low = to_low(upper)
        upper_low_ref[:, at] = upper_low
        up_sums_ref[:, at] += jnp.sum(upper.reshape(-1, 8, chunk), axis=0)
        hidden = hidden + dot(upper_low, up_ref[:, at], NT)
    normed = normed_one_ref[...].astype(jnp.float32)
    gain = gain_one_ref[...].reshape(1, -1)
    resid = normalize_back(hidden, normed, scales_ref[:, 0:1], gain)
    resid_ref[...] = resid
    branch_low = to_low(resid)
    branch_low_ref[...] = branch_low
    attended_low_ref[...] = to_low(dot(branch_low, out_ref[...], NT))
    add(3, hidden * normed)
    add(4, hidden)
    add(5, branch_low.astype(jnp.float32))


def feed_forward_back(d_final, slope, normed_one, normed_two, scales, final, up, down, out, gains, block):
    count, model = normed_one.shape
    inner = up.shape[1]
    part = lambda columns: pl.BlockSpec((block, columns), lambda i: (i, 0))
    shape = jax.ShapeDtypeStruct
    low, full = jnp.bfloat16, jnp.float32
    return pl.pallas_call(
        functools.partial(feed_forward_back_kernel, max(inner // model, 1)),
        grid=(count // block,),
        in_specs=[part(d_final.shape[1]), part(inner), part(model), part(model), part(PAIR)]
        + [rows_of(x) for x in (final, up, down, out)]
        + [vector_spec(x) for x in gains],
        out_specs=[pl.BlockSpec((model, block), lambda i: (0, i))]
        + [part(inner), part(model), part(model), part(model)]
        + [
            pl.BlockSpec((6, 8, model), lambda i: (0, 0, 0)),
            pl.BlockSpec((8, inner), lambda i: (0, 0)),
            pl.BlockSpec((8, d_final.shape[1]), lambda i: (0, 0)),
        ],
        out_shape=[
            shape((model, count), low),
            shape((count, inner), low),
            shape((count, model), full),
            shape((count, model), low),
            shape((count, model), low),
            shape((6, 8, model), full),
            shape((8, inner), full),
            shape((8, d_final.shape[1]), full),
        ],
        cost_estimate=small_cost,
        compiler_params=pltpu.CompilerParams(vmem_limit_bytes=62 << 20),
    )(d_final, slope, normed_one, normed_two, scales, final, up, down, out, *gains)


def candidate_kernel(
    slots, owners, keep, index_ref, rows_ref, unit_ref, scale_ref, positive_ref, masked_ref,
    loss_ref, final_low_ref, positive_part_ref, rows_grad_ref,
    packed, mass, pull, total, unit_low, weighted,
):
    step = pl.program_id(0)
    frames = unit_ref.shape[1]
    own = rows_ref.shape[0]
    lanes = 128
    words = lax.broadcasted_iota(jnp.int32, (128, lanes), 0)

    def fill(at_mass):
        def count(tile, _):
            at = pl.ds(pl.multiple_of(tile * lanes, lanes), lanes)
            acc = jnp.zeros((128, lanes), jnp.int32)
            for slot in range(slots):
                index = index_ref[0, pl.ds(slot, 1), at]
                low = jnp.bitwise_and(index, 127)
                unit = jnp.where(index >= 0, jnp.left_shift(1, 4 * jnp.right_shift(index, 7)), 0)
                acc = acc + jnp.where(words == low, unit, 0)
            packed[:, at] = acc
            return 0

        lax.fori_loop(0, frames // lanes, count, 0)

        wide = 4

        def part(number, _):
            first = number * (128 * wide)
            at = pl.ds(pl.multiple_of(first, 128 * wide), 128 * wide)
            cosines = dot(rows_ref[at, :], unit_low[...])
            for piece in range(wide):
                cosine = cosines[piece * 128 : (piece + 1) * 128]
                shift = 4 * (number * wide + piece)
                times = jnp.bitwise_and(lax.shift_right_logical(packed[...], shift), 15)
                value = times.astype(jnp.float32) * jnp.exp2(cosine)
                total[...] += jnp.sum(value.reshape(16, 8, frames), axis=0)
                low = pl.multiple_of(at_mass + first + piece * 128, 128)
                mass[pl.ds(low, 128), :] = to_low(value)
            return 0

        lax.fori_loop(0, own // (128 * wide), part, 0, unroll=1)

    @pl.when(step == 0)
    def _():
        unit_low[...] = to_low(unit_ref[...])
        total[...] = jnp.zeros_like(total)
        pull[...] = jnp.zeros_like(pull)

    @pl.when(step < owners)
    def _():
        at_mass = step * own if keep else 0
        fill(at_mass)
        pull[...] += dot(rows_ref[...], mass[pl.ds(pl.multiple_of(at_mass, own), own), :], TN)

    @pl.when(step == owners - 1)
    def _():
        score_scale = log2e / similarity_softening_factor
        unit, positive, masked = unit_ref[...], positive_ref[...], masked_ref[...]
        mass_sum = jnp.sum(total[...], axis=0, keepdims=True)
        score = jnp.sum(unit * positive, axis=0, keepdims=True) * (1.0 / similarity_softening_factor)
        whole = jnp.exp(score) + mass_sum
        loss_ref[...] = (masked * (jnp.log(whole) - score))[0]
        weight = masked / whole * (1.0 / similarity_softening_factor)
        d_score = -weight * mass_sum
        d_unit = d_score * positive + weight * (1.0 / score_scale) * pull[...]
        inner = jnp.sum(d_unit * unit, axis=0, keepdims=True)
        final_low_ref[...] = to_low((scale_ref[0:1, :] * (d_unit - unit * inner)).T)
        positive_part_ref[...] = (d_score * unit).T
        weighted[...] = to_low((weight * unit).T)

    @pl.when(step >= owners)
    def _():
        at_mass = (step - owners) * own if keep else 0
        if not keep:
            fill(at_mass)
        rows_grad_ref[...] = to_low(dot(mass[pl.ds(pl.multiple_of(at_mass, own), own), :], weighted[...]))


def candidates(index, rows, unit, scale, positive, masked):
    owners, slots, frames = index.shape
    width = rows.shape[1]
    own = rows.shape[0] // owners
    keep = rows.shape[0] * frames * 2 <= 16 << 20
    again = (lambda i: jnp.minimum(i, owners - 1)) if keep else (lambda i: lax.rem(i, owners))
    shape = jax.ShapeDtypeStruct
    return pl.pallas_call(
        functools.partial(candidate_kernel, slots, owners, keep),
        grid=(2 * owners,),
        in_specs=[
            pl.BlockSpec((1, slots, frames), lambda i: (again(i), 0, 0)),
            pl.BlockSpec((own, width), lambda i: (again(i), 0)),
            rows_of(unit),
            rows_of(scale),
            rows_of(positive),
            rows_of(masked),
        ],
        out_specs=[
            pl.BlockSpec((frames,), lambda i: (0,)),
            pl.BlockSpec((frames, width), lambda i: (0, 0)),
            pl.BlockSpec((frames, width), lambda i: (0, 0)),
            pl.BlockSpec((own, width), lambda i: (jnp.maximum(i - owners, 0), 0)),
        ],
        out_shape=[
            shape((frames,), jnp.float32),
            shape((frames, width), jnp.bfloat16),
            shape((frames, width), jnp.float32),
            shape((rows.shape[0], width), jnp.bfloat16),
        ],
        scratch_shapes=[
            pltpu.VMEM((128, frames), jnp.int32),
            pltpu.VMEM((rows.shape[0] if keep else own, frames), jnp.bfloat16),
            pltpu.VMEM((width, frames), jnp.float32),
            pltpu.VMEM((8, frames), jnp.float32),
            pltpu.VMEM((width, frames), jnp.bfloat16),
            pltpu.VMEM((frames, width), jnp.bfloat16),
        ],
        cost_estimate=small_cost,
        compiler_params=pltpu.CompilerParams(vmem_limit_bytes=62 << 20),
    )(index, rows, unit, scale, positive, masked)


def down_grad_kernel(active_ref, turned_ref, *refs):
    out_ref = refs[-1]
    here, groups, blocks, rows, wide = out_ref.shape
    value = to_low(dot(turned_ref[...], active_ref[...]))
    each = value.shape[0] // groups
    across = value.shape[1] // here // PAIR
    for group in range(groups):
        for tile in range(each // rows * across):
            top = group * each + tile // across * rows
            lanes = pl.ds(tile * PAIR % wide, PAIR)
            for number in range(here):
                low = (number * across + tile % across) * PAIR
                part = value[top : top + rows, low : low + PAIR]
                out_ref[number, group, tile * PAIR // wide, :, lanes] = part


def down_grad(active, turned, members, groups, width, after):
    count, inner = active.shape
    model = turned.shape[0]
    share, rows = inner // members, model // members
    block = (2, groups, model * share // (groups * rows * width), rows, width)
    return pl.pallas_call(
        down_grad_kernel,
        grid=(members // 2,),
        in_specs=[pl.BlockSpec((count, 2 * share), lambda i: (0, i)), rows_of(turned)]
        + [pl.BlockSpec(memory_space=pl.ANY)] * len(after),
        out_specs=pl.BlockSpec(block, lambda i: (i, 0, 0, 0, 0)),
        out_shape=jax.ShapeDtypeStruct((members, *block[1:]), jnp.bfloat16),
        cost_estimate=small_cost,
        compiler_params=pltpu.CompilerParams(vmem_limit_bytes=62 << 20),
    )(active, turned, *after)


def up_grad_kernel(
    groups, core_ref, hidden_ref, upper_ref, attended_ref, branch_ref, output_ref, final_ref, *refs
):
    kept_ref, sent_ref, attended_turned, held = refs[-4:]
    group = pl.program_id(0)
    core = core_ref[0]
    lines, share = kept_ref.shape[1], kept_ref.shape[2]

    @pl.when(group == 0)
    def _():
        attended_turned[...] = attended_ref[...].T

    wide = upper_ref.shape[1]
    side = final_ref.shape[1]
    held[:, :, :, :wide] = to_low(dot(hidden_ref[...], upper_ref[...])).reshape(lines, 2, share, wide)

    @pl.when(group < groups - 1)
    def _():
        value = dot(attended_turned[...], branch_ref[...])
        held[:, :, :, wide:] = to_low(value).reshape(lines, 2, share, side)

    @pl.when(group == groups - 1)
    def _():
        value = dot(output_ref[...], final_ref[...])
        held[:, :, :, wide:] = to_low(value).reshape(lines, 2, share, side)

    kept_ref[0] = held[:, core]
    sent_ref[0] = held[:, 1 - core]


def up_grad(core, hidden, upper, attended, branch, output, final, members, groups, after):
    model, count = hidden.shape
    wide, side = upper.shape[1] // groups, final.shape[1]
    lines, share = members // 2, model // members
    whole = lambda columns: pl.BlockSpec((count, columns), lambda g, core: (0, 0))
    out = pl.BlockSpec((1, lines, share, wide + side), lambda g, core: (g, 0, 0, 0))
    shape = jax.ShapeDtypeStruct((groups, lines, share, wide + side), jnp.bfloat16)
    last = model // side - 1
    return pl.pallas_call(
        functools.partial(up_grad_kernel, groups),
        grid_spec=pltpu.PrefetchScalarGridSpec(
            num_scalar_prefetch=1,
            grid=(groups,),
            in_specs=[
                rows_of(hidden),
                pl.BlockSpec((count, wide), lambda g, core: (0, g)),
                whole(model),
                pl.BlockSpec((count, side), lambda g, core: (0, jnp.minimum(g, last))),
                rows_of(output),
                whole(side),
            ]
            + [pl.BlockSpec(memory_space=pl.ANY)] * len(after),
            out_specs=[out, out],
            scratch_shapes=[
                pltpu.VMEM((model, count), jnp.bfloat16),
                pltpu.VMEM((lines, 2, share, wide + side), jnp.bfloat16),
            ],
        ),
        out_shape=[shape, shape],
        cost_estimate=small_cost,
        compiler_params=pltpu.CompilerParams(vmem_limit_bytes=62 << 20),
    )(core, hidden, upper, attended, branch, output, final, *after)


def projection_grad_kernel(grads, pieces, core_ref, frames_ref, *refs):
    kept_ref, sent_ref, held = refs[-3:]
    core = core_ref[0]
    turned = frames_ref[...].T
    each = kept_ref.shape[3] // PAIR
    lines, share = kept_ref.shape[1], kept_ref.shape[2]
    members = 2 * lines

    def put(number):
        for column in range(held.shape[3] // PAIR):
            tile = number * (held.shape[3] // PAIR) + column
            group, lanes = tile // each, pl.ds(tile % each * PAIR, PAIR)
            at = pl.ds(column * PAIR, PAIR)
            kept_ref[group, :, :, lanes] = held[:, core, :, at]
            sent_ref[group, :, :, lanes] = held[:, 1 - core, :, at]

    for number, ref in enumerate(refs[:grads]):
        held[...] = to_low(dot(turned, ref[...])).reshape(held.shape)
        put(number)
    if len(refs) == grads + 3:
        return
    piece_refs = refs[grads : grads + pieces]
    model_ref, up_ref, final_ref, target_ref, square_ref = refs[grads + pieces : -3]

    def total(values):
        return jnp.sum(values, axis=0, keepdims=True)

    vectors = (
        jnp.concatenate([total(ref[0]) for ref in piece_refs], axis=1),
        jnp.concatenate([total(ref[1]) for ref in piece_refs], axis=1),
        total(model_ref[5]),
        total(model_ref[3]),
        total(model_ref[4]),
        total(up_ref[...]),
        total(model_ref[2]),
        total(model_ref[0]),
        total(model_ref[1]),
        total(final_ref[...]),
        total(target_ref[...]),
    )
    square = square_ref[...]
    rows = square.shape[0] // members
    held[...] = jnp.zeros_like(held)
    for member in range(members):
        line, side = member // 2, member % 2
        parts = []
        for vector in vectors:
            size = vector.shape[1] // members
            for low in range(member * size, (member + 1) * size, PAIR):
                part = vector[:, low : min(low + PAIR, (member + 1) * size)]
                parts.append(jnp.pad(part, ((0, 0), (0, PAIR - part.shape[1]))))
        parts.append(jnp.zeros((share - len(parts), PAIR), jnp.float32))
        held[line, side, :, :PAIR] = to_low(jnp.concatenate(parts, axis=0))
        own = square[member * rows : (member + 1) * rows]
        for half in range(square.shape[1] // PAIR):
            part = own[:, half * PAIR : (half + 1) * PAIR]
            held[line, side, half * rows : (half + 1) * rows, PAIR:] = to_low(part)
    put(grads)


def projection_grad(core, frames, grads, pieces, sums, members, groups, after):
    count, model = frames.shape
    lines, share = members // 2, model // members
    width = grads[0].shape[1]
    wide = (len(grads) + bool(sums)) * width // groups
    shape = jax.ShapeDtypeStruct((groups, lines, share, wide), jnp.bfloat16)
    vmem = pl.BlockSpec(memory_space=pltpu.VMEM)

    def kernel(*refs):
        used = 2 + len(grads) + len(pieces) + len(sums)
        projection_grad_kernel(len(grads), len(pieces), *refs[:used], *refs[used + len(after) :])

    return pl.pallas_call(
        kernel,
        in_specs=[pl.BlockSpec(memory_space=pltpu.SMEM)]
        + [vmem] * (1 + len(grads) + len(pieces) + len(sums))
        + [pl.BlockSpec(memory_space=pl.ANY)] * len(after),
        out_specs=[vmem, vmem],
        out_shape=[shape, shape],
        scratch_shapes=[pltpu.VMEM((lines, 2, share, width), jnp.bfloat16)],
        cost_estimate=small_cost,
        compiler_params=pltpu.CompilerParams(vmem_limit_bytes=62 << 20),
    )(core, frames, *grads, *pieces, *sums, *after)


def slot_rows(distractors, members):
    count, slots = distractors.shape
    turns = -(-slots // members)
    padded = jnp.pad(distractors, ((0, 0), (0, turns * members - slots)), constant_values=-1)
    padded = padded.T.reshape(turns, members, count)
    period = members // math.gcd(slots, members)
    frame = jnp.arange(count, dtype=jnp.int32) % period
    placed = padded
    for phase in range(1, period):
        turned = jnp.roll(padded, phase * slots % members, axis=1)
        placed = jnp.where(frame == phase, turned, placed)
    return placed.transpose(1, 0, 2)


def target_kernel(came_ref, part_ref, unit_ref, scale_ref, low_ref, matrix_ref, *refs):
    grad_ref, matrix_grad_ref, sums_ref = refs[-3:]
    grad_unit = part_ref[...] + came_ref[...].astype(jnp.float32)
    unit = unit_ref[...]
    inner = jnp.sum(grad_unit * unit, axis=-1, keepdims=True)
    low = to_low(scale_ref[:, 0:1] * (grad_unit - unit * inner))
    grad_ref[...] = dot(low, to_low(matrix_ref[...]), NT)
    matrix_grad_ref[...] = dot(to_low(low_ref[...]), low, TN)
    sums_ref[...] = jnp.sum(low.astype(jnp.float32).reshape(-1, 8, low.shape[1]), axis=0)


def target_back(came, part, unit, scale, low, matrix, after):
    count, width = part.shape
    vmem = pl.BlockSpec(memory_space=pltpu.VMEM)
    shape = jax.ShapeDtypeStruct
    return pl.pallas_call(
        target_kernel,
        in_specs=[vmem] * 6 + [pl.BlockSpec(memory_space=pl.ANY)] * len(after),
        out_specs=[vmem] * 3,
        out_shape=[
            shape((count, width), jnp.float32),
            shape((width, width), jnp.float32),
            shape((8, width), jnp.float32),
        ],
        cost_estimate=small_cost,
        compiler_params=pltpu.CompilerParams(vmem_limit_bytes=62 << 20),
    )(came, part, unit, scale, low, matrix, *after)


def inputs_kernel(parts, resid_ref, *refs):
    out_ref = refs[-1]
    total = resid_ref[...]
    for matrix in range(3):
        low = 0
        for part in range(parts):
            grad_ref = refs[matrix * parts + part]
            high = low + grad_ref.shape[1]
            total = total + dot(grad_ref[...], refs[3 * parts + matrix][:, low:high], NT)
            low = high
    out_ref[...] = total


def inputs_back(resid, grads, matrices, block, after):
    count, model = resid.shape
    part = lambda x: pl.BlockSpec((block, x.shape[1]), lambda i: (i, 0))
    flat = [g for parts in grads for g in parts]
    return pl.pallas_call(
        functools.partial(inputs_kernel, len(grads[0])),
        grid=(count // block,),
        in_specs=[part(resid)]
        + [part(g) for g in flat]
        + [rows_of(m) for m in matrices]
        + [pl.BlockSpec(memory_space=pl.ANY)] * len(after),
        out_specs=part(resid),
        out_shape=jax.ShapeDtypeStruct(resid.shape, jnp.float32),
        cost_estimate=small_cost,
        compiler_params=pltpu.CompilerParams(vmem_limit_bytes=62 << 20),
    )(resid, *flat, *matrices, *after)


def prepare_kernel(
    blocks, chunks, lengths_ref, starts_ref, targets_ref, matrix_ref, bias_ref, *refs
):
    rows_ref, unit_ref, turned_ref, scale_ref, hot_query_ref, hot_key_ref, masked_ref = refs[:7]
    low = to_low(dot(to_low(targets_ref[...]), to_low(matrix_ref[...])) + bias_ref[...].reshape(1, -1))
    positive = low.astype(jnp.float32)
    scale = lax.rsqrt(jnp.sum(positive * positive, axis=-1, keepdims=True) + cosine_eps)
    unit = positive * scale
    rows_ref[...] = to_low(unit * (log2e / similarity_softening_factor))
    unit_ref[...] = unit
    turned_ref[...] = unit.T
    scale_ref[...] = jnp.broadcast_to(scale, scale_ref.shape)

    count = targets_ref.shape[0]
    kinds = lengths_ref.shape[1]
    bounds = [jnp.int32(0)]
    for kind in range(kinds):
        bounds.append(bounds[-1] + lengths_ref[0, kind])
    for span_ref, block, chunk in zip(refs[7:], blocks, chunks):
        for number in range(count // block):
            first, last = number * block, (number + 1) * block - 1
            begin, end = jnp.int32(0), jnp.int32(count)
            for kind in range(kinds):
                begin = jnp.where(bounds[kind] <= first, jnp.maximum(begin, bounds[kind]), begin)
                end = jnp.where(bounds[kind + 1] > last, jnp.minimum(end, bounds[kind + 1]), end)
            begin = lax.div(begin, chunk)
            span_ref[0, number] = begin
            span_ref[1, number] = lax.div(end + (chunk - 1), chunk) - begin

    row = lax.broadcasted_iota(jnp.int32, hot_query_ref.shape, 0)
    lane = lax.rem(lax.broadcasted_iota(jnp.int32, hot_query_ref.shape, 1), HD)
    same = jnp.zeros(hot_query_ref.shape, jnp.float32)
    for kind in range(kinds):
        inside = (row >= bounds[kind]) & (row < bounds[kind + 1]) & (lane == kind)
        same = jnp.where(inside, 1.0, same)
    hot_query_ref[...] = to_low(jnp.where(lane < kinds, 1e30 * (1.0 - same), 0.0))
    spare = (lane >= kinds) & (lane < kinds + 3)
    hot_key_ref[...] = to_low(jnp.where(spare, 1.0, -same))

    place = lax.broadcasted_iota(jnp.int32, masked_ref.shape, 1)
    age = place
    for kind in range(1, kinds):
        age = jnp.where(place >= bounds[kind], place - bounds[kind], age)
    starts = starts_ref[...].astype(jnp.float32)
    covered = starts
    for offset in range(1, SPAN):
        earlier = pltpu.roll(starts, offset, 1)
        covered = jnp.maximum(covered, jnp.where(age >= offset, earlier, 0.0))
    masked_ref[...] = covered


def prepare(lengths, starts, targets, matrix, bias, blocks, chunks):
    count, width = targets.shape
    vmem = pl.BlockSpec(memory_space=pltpu.VMEM)
    smem = pl.BlockSpec(memory_space=pltpu.SMEM)
    shape = jax.ShapeDtypeStruct
    return pl.pallas_call(
        functools.partial(prepare_kernel, blocks, chunks),
        in_specs=[smem] + [vmem] * 4,
        out_specs=[vmem] * 7 + [smem] * len(blocks),
        out_shape=[
            shape((count, width), jnp.bfloat16),
            shape((count, width), jnp.float32),
            shape((width, count), jnp.float32),
            shape((count, PAIR), jnp.float32),
            shape((count, PAIR), jnp.bfloat16),
            shape((count, PAIR), jnp.bfloat16),
            shape((1, count), jnp.float32),
        ]
        + [shape((2, count // block), jnp.int32) for block in blocks],
        cost_estimate=small_cost,
        compiler_params=pltpu.CompilerParams(vmem_limit_bytes=62 << 20),
    )(lengths, starts[None], targets, matrix, bias)


def project_kernel(frames_ref, wq_ref, wk_ref, wv_ref, bq_ref, bv_ref, *refs):
    low_ref, q_ref, k_ref, v_ref, mq, mk, mv = refs[-7:]


    @pl.when(pl.program_id(0) == 0)
    def _():
        mq[...] = to_low(wq_ref[...])
        mk[...] = to_low(wk_ref[...])
        mv[...] = to_low(wv_ref[...])

    low = to_low(frames_ref[...])
    low_ref[...] = low
    q_ref[...] = to_low(dot(low, mq[...]) + bq_ref[...].reshape(1, -1))
    k_ref[...] = to_low(dot(low, mk[...]))
    v_ref[...] = to_low(dot(low, mv[...]) + bv_ref[...].reshape(1, -1))


def vector_spec(values):
    return pl.BlockSpec(values.shape, lambda i, *_: (0,))


def project(frames, w_query, w_key, w_value, b_query, b_value, block, after):
    count, model = frames.shape
    part = pl.BlockSpec((block, model), lambda i: (i, 0))
    return pl.pallas_call(
        project_kernel,
        grid=(count // block,),
        in_specs=[part]
        + [rows_of(w) for w in (w_query, w_key, w_value)]
        + [vector_spec(b) for b in (b_query, b_value)]
        + [pl.BlockSpec(memory_space=pl.ANY)] * len(after),
        out_specs=[part] * 4 + [rows_of(w_query)] * 3,
        out_shape=[jax.ShapeDtypeStruct((count, model), jnp.bfloat16)] * 4
        + [jax.ShapeDtypeStruct((model, model), jnp.bfloat16)] * 3,
        cost_estimate=small_cost,
        compiler_params=pltpu.CompilerParams(vmem_limit_bytes=62 << 20),
    )(frames, w_query, w_key, w_value, b_query, b_value, *after)


def exchange(sent):
    members = lax.axis_size("tm")
    return lax.ppermute(sent, "tm", [(i, i ^ 1) for i in range(members)])


def split_kernel(counts, pieces, choice_ref, *refs):
    out_refs = refs[-pieces:]
    number, low, lanes = 0, 0, 0
    for count in counts:
        if count < 3:
            total = sum((refs[number + term][0] for term in range(1, count)), refs[number][0])
        else:
            total = to_low(sum(refs[number + term][0].astype(jnp.float32) for term in range(count)))
        high = lanes + total.shape[-1]
        for piece in range(pieces):

            @pl.when(pl.program_id(0) == piece)
            def _(piece=piece, total=total, low=low, lanes=lanes, high=high):
                if total.ndim == 3:
                    out_refs[piece][low : low + total.shape[0]] = total
                else:
                    out_refs[piece][:, lanes:high] = total

        number, low, lanes = number + count, low + total.shape[0], high


def split_sum(choice, sums, pieces, after):
    terms = [term for group in sums for term in group]
    first = [group[0].shape[1:] for group in sums]
    if len(first[0]) == 3:
        rest = (sum(shape[0] for shape in first), *first[0][1:])
    else:
        rest = (first[0][0], sum(shape[1] for shape in first))

    def source(term):
        zeros = (0,) * (term.ndim - 1)
        return pl.BlockSpec((1, *term.shape[1:]), lambda i, choice: (choice[0] ^ i, *zeros))

    return pl.pallas_call(
        functools.partial(split_kernel, [len(group) for group in sums], pieces),
        grid_spec=pltpu.PrefetchScalarGridSpec(
            num_scalar_prefetch=1,
            grid=(pieces,),
            in_specs=[source(term) for term in terms]
            + [pl.BlockSpec(memory_space=pl.ANY)] * len(after),
            out_specs=[pl.BlockSpec(rest, lambda i, choice: (0,) * len(rest))] * pieces,
        ),
        out_shape=[jax.ShapeDtypeStruct(rest, jnp.bfloat16)] * pieces,
        cost_estimate=small_cost,
        compiler_params=pltpu.CompilerParams(vmem_limit_bytes=62 << 20),
    )(choice, *terms, *after)


def swap(pieces, axis="grp", stride=1):
    size = lax.axis_size(axis)
    return [pieces[0]] + [
        lax.ppermute(piece, axis, [(i, i ^ (k * stride)) for i in range(size)])
        for k, piece in enumerate(pieces)
        if k
    ]


def line_kernel(terms, *refs):
    total = refs[0][...].astype(jnp.float32)
    for term in range(1, terms):
        total = total + refs[term][...].astype(jnp.float32)
    refs[-1][...] = to_low(total)


def line_sum(terms, after):
    lines, rest = terms[0].shape[0], terms[0].shape[1:]
    block = pl.BlockSpec((lines // 2, *rest), lambda i: (i, *(0,) * len(rest)))
    return pl.pallas_call(
        functools.partial(line_kernel, len(terms)),
        grid=(2,),
        in_specs=[block] * len(terms) + [pl.BlockSpec(memory_space=pl.ANY)] * len(after),
        out_specs=block,
        out_shape=jax.ShapeDtypeStruct(terms[0].shape, jnp.bfloat16),
        cost_estimate=large_cost,
        compiler_params=pltpu.CompilerParams(vmem_limit_bytes=62 << 20),
    )(*terms, *after)


def chip_lines():
    return [list(range(first, lax.axis_size("tm"), 2)) for first in range(2)]


def scatter(value, axis, among=None):
    return lax.psum_scatter(value, axis, scatter_dimension=0, axis_index_groups=among)


def share_kernel(terms, start, *refs):
    out_ref, share_ref = refs[-1], refs[terms]
    wide = refs[0].shape[2]
    for copy in range(out_ref.shape[0]):
        low = 0
        for at in range(start, refs[0].shape[0]):
            total = sum(ref[at].astype(jnp.float32) for ref in refs[:terms])
            out_ref[copy, :, low : low + wide] = to_low(total)
            low += wide
        out_ref[copy, :, low:] = share_ref[...]


def shares(terms, start, share, groups, after):
    blocks, rows, wide = terms[0].shape
    wide = (blocks - start) * wide + share.shape[1]
    vmem = pl.BlockSpec(memory_space=pltpu.VMEM)
    return pl.pallas_call(
        functools.partial(share_kernel, len(terms), start),
        in_specs=[vmem] * (len(terms) + 1) + [pl.BlockSpec(memory_space=pl.ANY)] * len(after),
        out_specs=vmem,
        out_shape=jax.ShapeDtypeStruct((groups, rows, wide), jnp.bfloat16),
        cost_estimate=small_cost,
        compiler_params=pltpu.CompilerParams(vmem_limit_bytes=62 << 20),
    )(*terms, share, *after)


def place(kernel, arrays, shapes, after, choice=None):
    vmem = pl.BlockSpec(memory_space=pltpu.VMEM)
    first = [] if choice is None else [choice]
    used = len(first) + len(arrays)
    return pl.pallas_call(
        lambda *refs: kernel(*refs[:used], *refs[used + len(after) :]),
        in_specs=[pl.BlockSpec(memory_space=pltpu.SMEM)] * len(first)
        + [vmem] * len(arrays)
        + [pl.BlockSpec(memory_space=pl.ANY)] * len(after),
        out_specs=[vmem] * len(shapes),
        out_shape=[jax.ShapeDtypeStruct(s, jnp.float32) for s in shapes],
        cost_estimate=small_cost,
        compiler_params=pltpu.CompilerParams(vmem_limit_bytes=62 << 20),
    )(*first, *arrays, *after)


def line_total(terms, after):
    vmem = pl.BlockSpec(memory_space=pltpu.VMEM)
    return pl.pallas_call(
        functools.partial(line_kernel, len(terms)),
        in_specs=[vmem] * len(terms) + [pl.BlockSpec(memory_space=pl.ANY)] * len(after),
        out_specs=vmem,
        out_shape=jax.ShapeDtypeStruct(terms[0].shape, jnp.bfloat16),
        cost_estimate=small_cost,
        compiler_params=pltpu.CompilerParams(vmem_limit_bytes=62 << 20),
    )(*terms, *after)


def on_device(
    frames,
    targets,
    lengths,
    span_starts,
    distractors,
    w_query,
    b_query,
    w_key,
    w_value,
    b_value,
    w_out,
    b_out,
    norm_gain,
    norm_bias,
    w_up,
    b_up,
    w_down,
    b_down,
    final_gain,
    final_bias,
    w_final,
    b_final,
    w_target,
    b_target,
):
    count, model = frames.shape
    width = targets.shape[1]
    inner = w_up.shape[1]
    members, groups = lax.axis_size("tm"), lax.axis_size("grp")
    block = min(count, 256)
    share = model // members
    place_in_line = lax.axis_index("tm")
    core = (place_in_line % 2)[None].astype(jnp.int32)
    line = (place_in_line // 2)[None].astype(jnp.int32)
    group = lax.axis_index("grp")[None].astype(jnp.int32)

    (
        own_rows,
        positive_unit,
        positive_turned,
        positive_scale,
        hot_query,
        hot_key,
        masked,
        span,
        span_back,
    ) = prepare(
        lengths, span_starts, targets, w_target, b_target, (2 * block, block), (block, block)
    )
    rows = lax.all_gather(own_rows, "tm", tiled=True)
    index = slot_rows(distractors, members)

    frames_low, query, key, value, *own_matrices = project(
        frames, w_query, w_key, w_value, b_query, b_value, block, (own_rows,)
    )
    attended_low, log_total, out_matrix, up_matrix, down_matrix, final_matrix = attend(
        span, query, key, value, hot_query, hot_key, (w_out, w_up, w_down, w_final), 2 * block, block, 2
    )
    (
        hidden_turned,
        normed_one,
        active_low,
        slope,
        normed_two,
        output_turned,
        scales,
        final_unit,
        final_scale,
    ) = feed_forward(
        attended_low,
        frames,
        out_matrix,
        up_matrix,
        down_matrix,
        final_matrix,
        (b_out, norm_gain, norm_bias, b_down, final_gain, final_bias, b_up, b_final),
        block,
    )
    losses, d_final_low, positive_part, d_rows = candidates(
        index, rows, final_unit, final_scale, positive_turned, masked
    )
    came = lax.psum_scatter(d_rows, "tm", scatter_dimension=0, tiled=True)

    (
        d_down_turned,
        d_upper_low,
        d_resid,
        d_branch_low,
        d_attended_low,
        model_sums,
        up_sums,
        final_sums,
    ) = feed_forward_back(
        d_final_low,
        slope,
        normed_one,
        normed_two,
        scales,
        final_matrix,
        up_matrix,
        down_matrix,
        out_matrix,
        (norm_gain, final_gain),
        block,
    )
    def attention_back(piece, pieces, after):
        return attend_back(
            span_back,
            query,
            key,
            value,
            d_attended_low,
            attended_low,
            hot_query,
            hot_key,
            log_total,
            lengths.shape[1],
            block,
            block,
            2,
            piece,
            pieces,
            after,
        )


    def total(values):
        return jnp.sum(values, axis=0)

    def vector_sums(piece_sums, target_sums):
        return (
            jnp.concatenate([total(s[0]) for s in piece_sums]),
            jnp.concatenate([total(s[1]) for s in piece_sums]),
            total(model_sums[5]),
            total(model_sums[3]),
            total(model_sums[4]),
            total(up_sums),
            total(model_sums[2]),
            total(model_sums[0]),
            total(model_sums[1]),
            total(final_sums),
            total(target_sums),
        )

    if share % 16 or (inner // members) % PAIR or model != (groups - 1) * width:
        back = [attention_back(piece, 3, ()) for piece in range(3)]
        d_query, d_key, d_value, piece_sums = ([part[k] for part in back] for k in range(4))
        target_grad, grad_w_target, target_sums = target_back(
            came, positive_part, positive_unit, positive_scale, targets, w_target, ()
        )
        input_grad = inputs_back(
            d_resid, (d_query, d_key, d_value), own_matrices, block, ()
        )

        def reduced(grad):
            part = lax.psum_scatter(grad, "tm", scatter_dimension=0, tiled=True)
            return lax.psum(to_low(part), "grp").astype(jnp.float32)

        def projected(parts):
            return reduced(product_left(frames_low, jnp.concatenate(parts, axis=1)))

        small = [reduced(vector) for vector in vector_sums(piece_sums, target_sums)]
        return (
            losses,
            input_grad,
            target_grad,
            projected(d_query),
            small[0],
            projected(d_key),
            projected(d_value),
            small[1],
            reduced(product_left(attended_low, d_branch_low)),
            small[2],
            small[3],
            small[4],
            reduced(product(hidden_turned, d_upper_low)),
            small[5],
            reduced(product(d_down_turned, active_low).T),
            small[6],
            small[7],
            small[8],
            reduced(product(output_turned, d_final_low)),
            small[9],
            reduced(grad_w_target),
            small[10],
        )

    up_kept, up_sent = up_grad(
        core,
        hidden_turned,
        d_upper_low,
        attended_low,
        d_branch_low,
        output_turned,
        d_final_low,
        members,
        groups,
        (),
    )
    up_came = exchange(up_sent)
    down_parts = down_grad(active_low, d_down_turned, members, groups, width, (up_sent,))
    down_part = scatter(down_parts, "tm")
    up_group = split_sum(group, [[up_kept, up_came]], groups, (down_parts,))
    up_groups = swap(up_group)

    def projections(pieces, sums, after):
        grads = [back[piece][k] for k in range(3) for piece in pieces]
        sums_of = [part[3] for part in back] if sums else []
        return projection_grad(core, frames_low, grads, sums_of, sums, members, groups, after)

    back = [attention_back(0, 3, (up_group[1],))]
    target_grad, grad_w_target, target_sums = target_back(
        came, positive_part, positive_unit, positive_scale, targets, w_target, (back[0][0],)
    )
    back.append(attention_back(1, 3, (grad_w_target,)))
    early_kept, early_sent = projections((0, 1), (), ())
    early_came = exchange(early_sent)
    up_line = line_sum(up_groups, (early_sent,))
    up_share = scatter(up_line, "tm", chip_lines())
    early_group = split_sum(group, [[early_kept, early_came]], groups, (up_line,))
    early_groups = swap(early_group)
    back.append(attention_back(2, 3, (early_group[1],)))
    d_query, d_key, d_value, piece_sums = ([part[k] for part in back] for k in range(4))
    late_kept, late_sent = projections(
        (2,), (model_sums, up_sums, final_sums, target_sums, grad_w_target), ()
    )
    late_came = exchange(late_sent)
    early_line = line_sum(early_groups, (late_sent,))
    late_group = split_sum(group, [[late_kept, late_came], [down_part]], groups, (early_line,))
    late_groups = swap(late_group)
    input_grad = inputs_back(
        d_resid, (d_query, d_key, d_value), own_matrices, block, (late_group[1],)
    )
    own_line = split_sum(line, [[early_line], late_groups], members // 2, (input_grad,))
    own_lines = swap(own_line, "tm", 2)
    most_shares = shares(late_groups, members // 2, up_share, groups, (own_line[1],))
    most = lax.all_to_all(most_shares, "grp", 0, 0, tiled=True)

    def by_group(choice_ref, refs, put):
        for piece in range(groups):
            for number in range(groups):

                @pl.when(choice_ref[0] ^ piece == number)
                def _(piece=piece, number=number):
                    put(number, refs[piece], refs[groups:])

    last = swap([line_total(own_lines, (most_shares,))] * groups)
    up_at = inner // members * (model // groups // share)
    side_at = up_at + inner // groups

    def put_most(most_ref, down_ref, up_ref, out_ref, final_ref):
        rows = model // groups
        across = inner // members // PAIR
        for at in range(groups):
            part = lambda low, high: most_ref[at, :, low:high].astype(jnp.float32)
            for tile in range(up_at // PAIR):
                top = at * rows + tile // across * share
                low = tile % across * PAIR
                down_ref[low : low + PAIR, top : top + share] = part(tile * PAIR, (tile + 1) * PAIR).T
            wide = inner // groups
            up_ref[:, at * wide : (at + 1) * wide] = part(up_at, side_at)
            if at < groups - 1:
                out_ref[:, at * width : (at + 1) * width] = part(side_at, side_at + width)
            else:
                final_ref[...] = part(side_at, side_at + width)

    grad_down, grad_up, grad_out, grad_final = place(
        put_most,
        [most],
        [(inner // members, model), (share, inner), (share, model), (share, width)],
        (last[0],),
    )
    third = model // 3
    early = [(k, piece * third + at) for k in range(3) for piece in (0, 1) for at in range(0, third, PAIR)]
    late = [(k, 2 * third + at) for k in range(3) for at in range(0, third, PAIR)]
    late += [(3, at) for at in range(0, 2 * PAIR, PAIR)]

    def put_last(number, ref, outs):
        low = 0
        for tiles in (early, late):
            each = len(tiles) // groups
            for k, lanes in tiles[number * each : (number + 1) * each]:
                value = ref[:, low : low + PAIR].astype(jnp.float32)
                low += PAIR
                if k < 3:
                    outs[k][:, lanes : lanes + PAIR] = value
                elif lanes:
                    rows = width // members
                    for half in range(width // PAIR):
                        part = value[half * rows : (half + 1) * rows]
                        outs[3][:, half * PAIR : (half + 1) * PAIR] = part
                else:
                    row = 0
                    for out in outs[4:]:
                        for start in range(0, out.shape[0], PAIR):
                            size = min(PAIR, out.shape[0] - start)
                            out[start : start + size] = value[row, :size]
                            row += 1

    sizes = [model] * 5 + [inner] + [model] * 3 + [width] * 2
    grad_query, grad_key, grad_value, grad_target, *small = place(
        lambda choice_ref, *refs: by_group(choice_ref, refs, put_last),
        last,
        [(share, model)] * 3
        + [(width // members, width)]
        + [(size // members,) for size in sizes],
        (grad_up,),
        group,
    )
    return (
        losses,
        input_grad,
        target_grad,
        grad_query,
        small[0],
        grad_key,
        grad_value,
        small[1],
        grad_out,
        small[2],
        small[3],
        small[4],
        grad_up,
        small[5],
        grad_down,
        small[6],
        small[7],
        small[8],
        grad_final,
        small[9],
        grad_target,
        small[10],
    )


def solution(mesh):
    placed = (
        P(("grp", "tm"), None),
        P(("grp", "tm"), None),
        P(("grp", "tm"), None),
        P(("grp", "tm")),
        P(("grp", "tm"), None),
        P(),
        P(),
        P(),
        P(),
        P(),
        P(),
        P(),
        P(),
        P(),
        P(),
        P(),
        P(),
        P(),
        P(),
        P(),
        P(),
        P(),
        P(),
        P(),
    )
    return jax.shard_map(
        on_device,
        mesh=mesh,
        in_specs=placed,
        out_specs=(
            P(("grp", "tm")),
            P(("grp", "tm"), None),
            P(("grp", "tm"), None),
            P("tm", None),
            P("tm"),
            P("tm", None),
            P("tm", None),
            P("tm"),
            P("tm", None),
            P("tm"),
            P("tm"),
            P("tm"),
            P("tm", None),
            P("tm"),
            P("tm", None),
            P("tm"),
            P("tm"),
            P("tm"),
            P("tm", None),
            P("tm"),
            P("tm", None),
            P("tm"),
        ),
        check_vma=False,
    )
```

```python
import functools
import math

import jax
import jax.numpy as jnp
from jax import lax
from jax.experimental import pallas as pl
from jax.experimental.pallas import tpu as pltpu
from jax.sharding import PartitionSpec as P

H = 12
HD = 64
NEG = 100
SPAN = 10


norm_eps = 1e-05
cosine_eps = 1e-06
similarity_softening_factor = 0.1
log2e = 1.4426950408889634
PAIR = 2 * HD
COLUMNS = 256
NT = (((1,), (1,)), ((), ()))
TN = (((0,), (0,)), ((), ()))
large_cost = pl.CostEstimate(flops=230_000_000_000, bytes_accessed=1, transcendentals=0)
small_cost = pl.CostEstimate(flops=1, bytes_accessed=1, transcendentals=0)


def to_low(values):
    return values.astype(jnp.bfloat16)


def product(left, right):
    return jnp.dot(left, right, preferred_element_type=jnp.float32)


def product_left(left, right):
    return lax.dot_general(
        left, right, (((0,), (0,)), ((), ())), preferred_element_type=jnp.float32
    )


def dot(a, b, dims=(((1,), (0,)), ((), ()))):
    return lax.dot_general(a, b, dims, preferred_element_type=jnp.float32)

def first_half(rows):
    return lax.broadcasted_iota(jnp.int32, (rows, PAIR), 1) < HD


def windows(span_ref, block, chunk, count, body):
    i = pl.program_id(0)
    start, chunks = span_ref[0, i], span_ref[1, i]
    total = count // chunk
    sizes = list(range(2, total + 1))
    for size in sizes:
        hit = (chunks <= size) if size == sizes[0] else (chunks == size)

        @pl.when(hit)
        def _(size=size):
            at = pl.multiple_of(jnp.minimum(start, total - size) * chunk, chunk)
            body(at, size * chunk)


def either(first, one, other, half):
    return jnp.where(first, one, other) if half == 0 else jnp.where(first, other, one)


def forward_kernel(casts, pairs, chunk, unroll, span_ref, q_ref, k_ref, v_ref, hotq_ref, hotk_ref, *refs):
    sources, out_ref, log_ref = refs[:casts], refs[casts], refs[casts + 1]
    results = refs[casts + 2 : 2 * casts + 2]
    wides, lows = refs[2 * casts + 2 : 3 * casts + 2], refs[3 * casts + 2 : 4 * casts + 2]
    in_sems, out_sems = refs[-2:]
    step = pl.program_id(0)

    def copies(pairs_of, sems):
        return [
            pltpu.make_async_copy(source, target, sems.at[number])
            for number, (source, target) in enumerate(pairs_of)
        ]

    @pl.when(step == 0)
    def _():
        for copy in copies(zip(sources, wides), in_sems):
            copy.start()

    block = q_ref.shape[0]
    count = k_ref.shape[0]
    scale = HD**-0.5 * log2e

    def body(at, size):
        near = pl.ds(at, size)
        lane = lax.broadcasted_iota(jnp.int32, (block, PAIR), 1)
        first_q, first_k = first_half(block), first_half(size)
        ones = jnp.ones((size, PAIR), jnp.bfloat16)

        def pair(p, logs):
            cols = pl.ds(pl.multiple_of(p * PAIR, PAIR), PAIR)
            q, k, v = q_ref[:, cols], k_ref[near, cols], v_ref[near, cols]
            hotq, hotk = hotq_ref[...], hotk_ref[near, :]
            outs = []
            for half in range(2):
                scores = dot(either(first_q, q, hotq, half), either(first_k, k, hotk, half), NT)
                top = jnp.max(scores, axis=1, keepdims=True) * scale
                raised = to_low(jnp.exp2(scores * scale - top))
                result = dot(raised, either(first_k, v, ones, half))
                spare = HD * (1 - half)
                total = result[:, spare : spare + 1]
                outs.append(result * (1.0 / total))
                logs = jnp.where(lane == 2 * p + half, top + jnp.log2(total), logs)
            out_ref[:, cols] = to_low(jnp.where(first_q, outs[0], outs[1]))
            return logs

        empty = jnp.zeros((block, PAIR), jnp.float32)
        log_ref[...] = lax.fori_loop(0, pairs, pair, empty, unroll=unroll)

    windows(span_ref, block, chunk, count, body)

    @pl.when(step == 0)
    def _():
        for copy, wide, low in zip(copies(zip(sources, wides), in_sems), wides, lows):
            copy.wait()
            low[...] = to_low(wide[...])
        for copy in copies(zip(lows, results), out_sems):
            copy.start()

    @pl.when(step == pl.num_programs(0) - 1)
    def _():
        for copy in copies(zip(lows, results), out_sems):
            copy.wait()


def attend(span, query, key, value, hotq, hotk, casts, block, chunk, unroll):
    count, width = query.shape
    whole = lambda w: pl.BlockSpec((count, w), lambda i, *_: (0, 0))
    part = lambda w: pl.BlockSpec((block, w), lambda i, *_: (i, 0))
    anywhere = [pl.BlockSpec(memory_space=pl.ANY)] * len(casts)
    shape = jax.ShapeDtypeStruct
    return pl.pallas_call(
        functools.partial(forward_kernel, len(casts), width // PAIR, chunk, unroll),
        grid_spec=pltpu.PrefetchScalarGridSpec(
            num_scalar_prefetch=1,
            grid=(count // block,),
            in_specs=[part(width), whole(width), whole(width), part(PAIR), whole(PAIR)] + anywhere,
            out_specs=[part(width), part(PAIR)] + anywhere,
            scratch_shapes=[pltpu.VMEM(x.shape, jnp.float32) for x in casts]
            + [pltpu.VMEM(x.shape, jnp.bfloat16) for x in casts]
            + [pltpu.SemaphoreType.DMA((len(casts),))] * 2,
        ),
        out_shape=[shape((count, width), jnp.bfloat16), shape((count, PAIR), jnp.float32)]
        + [shape(x.shape, jnp.bfloat16) for x in casts],
        cost_estimate=small_cost,
        compiler_params=pltpu.CompilerParams(vmem_limit_bytes=62 << 20),
    )(span, query, key, value, hotq, hotk, *casts)


def thirds(values):
    high = to_low(values)
    rest = values - high.astype(jnp.float32)
    middle = to_low(rest)
    return high, middle, to_low(rest - middle.astype(jnp.float32))


def backward_kernel(
    kinds,
    pairs,
    chunk,
    unroll,
    piece,
    span_ref,
    q_ref,
    k_ref,
    v_ref,
    g_ref,
    o_ref,
    hotq_ref,
    hotk_ref,
    log_ref,
    *refs,
):
    dq_ref, dk_ref, dv_ref, sums_ref, dk_sum, dv_sum = refs[-6:]
    block = q_ref.shape[0]
    count = k_ref.shape[0]
    scale = HD**-0.5 * log2e

    @pl.when(pl.program_id(0) == 0)
    def _():
        dk_sum[...] = jnp.zeros_like(dk_sum)
        dv_sum[...] = jnp.zeros_like(dv_sum)
        sums_ref[...] = jnp.zeros_like(sums_ref)

    def body(at, size):
        near = pl.ds(at, size)
        lane = lax.broadcasted_iota(jnp.int32, (block, PAIR), 1)
        first_q, first_k = first_half(block), first_half(size)
        spare = lax.rem(lane, HD) - kinds

        def affine(values, rest):
            for number, part in enumerate(thirds(values)):
                rest = jnp.where(spare == number, part, rest)
            return rest

        def pair(p, _):
            cols = pl.ds(pl.multiple_of(p * PAIR, PAIR), PAIR)
            q, k, v, g = q_ref[:, cols], k_ref[near, cols], v_ref[near, cols], g_ref[:, cols]
            hotq, hotk, logs = hotq_ref[...], hotk_ref[near, :], log_ref[...]
            products = g.astype(jnp.float32) * o_ref[:, cols].astype(jnp.float32)
            zero = jnp.zeros_like(g)
            dqs, dks, dvs = [], [], []
            for half in range(2):
                mine = lane == 2 * (p + piece * pairs) + half
                log = jnp.sum(jnp.where(mine, logs, 0.0), axis=1, keepdims=True)
                inner = jnp.sum(either(first_q, products, 0.0, half), axis=1, keepdims=True)
                qh = either(first_q, q, affine(log * (-1.0 / scale), hotq), half)
                gh = either(first_q, g, affine(-inner, zero), half)
                kh = either(first_k, k, hotk, half)
                vh = either(first_k, v, hotk, half)
                prob = jnp.exp2(dot(qh, kh, NT) * scale)
                d_scores = to_low(prob * dot(gh, vh, NT))
                dqs.append(dot(d_scores, k))
                dks.append(dot(d_scores, q, TN))
                dvs.append(dot(to_low(prob), g, TN))
            dq_ref[:, cols] = to_low(jnp.where(first_q, dqs[0], dqs[1]) * HD**-0.5)
            dk_sum[near, cols] += jnp.where(first_k, dks[0], dks[1])
            dv_sum[near, cols] += jnp.where(first_k, dvs[0], dvs[1])
            return 0

        lax.fori_loop(0, pairs, pair, 0, unroll=unroll)

    windows(span_ref, block, chunk, count, body)
    rounded = dq_ref[...].astype(jnp.float32)
    sums_ref[0] += jnp.sum(rounded.reshape(-1, 8, rounded.shape[1]), axis=0)

    @pl.when(pl.program_id(0) == pl.num_programs(0) - 1)
    def _():
        sums_ref[1] = jnp.sum(dv_sum[...].reshape(-1, 8, dv_sum.shape[1]), axis=0)
        dk_ref[...] = to_low(dk_sum[...] * HD**-0.5)
        dv_ref[...] = to_low(dv_sum[...])


def attend_back(
    span, query, key, value, grad, result, hotq, hotk, logs, kinds, block, chunk, unroll, piece, pieces, after
):
    count = query.shape[0]
    width = query.shape[1] // pieces
    whole = lambda w, j=0: pl.BlockSpec((count, w), lambda i, *_: (0, j))
    part = lambda w, j=0: pl.BlockSpec((block, w), lambda i, *_: (i, j))
    shape = jax.ShapeDtypeStruct
    return pl.pallas_call(
        functools.partial(backward_kernel, kinds, width // PAIR, chunk, unroll, piece),
        grid_spec=pltpu.PrefetchScalarGridSpec(
            num_scalar_prefetch=1,
            grid=(count // block,),
            in_specs=[
                part(width, piece),
                whole(width, piece),
                whole(width, piece),
                part(width, piece),
                part(width, piece),
                part(PAIR),
                whole(PAIR),
                part(PAIR),
            ]
            + [pl.BlockSpec(memory_space=pl.ANY)] * len(after),
            out_specs=[
                part(width),
                whole(width),
                whole(width),
                pl.BlockSpec((2, 8, width), lambda i, *_: (0, 0, 0)),
            ],
            scratch_shapes=[pltpu.VMEM((count, width), jnp.float32)] * 2,
        ),
        out_shape=[shape((count, width), jnp.bfloat16)] * 3 + [shape((2, 8, width), jnp.float32)],
        cost_estimate=small_cost,
        compiler_params=pltpu.CompilerParams(vmem_limit_bytes=62 << 20),
    )(span, query, key, value, grad, result, hotq, hotk, logs, *after)


def rows_of(values):
    return pl.BlockSpec((values.shape[0], values.shape[1]), lambda i, *_: (0, 0))


def gelu_and_slope(values):
    size = jnp.abs(values) * 0.7071067811865476
    near = 1.0 / (1.0 + 0.3275911 * size)
    bell = jnp.exp2(values * values * (-0.5 * log2e))
    poly = near * (
        0.254829592
        + near * (-0.284496736 + near * (1.421413741 + near * (-1.453152027 + near * 1.061405429)))
    )
    tail = 0.5 * poly * bell
    share = jnp.where(values >= 0, 1.0 - tail, tail)
    return values * share, share + values * bell * 0.3989422804014327


def normalize(values):
    center = values - jnp.mean(values, axis=-1, keepdims=True)
    scale = lax.rsqrt(jnp.mean(center * center, axis=-1, keepdims=True) + norm_eps)
    return center * scale, scale


def normalize_back(grad, normed, scale, gain):
    moved = grad * gain
    inner = (
        moved
        - jnp.mean(moved, axis=-1, keepdims=True)
        - normed * jnp.mean(moved * normed, axis=-1, keepdims=True)
    )
    return inner * scale


def feed_forward_kernel(
    parts,
    attended_ref,
    frames_ref,
    out_ref,
    up_ref,
    down_ref,
    final_ref,
    *refs,
):
    vectors, up_bias_ref, final_bias_ref = refs[:6], refs[6], refs[7]
    (
        attended_turned_ref,
        hidden_turned_ref,
        normed_one_ref,
        active_ref,
        slope_ref,
        normed_two_ref,
        output_turned_ref,
        scales_ref,
        unit_ref,
        unit_scale_ref,
    ) = refs[8:]
    vector = lambda row: vectors[row][...].reshape(1, -1)
    attended_turned_ref[...] = attended_ref[...].T
    resid = frames_ref[...] + dot(attended_ref[...], out_ref[...]) + vector(0)
    normed, scale_one = normalize(resid)
    normed_one_ref[...] = to_low(normed)
    hidden = normed * vector(1) + vector(2)
    hidden_low = to_low(hidden)
    hidden_turned_ref[...] = hidden_low.T
    second = hidden + vector(3)
    chunk = up_ref.shape[1] // parts
    for part in range(parts):
        at = pl.ds(part * chunk, chunk)
        upper = dot(hidden_low, up_ref[:, at]) + up_bias_ref[at].reshape(1, -1)
        active, slope = gelu_and_slope(upper)
        active = to_low(active)
        active_ref[:, at] = active
        slope_ref[:, at] = to_low(slope)
        second = second + dot(active, down_ref[at, :])
    normed, scale_two = normalize(second)
    normed_two_ref[...] = to_low(normed)
    output_low = to_low(normed * vector(4) + vector(5))
    output_turned_ref[...] = output_low.T
    final = dot(output_low, final_ref[...]) + final_bias_ref[...].reshape(1, -1)
    turned = final.T
    unit_scale = lax.rsqrt(jnp.sum(turned * turned, axis=0, keepdims=True) + cosine_eps)
    unit_ref[...] = turned * unit_scale
    unit_scale_ref[...] = jnp.broadcast_to(unit_scale, unit_scale_ref.shape)
    lane = lax.broadcasted_iota(jnp.int32, scales_ref.shape, 1)
    scales_ref[...] = jnp.where(lane == 0, scale_one, scale_two)


def feed_forward(attended, frames, out, up, down, final, vectors, block):
    count, model = frames.shape
    inner, width = up.shape[1], final.shape[1]
    part = lambda columns: pl.BlockSpec((block, columns), lambda i: (i, 0))
    turned = lambda rows: pl.BlockSpec((rows, block), lambda i: (0, i))
    shape = jax.ShapeDtypeStruct
    low, full = jnp.bfloat16, jnp.float32
    operands = (attended, frames, out, up, down, final)
    return pl.pallas_call(
        functools.partial(feed_forward_kernel, max(inner // model, 1)),
        grid=(count // block,),
        in_specs=[part(model), part(model)]
        + [rows_of(x) for x in operands[2:]]
        + [vector_spec(x) for x in vectors],
        out_specs=[turned(model)] * 2
        + [part(model), part(inner), part(inner), part(model), turned(model), part(PAIR)]
        + [turned(width), turned(8)],
        out_shape=[
            shape((model, count), low),
            shape((model, count), low),
            shape((count, model), low),
            shape((count, inner), low),
            shape((count, inner), low),
            shape((count, model), low),
            shape((model, count), low),
            shape((count, PAIR), full),
            shape((width, count), full),
            shape((8, count), full),
        ],
        cost_estimate=small_cost,
        compiler_params=pltpu.CompilerParams(vmem_limit_bytes=62 << 20),
    )(*operands, *vectors)


def feed_forward_back_kernel(
    parts,
    d_final_ref,
    slope_ref,
    normed_one_ref,
    normed_two_ref,
    scales_ref,
    final_ref,
    up_ref,
    down_ref,
    out_ref,
    gain_one_ref,
    gain_two_ref,
    down_turned_ref,
    upper_low_ref,
    resid_ref,
    branch_low_ref,
    attended_low_ref,
    sums_ref,
    up_sums_ref,
    final_sums_ref,
):
    @pl.when(pl.program_id(0) == 0)
    def _():
        sums_ref[...] = jnp.zeros_like(sums_ref)
        up_sums_ref[...] = jnp.zeros_like(up_sums_ref)
        final_sums_ref[...] = jnp.zeros_like(final_sums_ref)

    def add(row, values):
        sums_ref[row] += jnp.sum(values.reshape(-1, 8, values.shape[1]), axis=0)

    d_final = d_final_ref[...]
    final_sums_ref[...] += jnp.sum(d_final.astype(jnp.float32).reshape(-1, 8, d_final.shape[1]), axis=0)
    grad = dot(d_final, final_ref[...], NT)
    normed = normed_two_ref[...].astype(jnp.float32)
    gain = gain_two_ref[...].reshape(1, -1)
    hidden = normalize_back(grad, normed, scales_ref[:, 1:2], gain)
    down_low = to_low(hidden)
    down_turned_ref[...] = down_low.T
    add(0, grad * normed)
    add(1, grad)
    add(2, down_low.astype(jnp.float32))
    chunk = up_ref.shape[1] // parts
    for part in range(parts):
        at = pl.ds(part * chunk, chunk)
        upper = dot(down_low, down_ref[at, :], NT) * slope_ref[:, at].astype(jnp.float32)
        upper_low = to_low(upper)
        upper_low_ref[:, at] = upper_low
        up_sums_ref[:, at] += jnp.sum(upper.reshape(-1, 8, chunk), axis=0)
        hidden = hidden + dot(upper_low, up_ref[:, at], NT)
    normed = normed_one_ref[...].astype(jnp.float32)
    gain = gain_one_ref[...].reshape(1, -1)
    resid = normalize_back(hidden, normed, scales_ref[:, 0:1], gain)
    resid_ref[...] = resid
    branch_low = to_low(resid)
    branch_low_ref[...] = branch_low
    attended_low_ref[...] = to_low(dot(branch_low, out_ref[...], NT))
    add(3, hidden * normed)
    add(4, hidden)
    add(5, branch_low.astype(jnp.float32))


def feed_forward_back(d_final, slope, normed_one, normed_two, scales, final, up, down, out, gains, block):
    count, model = normed_one.shape
    inner = up.shape[1]
    part = lambda columns: pl.BlockSpec((block, columns), lambda i: (i, 0))
    shape = jax.ShapeDtypeStruct
    low, full = jnp.bfloat16, jnp.float32
    return pl.pallas_call(
        functools.partial(feed_forward_back_kernel, max(inner // model, 1)),
        grid=(count // block,),
        in_specs=[part(d_final.shape[1]), part(inner), part(model), part(model), part(PAIR)]
        + [rows_of(x) for x in (final, up, down, out)]
        + [vector_spec(x) for x in gains],
        out_specs=[pl.BlockSpec((model, block), lambda i: (0, i))]
        + [part(inner), part(model), part(model), part(model)]
        + [
            pl.BlockSpec((6, 8, model), lambda i: (0, 0, 0)),
            pl.BlockSpec((8, inner), lambda i: (0, 0)),
            pl.BlockSpec((8, d_final.shape[1]), lambda i: (0, 0)),
        ],
        out_shape=[
            shape((model, count), low),
            shape((count, inner), low),
            shape((count, model), full),
            shape((count, model), low),
            shape((count, model), low),
            shape((6, 8, model), full),
            shape((8, inner), full),
            shape((8, d_final.shape[1]), full),
        ],
        cost_estimate=small_cost,
        compiler_params=pltpu.CompilerParams(vmem_limit_bytes=62 << 20),
    )(d_final, slope, normed_one, normed_two, scales, final, up, down, out, *gains)


def candidate_kernel(
    slots, owners, keep, index_ref, rows_ref, unit_ref, scale_ref, positive_ref, masked_ref,
    loss_ref, final_low_ref, positive_part_ref, rows_grad_ref,
    packed, mass, pull, total, unit_low, weighted,
):
    step = pl.program_id(0)
    frames = unit_ref.shape[1]
    own = rows_ref.shape[0]
    lanes = 128
    words = lax.broadcasted_iota(jnp.int32, (128, lanes), 0)

    def fill(at_mass):
        def count(tile, _):
            at = pl.ds(pl.multiple_of(tile * lanes, lanes), lanes)
            acc = jnp.zeros((128, lanes), jnp.int32)
            for slot in range(slots):
                index = index_ref[0, pl.ds(slot, 1), at]
                low = jnp.bitwise_and(index, 127)
                unit = jnp.where(index >= 0, jnp.left_shift(1, 4 * jnp.right_shift(index, 7)), 0)
                acc = acc + jnp.where(words == low, unit, 0)
            packed[:, at] = acc
            return 0

        lax.fori_loop(0, frames // lanes, count, 0)

        wide = 4

        def part(number, _):
            first = number * (128 * wide)
            at = pl.ds(pl.multiple_of(first, 128 * wide), 128 * wide)
            cosines = dot(rows_ref[at, :], unit_low[...])
            for piece in range(wide):
                cosine = cosines[piece * 128 : (piece + 1) * 128]
                shift = 4 * (number * wide + piece)
                times = jnp.bitwise_and(lax.shift_right_logical(packed[...], shift), 15)
                value = times.astype(jnp.float32) * jnp.exp2(cosine)
                total[...] += jnp.sum(value.reshape(16, 8, frames), axis=0)
                low = pl.multiple_of(at_mass + first + piece * 128, 128)
                mass[pl.ds(low, 128), :] = to_low(value)
            return 0

        lax.fori_loop(0, own // (128 * wide), part, 0, unroll=1)

    @pl.when(step == 0)
    def _():
        unit_low[...] = to_low(unit_ref[...])
        total[...] = jnp.zeros_like(total)
        pull[...] = jnp.zeros_like(pull)

    @pl.when(step < owners)
    def _():
        at_mass = step * own if keep else 0
        fill(at_mass)
        pull[...] += dot(rows_ref[...], mass[pl.ds(pl.multiple_of(at_mass, own), own), :], TN)

    @pl.when(step == owners - 1)
    def _():
        score_scale = log2e / similarity_softening_factor
        unit, positive, masked = unit_ref[...], positive_ref[...], masked_ref[...]
        mass_sum = jnp.sum(total[...], axis=0, keepdims=True)
        score = jnp.sum(unit * positive, axis=0, keepdims=True) * (1.0 / similarity_softening_factor)
        whole = jnp.exp(score) + mass_sum
        loss_ref[...] = (masked * (jnp.log(whole) - score))[0]
        weight = masked / whole * (1.0 / similarity_softening_factor)
        d_score = -weight * mass_sum
        d_unit = d_score * positive + weight * (1.0 / score_scale) * pull[...]
        inner = jnp.sum(d_unit * unit, axis=0, keepdims=True)
        final_low_ref[...] = to_low((scale_ref[0:1, :] * (d_unit - unit * inner)).T)
        positive_part_ref[...] = (d_score * unit).T
        weighted[...] = to_low((weight * unit).T)

    @pl.when(step >= owners)
    def _():
        at_mass = (step - owners) * own if keep else 0
        if not keep:
            fill(at_mass)
        rows_grad_ref[...] = to_low(dot(mass[pl.ds(pl.multiple_of(at_mass, own), own), :], weighted[...]))


def candidates(index, rows, unit, scale, positive, masked):
    owners, slots, frames = index.shape
    width = rows.shape[1]
    own = rows.shape[0] // owners
    keep = rows.shape[0] * frames * 2 <= 16 << 20
    again = (lambda i: jnp.minimum(i, owners - 1)) if keep else (lambda i: lax.rem(i, owners))
    shape = jax.ShapeDtypeStruct
    return pl.pallas_call(
        functools.partial(candidate_kernel, slots, owners, keep),
        grid=(2 * owners,),
        in_specs=[
            pl.BlockSpec((1, slots, frames), lambda i: (again(i), 0, 0)),
            pl.BlockSpec((own, width), lambda i: (again(i), 0)),
            rows_of(unit),
            rows_of(scale),
            rows_of(positive),
            rows_of(masked),
        ],
        out_specs=[
            pl.BlockSpec((frames,), lambda i: (0,)),
            pl.BlockSpec((frames, width), lambda i: (0, 0)),
            pl.BlockSpec((frames, width), lambda i: (0, 0)),
            pl.BlockSpec((own, width), lambda i: (jnp.maximum(i - owners, 0), 0)),
        ],
        out_shape=[
            shape((frames,), jnp.float32),
            shape((frames, width), jnp.bfloat16),
            shape((frames, width), jnp.float32),
            shape((rows.shape[0], width), jnp.bfloat16),
        ],
        scratch_shapes=[
            pltpu.VMEM((128, frames), jnp.int32),
            pltpu.VMEM((rows.shape[0] if keep else own, frames), jnp.bfloat16),
            pltpu.VMEM((width, frames), jnp.float32),
            pltpu.VMEM((8, frames), jnp.float32),
            pltpu.VMEM((width, frames), jnp.bfloat16),
            pltpu.VMEM((frames, width), jnp.bfloat16),
        ],
        cost_estimate=small_cost,
        compiler_params=pltpu.CompilerParams(vmem_limit_bytes=62 << 20),
    )(index, rows, unit, scale, positive, masked)


def down_grad_kernel(active_ref, turned_ref, *refs):
    out_ref = refs[-1]
    here, groups, blocks, rows, wide = out_ref.shape
    value = to_low(dot(turned_ref[...], active_ref[...]))
    each = value.shape[0] // groups
    across = value.shape[1] // here // PAIR
    for group in range(groups):
        for tile in range(each // rows * across):
            top = group * each + tile // across * rows
            lanes = pl.ds(tile * PAIR % wide, PAIR)
            for number in range(here):
                low = (number * across + tile % across) * PAIR
                part = value[top : top + rows, low : low + PAIR]
                out_ref[number, group, tile * PAIR // wide, :, lanes] = part


def down_grad(active, turned, members, groups, width, after):
    count, inner = active.shape
    model = turned.shape[0]
    share, rows = inner // members, model // members
    block = (2, groups, model * share // (groups * rows * width), rows, width)
    return pl.pallas_call(
        down_grad_kernel,
        grid=(members // 2,),
        in_specs=[pl.BlockSpec((count, 2 * share), lambda i: (0, i)), rows_of(turned)]
        + [pl.BlockSpec(memory_space=pl.ANY)] * len(after),
        out_specs=pl.BlockSpec(block, lambda i: (i, 0, 0, 0, 0)),
        out_shape=jax.ShapeDtypeStruct((members, *block[1:]), jnp.bfloat16),
        cost_estimate=small_cost,
        compiler_params=pltpu.CompilerParams(vmem_limit_bytes=62 << 20),
    )(active, turned, *after)


def up_grad_kernel(
    groups, core_ref, hidden_ref, upper_ref, attended_ref, branch_ref, output_ref, final_ref, *refs
):
    kept_ref, sent_ref, held = refs[-3:]
    group = pl.program_id(0)
    core = core_ref[0]
    lines, share = kept_ref.shape[1], kept_ref.shape[2]

    wide = upper_ref.shape[1]
    side = final_ref.shape[1]
    held[:, :, :, :wide] = to_low(dot(hidden_ref[...], upper_ref[...])).reshape(lines, 2, share, wide)

    @pl.when(group < groups - 1)
    def _():
        value = dot(attended_ref[...], branch_ref[...])
        held[:, :, :, wide:] = to_low(value).reshape(lines, 2, share, side)

    @pl.when(group == groups - 1)
    def _():
        value = dot(output_ref[...], final_ref[...])
        held[:, :, :, wide:] = to_low(value).reshape(lines, 2, share, side)

    kept_ref[0] = held[:, core]
    sent_ref[0] = held[:, 1 - core]


def up_grad(core, hidden, upper, attended, branch, output, final, members, groups, after):
    model, count = hidden.shape
    wide, side = upper.shape[1] // groups, final.shape[1]
    lines, share = members // 2, model // members
    whole = lambda columns: pl.BlockSpec((count, columns), lambda g, core: (0, 0))
    out = pl.BlockSpec((1, lines, share, wide + side), lambda g, core: (g, 0, 0, 0))
    shape = jax.ShapeDtypeStruct((groups, lines, share, wide + side), jnp.bfloat16)
    last = model // side - 1
    return pl.pallas_call(
        functools.partial(up_grad_kernel, groups),
        grid_spec=pltpu.PrefetchScalarGridSpec(
            num_scalar_prefetch=1,
            grid=(groups,),
            in_specs=[
                rows_of(hidden),
                pl.BlockSpec((count, wide), lambda g, core: (0, g)),
                rows_of(attended),
                pl.BlockSpec((count, side), lambda g, core: (0, jnp.minimum(g, last))),
                rows_of(output),
                whole(side),
            ]
            + [pl.BlockSpec(memory_space=pl.ANY)] * len(after),
            out_specs=[out, out],
            scratch_shapes=[
                pltpu.VMEM((lines, 2, share, wide + side), jnp.bfloat16),
            ],
        ),
        out_shape=[shape, shape],
        cost_estimate=small_cost,
        compiler_params=pltpu.CompilerParams(vmem_limit_bytes=62 << 20),
    )(core, hidden, upper, attended, branch, output, final, *after)


def projection_grad_kernel(grads, pieces, core_ref, turned_ref, *refs):
    kept_ref, sent_ref, held = refs[-3:]
    core = core_ref[0]
    turned = turned_ref[...]
    each = kept_ref.shape[3] // PAIR
    lines, share = kept_ref.shape[1], kept_ref.shape[2]
    members = 2 * lines

    def put(number):
        for column in range(held.shape[3] // PAIR):
            tile = number * (held.shape[3] // PAIR) + column
            group, lanes = tile // each, pl.ds(tile % each * PAIR, PAIR)
            at = pl.ds(column * PAIR, PAIR)
            kept_ref[group, :, :, lanes] = held[:, core, :, at]
            sent_ref[group, :, :, lanes] = held[:, 1 - core, :, at]

    for number, ref in enumerate(refs[:grads]):
        held[...] = to_low(dot(turned, ref[...])).reshape(held.shape)
        put(number)
    if len(refs) == grads + 3:
        return
    piece_refs = refs[grads : grads + pieces]
    model_ref, up_ref, final_ref, target_ref, square_ref = refs[grads + pieces : -3]

    def total(values):
        return jnp.sum(values, axis=0, keepdims=True)

    vectors = (
        jnp.concatenate([total(ref[0]) for ref in piece_refs], axis=1),
        jnp.concatenate([total(ref[1]) for ref in piece_refs], axis=1),
        total(model_ref[5]),
        total(model_ref[3]),
        total(model_ref[4]),
        total(up_ref[...]),
        total(model_ref[2]),
        total(model_ref[0]),
        total(model_ref[1]),
        total(final_ref[...]),
        total(target_ref[...]),
    )
    square = square_ref[...]
    rows = square.shape[0] // members
    held[...] = jnp.zeros_like(held)
    for member in range(members):
        line, side = member // 2, member % 2
        parts = []
        for vector in vectors:
            size = vector.shape[1] // members
            for low in range(member * size, (member + 1) * size, PAIR):
                part = vector[:, low : min(low + PAIR, (member + 1) * size)]
                parts.append(jnp.pad(part, ((0, 0), (0, PAIR - part.shape[1]))))
        parts.append(jnp.zeros((share - len(parts), PAIR), jnp.float32))
        held[line, side, :, :PAIR] = to_low(jnp.concatenate(parts, axis=0))
        own = square[member * rows : (member + 1) * rows]
        for half in range(square.shape[1] // PAIR):
            part = own[:, half * PAIR : (half + 1) * PAIR]
            held[line, side, half * rows : (half + 1) * rows, PAIR:] = to_low(part)
    put(grads)


def projection_grad(core, turned, grads, pieces, sums, members, groups, after):
    model = turned.shape[0]
    lines, share = members // 2, model // members
    width = grads[0].shape[1]
    wide = (len(grads) + bool(sums)) * width // groups
    shape = jax.ShapeDtypeStruct((groups, lines, share, wide), jnp.bfloat16)
    vmem = pl.BlockSpec(memory_space=pltpu.VMEM)

    def kernel(*refs):
        used = 2 + len(grads) + len(pieces) + len(sums)
        projection_grad_kernel(len(grads), len(pieces), *refs[:used], *refs[used + len(after) :])

    return pl.pallas_call(
        kernel,
        in_specs=[pl.BlockSpec(memory_space=pltpu.SMEM)]
        + [vmem] * (1 + len(grads) + len(pieces) + len(sums))
        + [pl.BlockSpec(memory_space=pl.ANY)] * len(after),
        out_specs=[vmem, vmem],
        out_shape=[shape, shape],
        scratch_shapes=[pltpu.VMEM((lines, 2, share, width), jnp.bfloat16)],
        cost_estimate=small_cost,
        compiler_params=pltpu.CompilerParams(vmem_limit_bytes=62 << 20),
    )(core, turned, *grads, *pieces, *sums, *after)


def slot_rows(distractors, members):
    count, slots = distractors.shape
    turns = -(-slots // members)
    padded = jnp.pad(distractors, ((0, 0), (0, turns * members - slots)), constant_values=-1)
    padded = padded.T.reshape(turns, members, count)
    period = members // math.gcd(slots, members)
    frame = jnp.arange(count, dtype=jnp.int32) % period
    placed = padded
    for phase in range(1, period):
        turned = jnp.roll(padded, phase * slots % members, axis=1)
        placed = jnp.where(frame == phase, turned, placed)
    return placed.transpose(1, 0, 2)


def target_kernel(came_ref, part_ref, unit_ref, scale_ref, low_ref, matrix_ref, *refs):
    grad_ref, matrix_grad_ref, sums_ref = refs[-3:]
    grad_unit = part_ref[...] + came_ref[...].astype(jnp.float32)
    unit = unit_ref[...]
    inner = jnp.sum(grad_unit * unit, axis=-1, keepdims=True)
    low = to_low(scale_ref[:, 0:1] * (grad_unit - unit * inner))
    grad_ref[...] = dot(low, to_low(matrix_ref[...]), NT)
    matrix_grad_ref[...] = dot(to_low(low_ref[...]), low, TN)
    sums_ref[...] = jnp.sum(low.astype(jnp.float32).reshape(-1, 8, low.shape[1]), axis=0)


def target_back(came, part, unit, scale, low, matrix, after):
    count, width = part.shape
    vmem = pl.BlockSpec(memory_space=pltpu.VMEM)
    shape = jax.ShapeDtypeStruct
    return pl.pallas_call(
        target_kernel,
        in_specs=[vmem] * 6 + [pl.BlockSpec(memory_space=pl.ANY)] * len(after),
        out_specs=[vmem] * 3,
        out_shape=[
            shape((count, width), jnp.float32),
            shape((width, width), jnp.float32),
            shape((8, width), jnp.float32),
        ],
        cost_estimate=small_cost,
        compiler_params=pltpu.CompilerParams(vmem_limit_bytes=62 << 20),
    )(came, part, unit, scale, low, matrix, *after)


def inputs_kernel(parts, resid_ref, *refs):
    out_ref = refs[-1]
    total = resid_ref[...]
    for matrix in range(3):
        low = 0
        for part in range(parts):
            grad_ref = refs[matrix * parts + part]
            high = low + grad_ref.shape[1]
            total = total + dot(grad_ref[...], refs[3 * parts + matrix][:, low:high], NT)
            low = high
    out_ref[...] = total


def inputs_back(resid, grads, matrices, block, after):
    count, model = resid.shape
    part = lambda x: pl.BlockSpec((block, x.shape[1]), lambda i: (i, 0))
    flat = [g for parts in grads for g in parts]
    return pl.pallas_call(
        functools.partial(inputs_kernel, len(grads[0])),
        grid=(count // block,),
        in_specs=[part(resid)]
        + [part(g) for g in flat]
        + [rows_of(m) for m in matrices]
        + [pl.BlockSpec(memory_space=pl.ANY)] * len(after),
        out_specs=part(resid),
        out_shape=jax.ShapeDtypeStruct(resid.shape, jnp.float32),
        cost_estimate=small_cost,
        compiler_params=pltpu.CompilerParams(vmem_limit_bytes=62 << 20),
    )(resid, *flat, *matrices, *after)


def prepare_kernel(
    blocks, chunks, lengths_ref, starts_ref, targets_ref, matrix_ref, bias_ref, *refs
):
    rows_ref, unit_ref, turned_ref, scale_ref, hot_query_ref, hot_key_ref, masked_ref = refs[:7]
    low = to_low(dot(to_low(targets_ref[...]), to_low(matrix_ref[...])) + bias_ref[...].reshape(1, -1))
    positive = low.astype(jnp.float32)
    scale = lax.rsqrt(jnp.sum(positive * positive, axis=-1, keepdims=True) + cosine_eps)
    unit = positive * scale
    rows_ref[...] = to_low(unit * (log2e / similarity_softening_factor))
    unit_ref[...] = unit
    turned_ref[...] = unit.T
    scale_ref[...] = jnp.broadcast_to(scale, scale_ref.shape)

    count = targets_ref.shape[0]
    kinds = lengths_ref.shape[1]
    bounds = [jnp.int32(0)]
    for kind in range(kinds):
        bounds.append(bounds[-1] + lengths_ref[0, kind])
    for span_ref, block, chunk in zip(refs[7:], blocks, chunks):
        for number in range(count // block):
            first, last = number * block, (number + 1) * block - 1
            begin, end = jnp.int32(0), jnp.int32(count)
            for kind in range(kinds):
                begin = jnp.where(bounds[kind] <= first, jnp.maximum(begin, bounds[kind]), begin)
                end = jnp.where(bounds[kind + 1] > last, jnp.minimum(end, bounds[kind + 1]), end)
            begin = lax.div(begin, chunk)
            span_ref[0, number] = begin
            span_ref[1, number] = lax.div(end + (chunk - 1), chunk) - begin

    row = lax.broadcasted_iota(jnp.int32, hot_query_ref.shape, 0)
    lane = lax.rem(lax.broadcasted_iota(jnp.int32, hot_query_ref.shape, 1), HD)
    same = jnp.zeros(hot_query_ref.shape, jnp.float32)
    for kind in range(kinds):
        inside = (row >= bounds[kind]) & (row < bounds[kind + 1]) & (lane == kind)
        same = jnp.where(inside, 1.0, same)
    hot_query_ref[...] = to_low(jnp.where(lane < kinds, 1e30 * (1.0 - same), 0.0))
    spare = (lane >= kinds) & (lane < kinds + 3)
    hot_key_ref[...] = to_low(jnp.where(spare, 1.0, -same))

    place = lax.broadcasted_iota(jnp.int32, masked_ref.shape, 1)
    age = place
    for kind in range(1, kinds):
        age = jnp.where(place >= bounds[kind], place - bounds[kind], age)
    starts = starts_ref[...].astype(jnp.float32)
    covered = starts
    for offset in range(1, SPAN):
        earlier = pltpu.roll(starts, offset, 1)
        covered = jnp.maximum(covered, jnp.where(age >= offset, earlier, 0.0))
    masked_ref[...] = covered


def prepare(lengths, starts, targets, matrix, bias, blocks, chunks):
    count, width = targets.shape
    vmem = pl.BlockSpec(memory_space=pltpu.VMEM)
    smem = pl.BlockSpec(memory_space=pltpu.SMEM)
    shape = jax.ShapeDtypeStruct
    return pl.pallas_call(
        functools.partial(prepare_kernel, blocks, chunks),
        in_specs=[smem] + [vmem] * 4,
        out_specs=[vmem] * 7 + [smem] * len(blocks),
        out_shape=[
            shape((count, width), jnp.bfloat16),
            shape((count, width), jnp.float32),
            shape((width, count), jnp.float32),
            shape((count, PAIR), jnp.float32),
            shape((count, PAIR), jnp.bfloat16),
            shape((count, PAIR), jnp.bfloat16),
            shape((1, count), jnp.float32),
        ]
        + [shape((2, count // block), jnp.int32) for block in blocks],
        cost_estimate=small_cost,
        compiler_params=pltpu.CompilerParams(vmem_limit_bytes=62 << 20),
    )(lengths, starts[None], targets, matrix, bias)


def project_kernel(frames_ref, wq_ref, wk_ref, wv_ref, bq_ref, bv_ref, *refs):
    turned_ref, q_ref, k_ref, v_ref, mq, mk, mv = refs[-7:]


    @pl.when(pl.program_id(0) == 0)
    def _():
        mq[...] = to_low(wq_ref[...])
        mk[...] = to_low(wk_ref[...])
        mv[...] = to_low(wv_ref[...])

    low = to_low(frames_ref[...])
    turned_ref[...] = low.T
    q_ref[...] = to_low(dot(low, mq[...]) + bq_ref[...].reshape(1, -1))
    k_ref[...] = to_low(dot(low, mk[...]))
    v_ref[...] = to_low(dot(low, mv[...]) + bv_ref[...].reshape(1, -1))


def vector_spec(values):
    return pl.BlockSpec(values.shape, lambda i, *_: (0,))


def project(frames, w_query, w_key, w_value, b_query, b_value, block, after):
    count, model = frames.shape
    part = pl.BlockSpec((block, model), lambda i: (i, 0))
    return pl.pallas_call(
        project_kernel,
        grid=(count // block,),
        in_specs=[part]
        + [rows_of(w) for w in (w_query, w_key, w_value)]
        + [vector_spec(b) for b in (b_query, b_value)]
        + [pl.BlockSpec(memory_space=pl.ANY)] * len(after),
        out_specs=[pl.BlockSpec((model, block), lambda i: (0, i))]
        + [part] * 3
        + [rows_of(w_query)] * 3,
        out_shape=[jax.ShapeDtypeStruct((model, count), jnp.bfloat16)]
        + [jax.ShapeDtypeStruct((count, model), jnp.bfloat16)] * 3
        + [jax.ShapeDtypeStruct((model, model), jnp.bfloat16)] * 3,
        cost_estimate=small_cost,
        compiler_params=pltpu.CompilerParams(vmem_limit_bytes=62 << 20),
    )(frames, w_query, w_key, w_value, b_query, b_value, *after)


def exchange(sent):
    members = lax.axis_size("tm")
    return lax.ppermute(sent, "tm", [(i, i ^ 1) for i in range(members)])


def split_kernel(counts, pieces, choice_ref, *refs):
    out_refs = refs[-pieces:]
    number, low, lanes = 0, 0, 0
    for count in counts:
        if count < 3:
            total = sum((refs[number + term][0] for term in range(1, count)), refs[number][0])
        else:
            total = to_low(sum(refs[number + term][0].astype(jnp.float32) for term in range(count)))
        high = lanes + total.shape[-1]
        for piece in range(pieces):

            @pl.when(pl.program_id(0) == piece)
            def _(piece=piece, total=total, low=low, lanes=lanes, high=high):
                if total.ndim == 3:
                    out_refs[piece][low : low + total.shape[0]] = total
                else:
                    out_refs[piece][:, lanes:high] = total

        number, low, lanes = number + count, low + total.shape[0], high


def split_sum(choice, sums, pieces, after):
    terms = [term for group in sums for term in group]
    first = [group[0].shape[1:] for group in sums]
    if len(first[0]) == 3:
        rest = (sum(shape[0] for shape in first), *first[0][1:])
    else:
        rest = (first[0][0], sum(shape[1] for shape in first))

    def source(term):
        zeros = (0,) * (term.ndim - 1)
        return pl.BlockSpec((1, *term.shape[1:]), lambda i, choice: (choice[0] ^ i, *zeros))

    return pl.pallas_call(
        functools.partial(split_kernel, [len(group) for group in sums], pieces),
        grid_spec=pltpu.PrefetchScalarGridSpec(
            num_scalar_prefetch=1,
            grid=(pieces,),
            in_specs=[source(term) for term in terms]
            + [pl.BlockSpec(memory_space=pl.ANY)] * len(after),
            out_specs=[pl.BlockSpec(rest, lambda i, choice: (0,) * len(rest))] * pieces,
        ),
        out_shape=[jax.ShapeDtypeStruct(rest, jnp.bfloat16)] * pieces,
        cost_estimate=small_cost,
        compiler_params=pltpu.CompilerParams(vmem_limit_bytes=62 << 20),
    )(choice, *terms, *after)


def swap(pieces, axis="grp", stride=1):
    size = lax.axis_size(axis)
    return [pieces[0]] + [
        lax.ppermute(piece, axis, [(i, i ^ (k * stride)) for i in range(size)])
        for k, piece in enumerate(pieces)
        if k
    ]


def line_kernel(terms, *refs):
    total = refs[0][...].astype(jnp.float32)
    for term in range(1, terms):
        total = total + refs[term][...].astype(jnp.float32)
    refs[-1][...] = to_low(total)


def line_sum(terms, after):
    lines, rest = terms[0].shape[0], terms[0].shape[1:]
    block = pl.BlockSpec((lines // 2, *rest), lambda i: (i, *(0,) * len(rest)))
    return pl.pallas_call(
        functools.partial(line_kernel, len(terms)),
        grid=(2,),
        in_specs=[block] * len(terms) + [pl.BlockSpec(memory_space=pl.ANY)] * len(after),
        out_specs=block,
        out_shape=jax.ShapeDtypeStruct(terms[0].shape, jnp.bfloat16),
        cost_estimate=large_cost,
        compiler_params=pltpu.CompilerParams(vmem_limit_bytes=62 << 20),
    )(*terms, *after)


def chip_lines():
    return [list(range(first, lax.axis_size("tm"), 2)) for first in range(2)]


def scatter(value, axis, among=None):
    return lax.psum_scatter(value, axis, scatter_dimension=0, axis_index_groups=among)


def share_kernel(lines_ref, share_ref, *refs):
    out_ref = refs[-1]
    wide = lines_ref.shape[3]
    low = 0
    for at in range(lines_ref.shape[1]):
        total = to_low(sum(lines_ref[term, at].astype(jnp.float32) for term in range(lines_ref.shape[0])))
        for copy in range(out_ref.shape[0]):
            out_ref[copy, :, low : low + wide] = total
        low += wide
    for copy in range(out_ref.shape[0]):
        out_ref[copy, :, low:] = share_ref[...]


def shares(lines, share, groups, after):
    _, blocks, rows, wide = lines.shape
    wide = blocks * wide + share.shape[1]
    vmem = pl.BlockSpec(memory_space=pltpu.VMEM)
    return pl.pallas_call(
        share_kernel,
        in_specs=[vmem] * 2 + [pl.BlockSpec(memory_space=pl.ANY)] * len(after),
        out_specs=vmem,
        out_shape=jax.ShapeDtypeStruct((groups, rows, wide), jnp.bfloat16),
        cost_estimate=small_cost,
        compiler_params=pltpu.CompilerParams(vmem_limit_bytes=62 << 20),
    )(lines, share, *after)


def place(kernel, arrays, shapes, after, choice=None):
    vmem = pl.BlockSpec(memory_space=pltpu.VMEM)
    first = [] if choice is None else [choice]
    used = len(first) + len(arrays)
    return pl.pallas_call(
        lambda *refs: kernel(*refs[:used], *refs[used + len(after) :]),
        in_specs=[pl.BlockSpec(memory_space=pltpu.SMEM)] * len(first)
        + [vmem] * len(arrays)
        + [pl.BlockSpec(memory_space=pl.ANY)] * len(after),
        out_specs=[vmem] * len(shapes),
        out_shape=[jax.ShapeDtypeStruct(s, jnp.float32) for s in shapes],
        cost_estimate=small_cost,
        compiler_params=pltpu.CompilerParams(vmem_limit_bytes=62 << 20),
    )(*first, *arrays, *after)


def line_total(terms, after):
    vmem = pl.BlockSpec(memory_space=pltpu.VMEM)
    return pl.pallas_call(
        functools.partial(line_kernel, len(terms)),
        in_specs=[vmem] * len(terms) + [pl.BlockSpec(memory_space=pl.ANY)] * len(after),
        out_specs=vmem,
        out_shape=jax.ShapeDtypeStruct(terms[0].shape, jnp.bfloat16),
        cost_estimate=small_cost,
        compiler_params=pltpu.CompilerParams(vmem_limit_bytes=62 << 20),
    )(*terms, *after)


def on_device(
    frames,
    targets,
    lengths,
    span_starts,
    distractors,
    w_query,
    b_query,
    w_key,
    w_value,
    b_value,
    w_out,
    b_out,
    norm_gain,
    norm_bias,
    w_up,
    b_up,
    w_down,
    b_down,
    final_gain,
    final_bias,
    w_final,
    b_final,
    w_target,
    b_target,
):
    count, model = frames.shape
    width = targets.shape[1]
    inner = w_up.shape[1]
    members, groups = lax.axis_size("tm"), lax.axis_size("grp")
    block = min(count, 256)
    share = model // members
    place_in_line = lax.axis_index("tm")
    core = (place_in_line % 2)[None].astype(jnp.int32)
    line = (place_in_line // 2)[None].astype(jnp.int32)
    group = lax.axis_index("grp")[None].astype(jnp.int32)

    (
        own_rows,
        positive_unit,
        positive_turned,
        positive_scale,
        hot_query,
        hot_key,
        masked,
        span,
        span_back,
    ) = prepare(
        lengths, span_starts, targets, w_target, b_target, (2 * block, block), (block, block)
    )
    rows = lax.all_gather(own_rows, "tm", tiled=True)
    index = slot_rows(distractors, members)

    frames_turned, query, key, value, *own_matrices = project(
        frames, w_query, w_key, w_value, b_query, b_value, block, (own_rows,)
    )
    attended_low, log_total, out_matrix, up_matrix, down_matrix, final_matrix = attend(
        span, query, key, value, hot_query, hot_key, (w_out, w_up, w_down, w_final), 2 * block, block, 2
    )
    (
        attended_turned,
        hidden_turned,
        normed_one,
        active_low,
        slope,
        normed_two,
        output_turned,
        scales,
        final_unit,
        final_scale,
    ) = feed_forward(
        attended_low,
        frames,
        out_matrix,
        up_matrix,
        down_matrix,
        final_matrix,
        (b_out, norm_gain, norm_bias, b_down, final_gain, final_bias, b_up, b_final),
        block,
    )
    losses, d_final_low, positive_part, d_rows = candidates(
        index, rows, final_unit, final_scale, positive_turned, masked
    )
    came = lax.psum_scatter(d_rows, "tm", scatter_dimension=0, tiled=True)

    (
        d_down_turned,
        d_upper_low,
        d_resid,
        d_branch_low,
        d_attended_low,
        model_sums,
        up_sums,
        final_sums,
    ) = feed_forward_back(
        d_final_low,
        slope,
        normed_one,
        normed_two,
        scales,
        final_matrix,
        up_matrix,
        down_matrix,
        out_matrix,
        (norm_gain, final_gain),
        block,
    )
    def attention_back(piece, pieces, after):
        return attend_back(
            span_back,
            query,
            key,
            value,
            d_attended_low,
            attended_low,
            hot_query,
            hot_key,
            log_total,
            lengths.shape[1],
            block,
            block,
            2,
            piece,
            pieces,
            after,
        )


    def total(values):
        return jnp.sum(values, axis=0)

    def vector_sums(piece_sums, target_sums):
        return (
            jnp.concatenate([total(s[0]) for s in piece_sums]),
            jnp.concatenate([total(s[1]) for s in piece_sums]),
            total(model_sums[5]),
            total(model_sums[3]),
            total(model_sums[4]),
            total(up_sums),
            total(model_sums[2]),
            total(model_sums[0]),
            total(model_sums[1]),
            total(final_sums),
            total(target_sums),
        )

    if share % 16 or (inner // members) % PAIR or model != (groups - 1) * width:
        back = [attention_back(piece, 3, ()) for piece in range(3)]
        d_query, d_key, d_value, piece_sums = ([part[k] for part in back] for k in range(4))
        target_grad, grad_w_target, target_sums = target_back(
            came, positive_part, positive_unit, positive_scale, targets, w_target, ()
        )
        input_grad = inputs_back(
            d_resid, (d_query, d_key, d_value), own_matrices, block, ()
        )

        def reduced(grad):
            part = lax.psum_scatter(grad, "tm", scatter_dimension=0, tiled=True)
            return lax.psum(to_low(part), "grp").astype(jnp.float32)

        def projected(parts):
            return reduced(product(frames_turned, jnp.concatenate(parts, axis=1)))

        small = [reduced(vector) for vector in vector_sums(piece_sums, target_sums)]
        return (
            losses,
            input_grad,
            target_grad,
            projected(d_query),
            small[0],
            projected(d_key),
            projected(d_value),
            small[1],
            reduced(product_left(attended_low, d_branch_low)),
            small[2],
            small[3],
            small[4],
            reduced(product(hidden_turned, d_upper_low)),
            small[5],
            reduced(product(d_down_turned, active_low).T),
            small[6],
            small[7],
            small[8],
            reduced(product(output_turned, d_final_low)),
            small[9],
            reduced(grad_w_target),
            small[10],
        )

    up_kept, up_sent = up_grad(
        core,
        hidden_turned,
        d_upper_low,
        attended_turned,
        d_branch_low,
        output_turned,
        d_final_low,
        members,
        groups,
        (),
    )
    up_came = exchange(up_sent)
    down_parts = down_grad(active_low, d_down_turned, members, groups, width, (up_sent,))
    down_part = scatter(down_parts, "tm")
    up_group = split_sum(group, [[up_kept, up_came]], groups, (down_parts,))
    up_groups = swap(up_group)

    def projections(pieces, sums, after):
        grads = [back[piece][k] for k in range(3) for piece in pieces]
        sums_of = [part[3] for part in back] if sums else []
        return projection_grad(core, frames_turned, grads, sums_of, sums, members, groups, after)

    back = [attention_back(0, 3, (up_group[1],))]
    target_grad, grad_w_target, target_sums = target_back(
        came, positive_part, positive_unit, positive_scale, targets, w_target, (back[0][0],)
    )
    back.append(attention_back(1, 3, (grad_w_target,)))
    early_kept, early_sent = projections((0, 1), (), ())
    early_came = exchange(early_sent)
    up_line = line_sum(up_groups, (early_sent,))
    up_share = scatter(up_line, "tm", chip_lines())
    early_group = split_sum(group, [[early_kept, early_came]], groups, (up_line,))
    early_groups = swap(early_group)
    back.append(attention_back(2, 3, (early_group[1],)))
    d_query, d_key, d_value, piece_sums = ([part[k] for part in back] for k in range(4))
    late_kept, late_sent = projections(
        (2,), (model_sums, up_sums, final_sums, target_sums, grad_w_target), ()
    )
    late_came = exchange(late_sent)
    down_lines = lax.all_to_all(down_part, "grp", 0, 0, tiled=True)
    early_line = line_sum(early_groups, (late_sent, down_lines))
    late_group = split_sum(group, [[late_kept, late_came]], groups, (early_line,))
    late_groups = swap(late_group)
    input_grad = inputs_back(
        d_resid, (d_query, d_key, d_value), own_matrices, block, (late_group[1],)
    )
    own_line = split_sum(line, [[early_line], late_groups], members // 2, (input_grad,))
    own_lines = swap(own_line, "tm", 2)
    most_shares = shares(down_lines, up_share, groups, (own_line[1],))
    most = lax.all_to_all(most_shares, "grp", 0, 0, tiled=True)

    def by_group(choice_ref, refs, put):
        for piece in range(groups):
            for number in range(groups):

                @pl.when(choice_ref[0] ^ piece == number)
                def _(piece=piece, number=number):
                    put(number, refs[piece], refs[groups:])

    last = swap([line_total(own_lines, (most_shares,))] * groups)
    up_at = inner // members * (model // groups // share)
    side_at = up_at + inner // groups

    def put_most(most_ref, down_ref, up_ref, out_ref, final_ref):
        rows = model // groups
        across = inner // members // PAIR
        for at in range(groups):
            raw = lambda low, high: most_ref[at, :, low:high]
            part = lambda low, high: raw(low, high).astype(jnp.float32)
            for tile in range(up_at // PAIR):
                top = at * rows + tile // across * share
                low = tile % across * PAIR
                turned = raw(tile * PAIR, (tile + 1) * PAIR).T
                down_ref[low : low + PAIR, top : top + share] = turned.astype(jnp.float32)
            wide = inner // groups
            up_ref[:, at * wide : (at + 1) * wide] = part(up_at, side_at)
            if at < groups - 1:
                out_ref[:, at * width : (at + 1) * width] = part(side_at, side_at + width)
            else:
                final_ref[...] = part(side_at, side_at + width)

    grad_down, grad_up, grad_out, grad_final = place(
        put_most,
        [most],
        [(inner // members, model), (share, inner), (share, model), (share, width)],
        (last[0],),
    )
    third = model // 3
    early = [(k, piece * third + at) for k in range(3) for piece in (0, 1) for at in range(0, third, PAIR)]
    late = [(k, 2 * third + at) for k in range(3) for at in range(0, third, PAIR)]
    late += [(3, at) for at in range(0, 2 * PAIR, PAIR)]

    def put_last(number, ref, outs):
        low = 0
        for tiles in (early, late):
            each = len(tiles) // groups
            for k, lanes in tiles[number * each : (number + 1) * each]:
                value = ref[:, low : low + PAIR].astype(jnp.float32)
                low += PAIR
                if k < 3:
                    outs[k][:, lanes : lanes + PAIR] = value
                elif lanes:
                    rows = width // members
                    for half in range(width // PAIR):
                        part = value[half * rows : (half + 1) * rows]
                        outs[3][:, half * PAIR : (half + 1) * PAIR] = part
                else:
                    row = 0
                    for out in outs[4:]:
                        for start in range(0, out.shape[0], PAIR):
                            size = min(PAIR, out.shape[0] - start)
                            out[start : start + size] = value[row, :size]
                            row += 1

    sizes = [model] * 5 + [inner] + [model] * 3 + [width] * 2
    grad_query, grad_key, grad_value, grad_target, *small = place(
        lambda choice_ref, *refs: by_group(choice_ref, refs, put_last),
        last,
        [(share, model)] * 3
        + [(width // members, width)]
        + [(size // members,) for size in sizes],
        (grad_up,),
        group,
    )
    return (
        losses,
        input_grad,
        target_grad,
        grad_query,
        small[0],
        grad_key,
        grad_value,
        small[1],
        grad_out,
        small[2],
        small[3],
        small[4],
        grad_up,
        small[5],
        grad_down,
        small[6],
        small[7],
        small[8],
        grad_final,
        small[9],
        grad_target,
        small[10],
    )


def solution(mesh):
    placed = (
        P(("grp", "tm"), None),
        P(("grp", "tm"), None),
        P(("grp", "tm"), None),
        P(("grp", "tm")),
        P(("grp", "tm"), None),
        P(),
        P(),
        P(),
        P(),
        P(),
        P(),
        P(),
        P(),
        P(),
        P(),
        P(),
        P(),
        P(),
        P(),
        P(),
        P(),
        P(),
        P(),
        P(),
    )
    return jax.shard_map(
        on_device,
        mesh=mesh,
        in_specs=placed,
        out_specs=(
            P(("grp", "tm")),
            P(("grp", "tm"), None),
            P(("grp", "tm"), None),
            P("tm", None),
            P("tm"),
            P("tm", None),
            P("tm", None),
            P("tm"),
            P("tm", None),
            P("tm"),
            P("tm"),
            P("tm"),
            P("tm", None),
            P("tm"),
            P("tm", None),
            P("tm"),
            P("tm"),
            P("tm"),
            P("tm", None),
            P("tm"),
            P("tm", None),
            P("tm"),
        ),
        check_vma=False,
    )
```
